128 devices in a mesh: dp: 8 (over z_hi, y), seq: 16 (over z_lo, x, core).
Axes of the slice: x: 4, y: 4, z: 4 (z_hi: 2, z_lo: 2; z = z_hi * 2 + z_lo), core: 2. Of those that a mesh axis runs over, the one named last changes fastest.
Arguments:
- tokens: bfloat16 [8, 2048, 1024], P('dp', 'seq'), may hold values from -6 to 6
- w_qkv: bfloat16 [1024, 3072], P('dp'), may hold values from -0.1875 to 0.1875
- qv_bias: bfloat16 [2048], P('dp'), may hold values from -3 to 3
- w_out: bfloat16 [1024, 1024], P('dp'), may hold values from -0.1875 to 0.1875
- out_bias: bfloat16 [1024], P('dp'), may hold values from -3 to 3
- w_up: bfloat16 [1024, 4096], P('dp'), may hold values from -0.1875 to 0.1875
- up_bias: bfloat16 [4096], P('dp'), may hold values from -3 to 3
- w_down: bfloat16 [4096, 1024], P('dp'), may hold values from -0.09375 to 0.09375
- down_bias: bfloat16 [1024], P('dp'), may hold values from -3 to 3
- gain_one: bfloat16 [1024], P('dp'), may hold values from 0.5 to 1.5
- shift_one: bfloat16 [1024], P('dp'), may hold values from -3 to 3
- gain_two: bfloat16 [1024], P('dp'), may hold values from 0.5 to 1.5
- shift_two: bfloat16 [1024], P('dp'), may hold values from -3 to 3
- cotangent: bfloat16 [8, 2048, 1024], P('dp', 'seq'), may hold values from -6 to 6
Outputs:
- activations: bfloat16 [8, 2048, 1024], P('dp', 'seq')
- input_grad: bfloat16 [8, 2048, 1024], P('dp', 'seq')
- w_qkv_grad: float32 [1024, 3072], P(('dp', 'seq'))
- qv_bias_grad: float32 [2048], P(('dp', 'seq'))
- w_out_grad: float32 [1024, 1024], P(('dp', 'seq'))
- out_bias_grad: float32 [1024], P(('dp', 'seq'))
- w_up_grad: float32 [1024, 4096], P(('dp', 'seq'))
- up_bias_grad: float32 [4096], P(('dp', 'seq'))
- w_down_grad: float32 [4096, 1024], P(('dp', 'seq'))
- down_bias_grad: float32 [1024], P(('dp', 'seq'))
- gain_one_grad: float32 [1024], P(('dp', 'seq'))
- shift_one_grad: float32 [1024], P(('dp', 'seq'))
- gain_two_grad: float32 [1024], P(('dp', 'seq'))
- shift_two_grad: float32 [1024], P(('dp', 'seq'))
The draws below stay inside these ranges and needn't reach their ends.
All inputs are finite; a program needn't handle non-finite values.
Results may differ from the reference program's by a relative error of at most 0.034.
Values may be sent and summed in bfloat16 or wider, within the bound.
A program may use at most 192 MiB of HBM per device.

```python
import jax
import jax.numpy as jnp
from jax import lax

D = 1024
H = 16
FF = 4096
CLIPS = 8
LEN = 2048


def block_scale(rng, dims, pieces, least, top_value):
    level, own = 1.0, jax.random.fold_in(rng, 6)
    for position, shards_of in pieces:
        steps = jnp.exp(jax.random.uniform(jax.random.fold_in(own, position), (shards_of,), jnp.float32, least / len(pieces), top_value / len(pieces)))
        level = level * jnp.repeat(steps, dims[position] // shards_of).reshape([-1 if axis == position else 1 for axis in range(len(dims))])
    return level


def gaussian(stream_key, extent, scale, reach, shards=(), held_as=jnp.bfloat16):
    values = jax.random.normal(stream_key, extent, jnp.float32) * scale
    if len(shards) > 0:
        values = block_scale(stream_key, extent, shards, -0.22, 0.18) * values
    return jnp.clip(values, min=-reach, max=reach).astype(held_as)


def setup_inputs(seed: int = 0) -> dict:
    seeds = jax.random.split(jax.random.key(seed), 15)
    return {
        "tokens": gaussian(seeds[0], (CLIPS, LEN, D), 1.0, 6.0, ((0, 8), (1, 16))),
        "w_qkv": gaussian(seeds[1], (D, 3 * D), D ** -0.5, 0.1875, ((0, 8),)),
        "qv_bias": gaussian(seeds[2], (2 * D,), 0.5, 3.0, ((0, 8),)),
        "w_out": gaussian(seeds[3], (D, D), D ** -0.5, 0.1875, ((0, 8),)),
        "out_bias": gaussian(seeds[4], (D,), 0.5, 3.0, ((0, 8),)),
        "w_up": gaussian(seeds[5], (D, FF), D ** -0.5, 0.1875, ((0, 8),)),
        "up_bias": gaussian(seeds[6], (FF,), 0.5, 3.0, ((0, 8),)),
        "w_down": gaussian(seeds[7], (FF, D), FF ** -0.5, 0.09375, ((0, 8),)),
        "down_bias": gaussian(seeds[8], (D,), 0.5, 3.0, ((0, 8),)),
        "gain_one": jnp.clip(1.0 + 0.1 * jax.random.normal(seeds[9], (D,), jnp.float32), 0.5, 1.5).astype(jnp.bfloat16),
        "shift_one": gaussian(seeds[10], (D,), 0.5, 3.0, ((0, 8),)),
        "gain_two": jnp.clip(1.0 + 0.1 * jax.random.normal(seeds[11], (D,), jnp.float32), 0.5, 1.5).astype(jnp.bfloat16),
        "shift_two": gaussian(seeds[12], (D,), 0.5, 3.0, ((0, 8),)),
        "cotangent": gaussian(seeds[13], (CLIPS, LEN, D), 1.0, 6.0, ((0, 8), (1, 16))),
    }


EPS = 1e-06
HIGH = lax.Precision.HIGHEST

@jax.custom_vjp
def low(v):
    return lax.optimization_barrier(v.astype(jnp.bfloat16)).astype(jnp.float32)

@jax.custom_vjp
def low_back(v):
    return v

def low_keep(v):
    return (low(v), None)

def low_pass(kept, grad):
    return (grad,)

def back_keep(v):
    return (v, None)

def back_low(kept, grad):
    return (low(grad),)
low.defvjp(low_keep, low_pass)
low_back.defvjp(back_keep, back_low)

def norm_rows(values, gain, shift):
    center = values - lax.optimization_barrier(jnp.mean(values, axis=-1, keepdims=True))
    spread = lax.optimization_barrier(jnp.mean(center * center, axis=-1, keepdims=True))
    return center * lax.rsqrt(spread + EPS) * gain + shift

def matmul(left, right):
    return jnp.dot(left, right, precision=HIGH)

def attend(queries, keys, values):
    length, heads, width = queries.shape
    block = min(512, length)
    scale = width ** (-0.5)

    def one_block(query_part):
        raw = low_back(jnp.einsum('bhd,khd->hbk', query_part, keys, precision=HIGH))
        prob = jax.nn.softmax(raw * scale, axis=-1)
        return jnp.einsum('hbk,khd->bhd', low(prob), values, precision=HIGH)
    blocks = queries.reshape(length // block, block, heads, width)
    return lax.map(jax.checkpoint(one_block), blocks).reshape(length, heads * width)

def layer(x, w_qkv, qv_bias, w_out, out_bias, w_up, up_bias, w_down, down_bias, gain_one, shift_one, gain_two, shift_two):
    length = x.shape[0]
    width = x.shape[1]
    head_width = width // H
    normed_one = low(norm_rows(x, gain_one, shift_one))
    bias_all = jnp.concatenate([qv_bias[:width], jnp.zeros((width,), jnp.float32), qv_bias[width:]])
    qkv = low_back(low(matmul(normed_one, w_qkv) + bias_all))
    queries = qkv[:, :width].reshape(length, H, head_width)
    keys = qkv[:, width:2 * width].reshape(length, H, head_width)
    values = qkv[:, 2 * width:].reshape(length, H, head_width)
    attended = low_back(low(attend(queries, keys, values)))
    branch_one = low_back(matmul(attended, w_out) + out_bias)
    mid = x + branch_one
    normed_two = low(norm_rows(mid, gain_two, shift_two))
    pre = low_back(matmul(normed_two, w_up) + up_bias)
    act = low(jax.nn.gelu(pre, approximate=False))
    branch_two = low_back(matmul(act, w_down) + down_bias)
    return mid + branch_two

def reference(tokens, w_qkv, qv_bias, w_out, out_bias, w_up, up_bias, w_down, down_bias, gain_one, shift_one, gain_two, shift_two, cotangent):
    params = [p.astype(jnp.float32) for p in (w_qkv, qv_bias, w_out, out_bias, w_up, up_bias, w_down, down_bias, gain_one, shift_one, gain_two, shift_two)]
    inputs = tokens.astype(jnp.float32)

    def forward(x_all, *weights):
        return lax.map(lambda clip: layer(clip, *weights), x_all)
    result, pull = jax.vjp(forward, inputs, *params)
    grads = pull(cotangent.astype(jnp.float32))
    return (result.astype(jnp.bfloat16), grads[0].astype(jnp.bfloat16), grads[1], grads[2], grads[3], grads[4], grads[5], grads[6], grads[7], grads[8], grads[9], grads[10], grads[11], grads[12])
```

```python
import functools

import jax
import jax.numpy as jnp
from jax import lax
from jax.experimental import pallas as pl
from jax.experimental.pallas import tpu as pltpu
from jax.sharding import PartitionSpec as P

MESH = pl.DeviceIdType.MESH
EPS = 1e-06
BF = jnp.bfloat16
F32 = jnp.float32
D = 1024
T = 128
VMEM = pltpu.VMEM
ANY = pl.ANY
DMA = pltpu.SemaphoreType.DMA


class Place:
    def __init__(self):
        self.i, self.j = lax.axis_index("dp"), lax.axis_index("seq")
        self.zh, self.y = self.i // 4, self.i % 4
        self.zl, self.xc = self.j // 8, self.j % 8
        self.x, self.c = self.xc // 2, self.xc % 2
        self.z = self.zh * 2 + self.zl

    def in_group(self, dx, dc):
        return (self.i, self.zl * 8 + ((self.x + dx) % 4) * 2 + (self.c + dc) % 2)

    def sibling(self):
        return self.in_group(0, 1)

    def across(self):
        return (self.i, (1 - self.zl) * 8 + self.xc)

    def along_y(self, dy):
        return (self.zh * 4 + (self.y + dy) % 4, self.j)

    def along_z(self, dz):
        z = (self.z + dz) % 4
        return ((z // 2) * 4 + self.y, (z % 2) * 8 + self.xc)

    def holder(self, dh, dy):
        near = (self.zl + dh) % 2
        return (((self.zh + dh) % 2) * 4 + (self.y + dy) % 4, near * 8 + self.xc)


GROUP = [(dx, dc) for dx in range(4) for dc in range(2) if (dx, dc) != (0, 0)]
RING = [(1, 0), (3, 0), (2, 0), (0, 1)]
HOLDERS = [(dh, dy) for dh in range(2) for dy in range(4) if (dh, dy) != (0, 0)]


def greet(devices, more=0):
    barrier = pltpu.get_barrier_semaphore()
    for device in devices:
        pl.semaphore_signal(barrier, inc=1, device_id=device, device_id_type=MESH)
    pl.semaphore_wait(barrier, len(devices) + more)


class Lines:
    def __init__(self, send, recv):
        self.send, self.recv, self.used = send, recv, 0

    def copy(self, src, dst, device):
        k = self.used
        self.used += 1
        return pltpu.make_async_remote_copy(
            src_ref=src,
            dst_ref=dst,
            send_sem=self.send.at[k],
            recv_sem=self.recv.at[k],
            device_id=device,
            device_id_type=MESH,
        )


def gather_group(at, lines, own, slots):
    started = []
    for dx in (1, 3, 2):
        copy = lines.copy(own, slots.at[at.xc], at.in_group(dx, 0))
        copy.start()
        started.append((dx, copy))
    beside = lines.copy(own, slots.at[at.xc], at.sibling())
    beside.start()

    def finish():
        forwards = []
        for dx, copy in started:
            copy.wait_recv()
            slot = ((at.x + 4 - dx) % 4) * 2 + at.c
            forward = lines.copy(slots.at[slot], slots.at[slot], at.sibling())
            forward.start()
            forwards.append(forward)
        beside.wait()
        for forward in forwards:
            forward.wait()
        for _, copy in started:
            copy.wait_send()

    return finish


def reduce_group(at, lines, parts, from_core, sums, from_ring):
    order = (2, 1, 3, 0)
    cores = {}
    for dx in order:
        slot = ((at.x + dx) % 4) * 2 + 1 - at.c
        cores[dx] = lines.copy(parts.at[slot], from_core.at[dx], at.sibling())
        cores[dx].start()
    ring = []
    for dx in order[:3]:
        slot = ((at.x + dx) % 4) * 2 + at.c
        cores[dx].wait_recv()
        sums[dx] = (parts[slot].astype(F32) + from_core[dx].astype(F32)).astype(BF)
        copy = lines.copy(sums.at[dx], from_ring.at[dx], at.in_group(dx, 0))
        copy.start()
        ring.append((dx, copy))

    def finish():
        cores[0].wait_recv()
        total = parts[at.xc].astype(F32) + from_core[0].astype(F32)
        for dx, copy in ring:
            copy.wait_recv()
            total = total + from_ring[dx].astype(F32)
        for dx in order:
            cores[dx].wait_send()
        for _, copy in ring:
            copy.wait_send()
        return total

    return finish


REDUCE_SCRATCH = [VMEM((4, T, D), BF), VMEM((4, T, D), BF), VMEM((4, T, D), BF)]


def normed(values):
    center = values - jnp.mean(values, axis=-1, keepdims=True)
    rstd = lax.rsqrt(jnp.mean(center * center, axis=-1, keepdims=True) + EPS)
    return center * rstd, rstd


def lanes_of(head, value):
    lane = lax.broadcasted_iota(jnp.int32, (1, 128), 1)
    mine = (lane < 64) if head == 0 else (lane >= 64)
    return jnp.where(mine, value, 0.0).astype(F32)


def by_head(zero, one):
    lane = lax.broadcasted_iota(jnp.int32, (1, 128), 1)
    return jnp.where(lane < 64, zero, one)


def dot(a, b, ca, cb):
    return lax.dot_general(a, b, (((ca,), (cb,)), ((), ())), preferred_element_type=F32)


QB = 256


def head_kernel(
    tok, cot, wq, wu, wd, wo, vec,
    n1, cg, wqg, wug, wdg, wog, vg, q, k, v, kr, vr, att, lse,
    xg, rows, bias, top, total, send, recv, local,
):
    at = Place()
    greet(
        [at.in_group(*d) for d in RING]
        + [at.holder(*d) for d in HOLDERS]
        + [at.across()]
    )
    lines = Lines(send, recv)
    first = []
    for dh, dy in HOLDERS:
        for src, dst in ((vec, vg.at[at.i]), (wq, wqg.at[at.i])):
            copy = lines.copy(src, dst, at.holder(dh, dy))
            copy.start()
            first.append(copy)
    x_done = gather_group(at, lines, tok, xg)
    own = [
        pltpu.make_async_copy(src, dst, local.at[n])
        for n, (src, dst) in enumerate(
            (
                (cot, cg.at[at.xc]),
                (wu, wug.at[at.i]),
                (wd, wdg.at[at.i]),
                (wo, wog.at[at.i, at.c]),
            )
        )
    ]
    for copy in own:
        copy.start()
    xg[at.xc] = tok[...]
    vg[at.i] = vec[...]
    wqg[at.i] = wq[...]
    later, halves = [], []
    for dh, dy in HOLDERS:
        device = at.holder(dh, dy)
        copy = lines.copy(wo, wog.at[at.i, at.c], device)
        copy.start()
        halves.append((dh, dy, copy))
        for src, dst in ((wu, wug.at[at.i]), (wd, wdg.at[at.i])):
            copy = lines.copy(src, dst, device)
            copy.start()
            later.append(copy)
    beside = lines.copy(wo, wog.at[at.i, at.c], at.sibling())
    beside.start()
    later.append(beside)
    for copy in first:
        copy.wait()
    for d in range(8):
        for r in range(2):
            rows[r : r + 1, d * 128 : (d + 1) * 128] = vg[d, 2 + r : 3 + r, :].astype(F32)
    for d in range(8):
        bias[d] = vg[d].astype(F32)
    x_done()
    cot_done = gather_group(at, lines, cot, cg)

    gain, shift = rows[0:1, :], rows[1:2, :]

    def norm_step(b, _):
        hat, _ = normed(xg[b].astype(F32))
        n1[b] = (hat * gain + shift).astype(BF)
        return 0

    lax.fori_loop(0, 8, norm_step, 0)
    at_row = pl.ds(10 + at.xc % 2, 1)
    q_bias = bias[at.xc // 2, at_row, :]
    v_bias = bias[4 + at.xc // 2, at_row, :]

    def kv_step(b, _):
        part = pl.ds(pl.multiple_of(b * T, T), T)
        acc = dot(n1[b], wqg[...].reshape(D, 384), 1, 0)
        q[part, :] = (acc[:, 0:128] + q_bias).astype(BF)
        k[part, :] = acc[:, 128:256].astype(BF)
        v[part, :] = (acc[:, 256:384] + v_bias).astype(BF)
        return 0

    lax.fori_loop(0, 8, kv_step, 0)
    swaps = [lines.copy(k, kr, at.across()), lines.copy(v, vr, at.across())]
    for copy in swaps:
        copy.start()

    def attend(keys, values, fresh):
        def step(t, _):
            part = pl.ds(pl.multiple_of(t * QB, QB), QB)
            block = q[part, :]
            tops, sums, outs, fades = [], [], [], []
            for h in range(2):
                mine = block * lanes_of(h, 0.125).astype(BF)
                score = dot(mine, keys[...], 1, 1)
                peak = jnp.max(score, axis=-1, keepdims=True)
                if not fresh:
                    old = top[part, 64 * h : 64 * h + 1]
                    peak = jnp.maximum(old, peak)
                    fades.append(jnp.exp(old - peak))
                expo = jnp.exp(score - peak)
                tops.append(peak)
                sums.append(jnp.sum(expo, axis=-1, keepdims=True))
                outs.append(dot(expo.astype(BF), values[...], 1, 0))
            peak, added, out = by_head(*tops), by_head(*sums), by_head(*outs)
            if fresh:
                top[part, :] = peak
                lse[part, :] = added
                total[part, :] = out
            else:
                fade = by_head(*fades)
                mass = lse[part, :] * fade + added
                att[part, :] = ((total[part, :] * fade + out) / mass).astype(BF)
                lse[part, :] = peak + jnp.log(mass)
            return 0

        lax.fori_loop(0, 1024 // QB, step, 0)

    attend(k, v, True)
    for copy in swaps:
        copy.wait()
    attend(kr, vr, False)
    cot_done()
    forwards = []
    for dh, dy, copy in halves:
        copy.wait_recv()
        holder = ((at.zh + dh) % 2) * 4 + (at.y + 4 - dy) % 4
        forward = lines.copy(wog.at[holder, at.c], wog.at[holder, at.c], at.sibling())
        forward.start()
        forwards.append(forward)
    for copy in later:
        copy.wait()
    for _, _, copy in halves:
        copy.wait_send()
    for copy in forwards:
        copy.wait()
    for copy in own:
        copy.wait()


def any_spec():
    return pl.BlockSpec(memory_space=ANY)


def vm_spec():
    return pl.BlockSpec(memory_space=VMEM)


def shape(*dims, of=BF):
    return jax.ShapeDtypeStruct(dims, of)


def call(kernel, name, ident, ins, outs, scratch, args):
    return pl.pallas_call(
        kernel,
        name=name,
        in_specs=[any_spec() if s == "a" else vm_spec() for s in ins],
        out_specs=[any_spec() if s == "a" else vm_spec() for s, _ in outs],
        out_shape=[o for _, o in outs],
        scratch_shapes=scratch,
        compiler_params=pltpu.CompilerParams(
            collective_id=ident, has_side_effects=True, vmem_limit_bytes=52 * 2**20
        ),
    )(*args)


def mid_kernel(att, x, wout, rows, mid, n2g, mixed, own, send, recv):
    at = Place()
    greet([at.in_group(*d) for d in GROUP])
    lines = Lines(send, recv)
    mine = pl.ds(pl.multiple_of(at.xc * 128, 128), 128)
    copies = []
    for dx, dc in GROUP:
        to = ((at.x + dx) % 4) * 2 + (at.c + dc) % 2
        copy = lines.copy(
            att.at[pl.ds(pl.multiple_of(to * T, T), T)], mixed.at[:, mine], at.in_group(dx, dc)
        )
        copy.start()
        copies.append(copy)
    mixed[:, mine] = att[pl.ds(pl.multiple_of(at.xc * T, T), T), :]
    for copy in copies:
        copy.wait()
    middle = x[...].astype(F32) + dot(mixed[...], wout[...], 1, 0) + rows[0:1, :]
    mid[...] = middle
    hat, _ = normed(middle)
    own[...] = (hat * rows[1:2, :] + rows[2:3, :]).astype(BF)
    done = gather_group(at, lines, own, n2g)
    n2g[at.xc] = own[...]
    done()


def back_kernel(parts, mid, cot, rows, dmid, dbg, sums, own, core, part, ring, send, recv):
    at = Place()
    greet([at.in_group(*d) for d in RING])
    lines = Lines(send, recv)
    finish = reduce_group(at, lines, parts, core, part, ring)
    hat, rstd = normed(mid[...])
    pulled = finish()
    sums[0:1, :] = jnp.sum(pulled * hat, axis=0, keepdims=True)
    sums[1:2, :] = jnp.sum(pulled, axis=0, keepdims=True)
    scaled = pulled * rows[1:2, :]
    inner = jnp.mean(scaled * hat, axis=-1, keepdims=True)
    middle = cot[...].astype(F32) + rstd * (
        scaled - jnp.mean(scaled, axis=-1, keepdims=True) - hat * inner
    )
    dmid[...] = middle
    low = middle.astype(BF)
    own[...] = low
    done = gather_group(at, lines, own, dbg)
    dbg[at.xc] = low
    low = low.astype(F32)
    sums[2:3, :] = jnp.sum(low, axis=0, keepdims=True)
    sums[3:4, :] = jnp.sum(cot[...].astype(F32), axis=0, keepdims=True)
    sums[4:8, :] = jnp.zeros((4, D), F32)
    done()


def pull_kernel(
    db, wout, att, q, k, v, kr, vr, lse,
    wog, dqkv,
    do, delta, dq, dk, dv, away, back, send, recv,
):
    at = Place()
    greet([at.across()])
    lines = Lines(send, recv)
    rows_w = wout[pl.ds(pl.multiple_of(at.xc * 128, 128), 128), :]
    grads = dot(db[...], rows_w, 1, 1).astype(BF)
    do[...] = grads
    wog[...] = dot(att[...], db[...], 0, 0).astype(BF)
    both = grads.astype(F32) * att[...].astype(F32)
    delta[...] = by_head(
        jnp.sum(both * lanes_of(0, 1.0), axis=-1, keepdims=True),
        jnp.sum(both * lanes_of(1, 1.0), axis=-1, keepdims=True),
    )

    def pull(keys, values, fresh):
        dk[...] = jnp.zeros_like(dk)
        dv[...] = jnp.zeros_like(dv)

        def step(t, _):
            part = pl.ds(pl.multiple_of(t * QB, QB), QB)
            block, grad = q[part, :], do[part, :]
            outs = []
            for h in range(2):
                mine = block * lanes_of(h, 0.125).astype(BF)
                pulled = grad * lanes_of(h, 1.0).astype(BF)
                prob = jnp.exp(dot(mine, keys[...], 1, 1) - lse[part, 64 * h : 64 * h + 1])
                dprob = dot(pulled, values[...], 1, 1)
                raw = (prob * (dprob - delta[part, 64 * h : 64 * h + 1])).astype(BF)
                dv[...] += dot(pulled, prob.astype(BF), 0, 0)
                dk[...] += dot(mine, raw, 0, 0)
                outs.append(dot(raw, keys[...], 1, 0))
            out = by_head(*outs) * 0.125
            dq[part, :] = out if fresh else dq[part, :] + out
            return 0

        lax.fori_loop(0, 1024 // QB, step, 0)

    pull(kr, vr, True)
    away[0] = dk[...].astype(BF)
    away[1] = dv[...].astype(BF)
    swap = lines.copy(away, back, at.across())
    swap.start()
    pull(k, v, False)
    swap.wait()
    dqkv[:, 0:128] = dq[...].astype(BF)
    dqkv[:, 128:256] = jnp.transpose(dk[...] + back[0].astype(F32)).astype(BF)
    dqkv[:, 256:384] = jnp.transpose(dv[...] + back[1].astype(F32)).astype(BF)


RA, RB, CA = 64, 48, 896


def last_kernel(
    parts, ends, ga, gb, tok, dmid, mid, rows,
    xgrad, result, wide, tall, vecs,
    core, part, ring, core2, part2, ring2, ra, rb, sa, sb, ra2, rb2, low, turn, row, send, recv,
):
    at = Place()
    swapped = (at.xc, at.zl * 8 + at.i)
    barrier = pltpu.get_barrier_semaphore()

    @pl.when(at.i != at.xc)
    def _():
        pl.semaphore_signal(barrier, inc=1, device_id=swapped, device_id_type=MESH)

    greet(
        [at.in_group(*d) for d in GROUP]
        + [at.along_y(d) for d in (1, 2, 3)]
        + [at.along_z(d) for d in (1, 2, 3)],
        jnp.where(at.i != at.xc, 1, 0),
    )
    lines = Lines(send, recv)
    first_a, first_b = [], []
    for d in (2, 1, 3):
        copy = lines.copy(ga.at[:, (at.y + d) % 4], ra.at[d - 1], at.along_y(d))
        copy.start()
        first_a.append((d, copy))
        z = (at.z + d) % 4
        copy = lines.copy(gb.at[z // 2, :, z % 2], rb.at[d - 1], at.along_z(d))
        copy.start()
        first_b.append((d, copy))
    finish = reduce_group(at, lines, parts, core, part, ring)
    finish2 = reduce_group(at, lines, ends, core2, part2, ring2)

    for d, copy in first_a:
        copy.wait_recv()
    for zh in range(2):
        for zl in range(2):
            acc = ga[zh, at.y, zl].astype(F32)
            for d in range(3):
                acc = acc + ra[d, zh, zl].astype(F32)
            sa[zh * 2 + zl] = acc.astype(BF)
    second = []
    for d in (2, 1, 3):
        copy = lines.copy(sa.at[(at.z + d) % 4], ra2.at[d - 1], at.along_z(d))
        copy.start()
        second.append(copy)
    for d, copy in first_b:
        copy.wait_recv()
    for y in range(4):
        acc = gb[at.zh, y, at.zl].astype(F32)
        for d in range(3):
            acc = acc + rb[d, y].astype(F32)
        sb[y] = acc.astype(BF)
    for d in (2, 1, 3):
        copy = lines.copy(sb.at[(at.y + d) % 4], rb2.at[d - 1], at.along_y(d))
        copy.start()
        second.append(copy)

    pulled = finish()
    hat, rstd = normed(tok[...].astype(F32))
    scaled = pulled * rows[3:4, :]
    inner = jnp.mean(scaled * hat, axis=-1, keepdims=True)
    xgrad[...] = (
        dmid[...] + rstd * (scaled - jnp.mean(scaled, axis=-1, keepdims=True) - hat * inner)
    ).astype(BF)
    result[...] = (mid[...] + finish2() + rows[4:5, :]).astype(BF)

    for copy in second:
        copy.wait_recv()
    acc = sa[at.z].astype(F32)
    for d in range(3):
        acc = acc + ra2[d].astype(F32)
    for b in range(8):
        low[b] = acc[b * 8 : (b + 1) * 8, :]
    acc = sb[at.y].astype(F32)
    for d in range(3):
        acc = acc + rb2[d].astype(F32)
    tall[0:32, :] = acc[0:32, :]
    turn[...] = acc[32:40, :]
    row[...] = acc[40:48, :]
    third = []
    for dx, dc in GROUP:
        to = ((at.x + dx) % 4) * 2 + (at.c + dc) % 2
        for src, dst in ((low.at[to], wide.at[at.xc]), (row, vecs.at[at.xc])):
            copy = lines.copy(src, dst, at.in_group(dx, dc))
            copy.start()
            third.append(copy)
    wide[at.xc] = low[at.xc]
    vecs[at.xc] = row[...]
    across = lines.copy(turn, tall.at[32:40, :], swapped)

    @pl.when(at.i != at.xc)
    def _():
        across.start()
        across.wait()

    @pl.when(at.i == at.xc)
    def _():
        tall[32:40, :] = turn[...]

    for copy in third:
        copy.wait()
    for _, copy in first_a + first_b:
        copy.wait_send()
    for copy in second:
        copy.wait_send()


def exact_gelu(values):
    return jax.nn.gelu(values, approximate=False)


def on_device(
    tokens, w_qkv, qv_bias, w_out, out_bias, w_up, up_bias, w_down, down_bias,
    gain_one, shift_one, gain_two, shift_two, cotangent,
):
    i, j = lax.axis_index("dp"), lax.axis_index("seq")
    zl, xc = j // 8, j % 8
    c = j % 2
    x, cot = tokens[0], cotangent[0]
    wq = jnp.concatenate(
        [lax.dynamic_slice_in_dim(w_qkv, n * D + xc * 128, 128, axis=1) for n in range(3)], axis=1
    )
    at_row = lax.broadcasted_iota(jnp.int32, (1024, 128), 0)
    at_col = lax.broadcasted_iota(jnp.int32, (1024, 128), 1)
    pick = (
        at_row == (at_col // 64) * 512 + ((at_col // 32) % 2) * 256 + xc * 32 + at_col % 32
    ).astype(BF)
    wu = jnp.concatenate(
        [
            jnp.dot(w_up[:, n * 1024 : (n + 1) * 1024], pick, preferred_element_type=F32).astype(BF)
            for n in range(4)
        ],
        axis=1,
    )
    wd = lax.dynamic_index_in_dim(w_down.reshape(2, 8, 32, D), xc, axis=1, keepdims=False)
    wd = wd.reshape(64, D)
    wo = lax.dynamic_slice_in_dim(w_out, c * 64, 64, axis=0)
    vec = jnp.concatenate(
        [
            out_bias, down_bias, gain_one, shift_one, gain_two, shift_two, up_bias, qv_bias,
            jnp.zeros((512,), BF),
        ]
    ).reshape(16, 128)
    n_lines = 14 + 14 + 21 + 1 + 2 + 7
    (n1, cg, wqg, wug, wdg, wog, vg, q, k, v, kr, vr, att, lse) = call(
        head_kernel, "gather_and_attend", 1, "vavaaav",
        [
            ("v", shape(8, T, D)), ("a", shape(8, T, D)), ("v", shape(8, 128, 384)),
            ("a", shape(8, 128, 512)), ("a", shape(8, 64, D)), ("a", shape(8, 2, 64, D)),
            ("v", shape(8, 16, 128)),
            *[("v", shape(1024, 128))] * 6,
            ("v", shape(1024, 128, of=F32)),
        ],
        [
            VMEM((8, T, D), BF), VMEM((8, D), F32), VMEM((8, 16, 128), F32),
            VMEM((1024, 128), F32), VMEM((1024, 128), F32),
            DMA((n_lines,)), DMA((n_lines,)), DMA((4,)),
        ],
        (x, cot, wq, wu, wd, wo, vec),
    )
    full_out = wog.reshape(D, D)
    flat = vg[:, :6].astype(F32)
    flat = jnp.moveaxis(flat, 1, 0).reshape(6, D)
    rows = jnp.stack([flat[0], flat[4], flat[5], flat[2], flat[1], flat[0], flat[0], flat[0]])
    ub = lax.dynamic_index_in_dim(vg[:, 6:10].reshape(8, 2, 8, 32), xc, axis=2, keepdims=False)
    ub = ub.reshape(512).astype(F32)
    mid, n2g = call(
        mid_kernel, "project_and_norm", 2, "vvvv",
        [("v", shape(T, D, of=F32)), ("v", shape(8, T, D))],
        [VMEM((T, D), BF), VMEM((T, D), BF), DMA((14,)), DMA((14,))],
        (att, x, full_out, rows),
    )
    n2 = n2g.reshape(D, D)
    cot_all = cg.reshape(D, D)
    w_up_here, w_down_here = wug.reshape(D, 512), wdg.reshape(512, D)
    pre = jnp.dot(n2, w_up_here, preferred_element_type=F32) + ub
    gelu, pull = jax.vjp(exact_gelu, pre)
    act = gelu.astype(BF)
    grad_act = dot(cot_all, w_down_here, 1, 1)
    grad_pre = pull(grad_act)[0].astype(BF)
    part_norm = dot(grad_pre, w_up_here, 1, 1).astype(BF).reshape(8, T, D)
    ends = jnp.dot(act, w_down_here, preferred_element_type=F32).astype(BF).reshape(8, T, D)
    dmid, dbg, sums = call(
        back_kernel, "norm_two_back", 3, "vvvv",
        [("v", shape(T, D, of=F32)), ("v", shape(8, T, D)), ("v", shape(8, D, of=F32))],
        [VMEM((T, D), BF), *REDUCE_SCRATCH, DMA((14,)), DMA((14,))],
        (part_norm, mid, cot, rows),
    )
    wdown_grad = dot(act, cot_all, 0, 0)
    wup_grad = dot(n2, grad_pre, 0, 0)
    up_sum = jnp.sum(grad_pre.astype(F32), axis=0)
    wout_grad, dqkv = call(
        pull_kernel, "attention_back", 4, "v" * 9,
        [("v", shape(128, D)), ("v", shape(D, 384))],
        [
            VMEM((1024, 128), BF), VMEM((1024, 128), F32), VMEM((1024, 128), F32),
            VMEM((128, 1024), F32), VMEM((128, 1024), F32),
            VMEM((2, 128, 1024), BF), VMEM((2, 128, 1024), BF), DMA((1,)), DMA((1,)),
        ],
        (dbg.reshape(D, D), full_out, att, q, k, v, kr, vr, lse),
    )
    wq_all = wqg.reshape(D, 384)
    part_one = dot(dqkv, wq_all, 1, 1).astype(BF).reshape(8, T, D)
    wqkv_grad = dot(n1.reshape(D, D), dqkv, 0, 0)
    qkv_sum = jnp.sum(dqkv.astype(F32), axis=0)
    shift_sum = jnp.sum(wq_all.astype(F32) * qkv_sum, axis=1)
    both_sum = jnp.sum(wq_all.astype(F32) * wqkv_grad, axis=1)
    gain_sum = (both_sum - flat[3] * shift_sum) / flat[2]
    vectors = jnp.stack([sums[2], sums[3], gain_sum, shift_sum, sums[0], sums[1]])
    vectors = jnp.moveaxis(vectors.reshape(6, 16, 64), 1, 0).reshape(16, 384)
    n = lax.broadcasted_iota(jnp.int32, (16, 1), 0)
    qv = jnp.where(n == xc, qkv_sum[0:128], jnp.where(n == 8 + xc, qkv_sum[256:384], 0.0))
    line = jnp.concatenate(
        [vectors, up_sum.reshape(16, 32), qv, jnp.zeros((16, 480), F32)], axis=1
    )
    ga = jnp.concatenate([wqkv_grad, wup_grad], axis=1).astype(BF).reshape(2, 4, 2, RA, CA)
    turned = jnp.moveaxis(wout_grad.reshape(2, 8, 8, D), 0, 1).reshape(16, 8, D)
    gb = jnp.concatenate(
        [
            wdown_grad.astype(BF).reshape(16, 32, D), turned,
            jnp.broadcast_to(line[:, None].astype(BF), (16, 8, D)),
        ],
        axis=1,
    ).reshape(2, 4, 2, RB, D)
    lines = 6 + 14 + 6 + 14 + 1
    xgrad, result, wide, tall, vecs = call(
        last_kernel, "reduce_gradients", 5, "v" * 8,
        [
            ("v", shape(T, D)), ("v", shape(T, D)), ("v", shape(8, 8, CA, of=F32)),
            ("v", shape(40, D, of=F32)), ("v", shape(8, 8, D, of=F32)),
        ],
        [
            *REDUCE_SCRATCH, *REDUCE_SCRATCH,
            VMEM((3, 2, 2, RA, CA), BF), VMEM((3, 4, RB, D), BF),
            VMEM((4, RA, CA), BF), VMEM((4, RB, D), BF),
            VMEM((3, RA, CA), BF), VMEM((3, RB, D), BF),
            VMEM((8, 8, CA), F32), VMEM((8, D), F32), VMEM((8, D), F32),
            DMA((lines,)), DMA((lines,)),
        ],
        (part_one, ends, ga, gb, x, dmid, mid, rows),
    )
    own = jnp.sum(vecs[:, 0, :], axis=0)
    small = lax.dynamic_slice_in_dim(own[:384].reshape(6, 64), xc * 8, 8, axis=1)
    up_bias_grad = lax.dynamic_index_in_dim(vecs[:, 0, 384:416], xc, axis=0, keepdims=False)
    qv_grad = lax.dynamic_slice_in_dim(own[416:544], xc * 16, 16, axis=0)
    w_qkv_grad = jnp.transpose(wide[:, :, :384].reshape(8, 8, 3, 128), (1, 2, 0, 3)).reshape(8, 3 * D)
    w_up_grad = jnp.transpose(
        wide[:, :, 384:].reshape(8, 8, 8, 2, 32), (1, 2, 3, 0, 4)
    ).reshape(8, 4 * D)
    return (
        result[None], xgrad[None], w_qkv_grad, qv_grad, tall[32:40], small[0], w_up_grad,
        up_bias_grad, tall[:32], small[1], small[2], small[3], small[4], small[5],
    )


def solution(mesh):
    return jax.shard_map(
        on_device,
        mesh=mesh,
        in_specs=(
            P("dp", "seq", None), P("dp", None), P("dp"), P("dp", None), P("dp"), P("dp", None),
            P("dp"), P("dp", None), P("dp"), P("dp"), P("dp"), P("dp"), P("dp"),
            P("dp", "seq", None),
        ),
        out_specs=(
            P("dp", "seq", None), P("dp", "seq", None), P(("dp", "seq"), None), P(("dp", "seq")),
            P(("dp", "seq"), None), P(("dp", "seq")), P(("dp", "seq"), None), P(("dp", "seq")),
            P(("dp", "seq"), None), P(("dp", "seq")), P(("dp", "seq")), P(("dp", "seq")),
            P(("dp", "seq")), P(("dp", "seq")),
        ),
        check_vma=False,
    )
```

```python
import functools

import jax
import jax.numpy as jnp
from jax import lax
from jax.experimental import pallas as pl
from jax.experimental.pallas import tpu as pltpu
from jax.sharding import PartitionSpec as P

MESH = pl.DeviceIdType.MESH
EPS = 1e-06
BF = jnp.bfloat16
F32 = jnp.float32
D = 1024
T = 128
VMEM = pltpu.VMEM
ANY = pl.ANY
DMA = pltpu.SemaphoreType.DMA


class Place:
    def __init__(self):
        self.i, self.j = lax.axis_index("dp"), lax.axis_index("seq")
        self.zh, self.y = self.i // 4, self.i % 4
        self.zl, self.xc = self.j // 8, self.j % 8
        self.x, self.c = self.xc // 2, self.xc % 2
        self.z = self.zh * 2 + self.zl

    def in_group(self, dx, dc):
        return (self.i, self.zl * 8 + ((self.x + dx) % 4) * 2 + (self.c + dc) % 2)

    def sibling(self):
        return self.in_group(0, 1)

    def across(self):
        return (self.i, (1 - self.zl) * 8 + self.xc)

    def along_y(self, dy):
        return (self.zh * 4 + (self.y + dy) % 4, self.j)

    def along_z(self, dz):
        z = (self.z + dz) % 4
        return ((z // 2) * 4 + self.y, (z % 2) * 8 + self.xc)

    def holder(self, dh, dy):
        near = (self.zl + dh) % 2
        return (((self.zh + dh) % 2) * 4 + (self.y + dy) % 4, near * 8 + self.xc)


GROUP = [(dx, dc) for dx in range(4) for dc in range(2) if (dx, dc) != (0, 0)]
RING = [(1, 0), (3, 0), (2, 0), (0, 1)]
HOLDERS = [(dh, dy) for dh in range(2) for dy in range(4) if (dh, dy) != (0, 0)]


def greet(devices, more=0):
    barrier = pltpu.get_barrier_semaphore()
    for device in devices:
        pl.semaphore_signal(barrier, inc=1, device_id=device, device_id_type=MESH)
    pl.semaphore_wait(barrier, len(devices) + more)


class Lines:
    def __init__(self, send, recv):
        self.send, self.recv, self.used = send, recv, 0

    def copy(self, src, dst, device):
        k = self.used
        self.used += 1
        return pltpu.make_async_remote_copy(
            src_ref=src,
            dst_ref=dst,
            send_sem=self.send.at[k],
            recv_sem=self.recv.at[k],
            device_id=device,
            device_id_type=MESH,
        )


def slot_of(ref, k, size=T):
    return ref.at[pl.ds(pl.multiple_of(k * size, size), size)]


class Gather:
    def __init__(self, at, lines, own, slot):
        self.at, self.lines, self.slot = at, lines, slot
        self.ring, self.forwards = {}, {}
        for dx in (1, 3, 2):
            self.ring[dx] = lines.copy(own, slot(at.xc), at.in_group(dx, 0))
            self.ring[dx].start()
        self.beside = lines.copy(own, slot(at.xc), at.sibling())
        self.beside.start()

    def forward(self, dx):
        at = self.at
        self.ring[dx].wait_recv()
        here = self.slot(((at.x + 4 - dx) % 4) * 2 + at.c)
        self.forwards[dx] = self.lines.copy(here, here, at.sibling())
        self.forwards[dx].start()

    def arrived(self, dx):
        (self.forwards[dx] if dx else self.beside).wait_recv()

    def sent(self):
        self.beside.wait_send()
        for dx in (1, 3, 2):
            self.forwards[dx].wait_send()
            self.ring[dx].wait_send()

    def finish(self):
        for dx in (1, 3, 2):
            self.forward(dx)
        for dx in (0, 1, 3, 2):
            self.arrived(dx)
        self.sent()


class Reduce:
    def __init__(self, at, lines, slot, from_core, sums, from_ring):
        self.at, self.lines, self.slot = at, lines, slot
        self.from_core, self.sums, self.from_ring = from_core, sums, from_ring
        self.cores, self.ring = {}, {}

    def core(self, dx):
        at = self.at
        theirs = self.slot(((at.x + dx) % 4) * 2 + 1 - at.c)
        self.cores[dx] = self.lines.copy(theirs, self.from_core.at[dx], at.sibling())
        self.cores[dx].start()

    def pass_on(self, dx):
        at = self.at
        self.cores[dx].wait_recv()
        mine = self.slot(((at.x + dx) % 4) * 2 + at.c)
        self.sums[dx] = (mine[...].astype(F32) + self.from_core[dx].astype(F32)).astype(BF)
        copy = self.lines.copy(self.sums.at[dx], self.from_ring.at[dx], at.in_group(dx, 0))
        copy.start()
        self.ring[dx] = copy

    def total(self):
        self.cores[0].wait_recv()
        total = self.slot(self.at.xc)[...].astype(F32) + self.from_core[0].astype(F32)
        for dx, copy in self.ring.items():
            copy.wait_recv()
            total = total + self.from_ring[dx].astype(F32)
        return total

    def sent(self):
        for copy in [*self.cores.values(), *self.ring.values()]:
            copy.wait_send()


REDUCE_SCRATCH = [VMEM((4, T, D), BF), VMEM((4, T, D), BF), VMEM((4, T, D), BF)]


def normed(values):
    center = values - jnp.mean(values, axis=-1, keepdims=True)
    rstd = lax.rsqrt(jnp.mean(center * center, axis=-1, keepdims=True) + EPS)
    return center * rstd, rstd


def lanes_of(head, value):
    lane = lax.broadcasted_iota(jnp.int32, (1, 128), 1)
    mine = (lane < 64) if head == 0 else (lane >= 64)
    return jnp.where(mine, value, 0.0).astype(F32)


def by_head(zero, one):
    lane = lax.broadcasted_iota(jnp.int32, (1, 128), 1)
    return jnp.where(lane < 64, zero, one)


def dot(a, b, ca, cb):
    return lax.dot_general(a, b, (((ca,), (cb,)), ((), ())), preferred_element_type=F32)


QB = 256


def head_kernel(
    tok, cot, wq, wu, wd, wo, vec,
    n1, cg, wqg, wug, wdg, wog, vg, q, k, v, kr, vr, att, lse,
    xg, rows, bias, top, total, send, recv, local,
):
    at = Place()
    greet(
        [at.in_group(*d) for d in RING]
        + [at.holder(*d) for d in HOLDERS]
        + [at.across()]
    )
    lines = Lines(send, recv)
    first = []
    for dh, dy in HOLDERS:
        for src, dst in ((vec, vg.at[at.i]), (wq, wqg.at[at.i])):
            copy = lines.copy(src, dst, at.holder(dh, dy))
            copy.start()
            first.append(copy)
    x_in = Gather(at, lines, tok, lambda k: xg.at[k])
    own = [
        pltpu.make_async_copy(src, dst, local.at[n])
        for n, (src, dst) in enumerate(
            (
                (cot, cg.at[at.xc]),
                (wu, wug.at[at.i]),
                (wd, wdg.at[at.i]),
                (wo, wog.at[at.i, at.c]),
            )
        )
    ]
    for copy in own:
        copy.start()
    xg[at.xc] = tok[...]
    vg[at.i] = vec[...]
    wqg[at.i] = wq[...]
    later, halves = [], []
    for dh, dy in HOLDERS:
        device = at.holder(dh, dy)
        copy = lines.copy(wo, wog.at[at.i, at.c], device)
        copy.start()
        halves.append((dh, dy, copy))
        for src, dst in ((wu, wug.at[at.i]), (wd, wdg.at[at.i])):
            copy = lines.copy(src, dst, device)
            copy.start()
            later.append(copy)
    beside = lines.copy(wo, wog.at[at.i, at.c], at.sibling())
    beside.start()
    later.append(beside)
    for copy in first:
        copy.wait()
    for d in range(8):
        for r in range(2):
            rows[r : r + 1, d * 128 : (d + 1) * 128] = vg[d, 2 + r : 3 + r, :].astype(F32)
    for d in range(8):
        bias[d] = vg[d].astype(F32)
    x_in.finish()
    cot_in = Gather(at, lines, cot, lambda k: cg.at[k])

    gain, shift = rows[0:1, :], rows[1:2, :]

    def norm_step(b, _):
        hat, _ = normed(xg[b].astype(F32))
        n1[b] = (hat * gain + shift).astype(BF)
        return 0

    lax.fori_loop(0, 8, norm_step, 0)
    at_row = pl.ds(10 + at.xc % 2, 1)
    q_bias = bias[at.xc // 2, at_row, :]
    v_bias = bias[4 + at.xc // 2, at_row, :]

    def kv_step(b, _):
        part = pl.ds(pl.multiple_of(b * T, T), T)
        acc = dot(n1[b], wqg[...].reshape(D, 384), 1, 0)
        q[part, :] = (acc[:, 0:128] + q_bias).astype(BF)
        k[part, :] = acc[:, 128:256].astype(BF)
        v[part, :] = (acc[:, 256:384] + v_bias).astype(BF)
        return 0

    lax.fori_loop(0, 8, kv_step, 0)
    swaps = [lines.copy(k, kr, at.across()), lines.copy(v, vr, at.across())]
    for copy in swaps:
        copy.start()

    def attend(keys, values, fresh):
        def step(t, _):
            part = pl.ds(pl.multiple_of(t * QB, QB), QB)
            block = q[part, :]
            tops, sums, outs, fades = [], [], [], []
            for h in range(2):
                mine = block * lanes_of(h, 0.125).astype(BF)
                score = dot(mine, keys[...], 1, 1)
                peak = jnp.max(score, axis=-1, keepdims=True)
                if not fresh:
                    old = top[part, 64 * h : 64 * h + 1]
                    peak = jnp.maximum(old, peak)
                    fades.append(jnp.exp(old - peak))
                expo = jnp.exp(score - peak)
                tops.append(peak)
                sums.append(jnp.sum(expo, axis=-1, keepdims=True))
                outs.append(dot(expo.astype(BF), values[...], 1, 0))
            peak, added, out = by_head(*tops), by_head(*sums), by_head(*outs)
            if fresh:
                top[part, :] = peak
                lse[part, :] = added
                total[part, :] = out
            else:
                fade = by_head(*fades)
                mass = lse[part, :] * fade + added
                att[part, :] = ((total[part, :] * fade + out) / mass).astype(BF)
                lse[part, :] = peak + jnp.log(mass)
            return 0

        lax.fori_loop(0, 1024 // QB, step, 0)

    attend(k, v, True)
    for copy in swaps:
        copy.wait()
    attend(kr, vr, False)
    cot_in.finish()
    forwards = []
    for dh, dy, copy in halves:
        copy.wait_recv()
        holder = ((at.zh + dh) % 2) * 4 + (at.y + 4 - dy) % 4
        forward = lines.copy(wog.at[holder, at.c], wog.at[holder, at.c], at.sibling())
        forward.start()
        forwards.append(forward)
    for copy in later:
        copy.wait()
    for _, _, copy in halves:
        copy.wait_send()
    for copy in forwards:
        copy.wait()
    for copy in own:
        copy.wait()


def any_spec():
    return pl.BlockSpec(memory_space=ANY)


def vm_spec():
    return pl.BlockSpec(memory_space=VMEM)


def shape(*dims, of=BF):
    return jax.ShapeDtypeStruct(dims, of)


def call(kernel, name, ident, ins, outs, scratch, args):
    return pl.pallas_call(
        kernel,
        name=name,
        in_specs=[any_spec() if s == "a" else vm_spec() for s in ins],
        out_specs=[any_spec() if s == "a" else vm_spec() for s, _ in outs],
        out_shape=[o for _, o in outs],
        scratch_shapes=scratch,
        compiler_params=pltpu.CompilerParams(
            collective_id=ident, has_side_effects=True, vmem_limit_bytes=52 * 2**20
        ),
    )(*args)


def norm_back(pulled, hat, rstd, gain):
    scaled = pulled * gain
    inner = jnp.mean(scaled * hat, axis=-1, keepdims=True)
    return rstd * (scaled - jnp.mean(scaled, axis=-1, keepdims=True) - hat * inner)


def mlp_kernel(
    att, x, cot, rows, ub, wout_at, wu_at, wd_at, cg_at,
    mid, dmid, dbg, ends, wup_grad, wdown_grad, sums, up_sum,
    wout, wu, wd, cg, mixed, own, low, n2g, act, dpre, parts, core, part, ring, local, send, recv,
):
    at = Place()
    loads = [
        pltpu.make_async_copy(src, dst, local.at[n])
        for n, (src, dst) in enumerate(((wout_at, wout), (wu_at, wu), (wd_at, wd), (cg_at, cg)))
    ]
    for load in loads:
        load.start()
    greet([at.in_group(*d) for d in GROUP])
    lines = Lines(send, recv)
    mine = pl.ds(pl.multiple_of(at.xc * 128, 128), 128)
    copies = []
    for dx, dc in GROUP:
        to = ((at.x + dx) % 4) * 2 + (at.c + dc) % 2
        copy = lines.copy(slot_of(att, to), mixed.at[:, mine], at.in_group(dx, dc))
        copy.start()
        copies.append(copy)
    mixed[:, mine] = slot_of(att, at.xc)[...]
    loads[0].wait()
    for copy in copies:
        copy.wait_recv()
    middle = x[...].astype(F32) + dot(mixed[...], wout[...], 1, 0) + rows[0:1, :]
    mid[...] = middle
    hat, rstd = normed(middle)
    own[...] = (hat * rows[4:5, :] + rows[5:6, :]).astype(BF)
    tokens_in = Gather(at, lines, own, lambda k: slot_of(n2g, k))
    slot_of(n2g, at.xc)[...] = own[...]
    for load in loads[1:]:
        load.wait()
    up_sum[...] = jnp.zeros_like(up_sum)
    out = Reduce(at, lines, lambda k: slot_of(parts, k), core, part, ring)

    def pair(dx):
        here = pl.ds(pl.multiple_of(((at.x + 4 - dx) % 4) * 256, 256), 256)
        pre = dot(n2g[here, :], wu[...], 1, 0) + ub[...]
        grad = dot(cg[here, :], wd[...], 1, 1)
        cdf = 0.5 * (1.0 + lax.erf(pre * (0.5**0.5)))
        act[here, :] = (pre * cdf).astype(BF)
        slope = cdf + pre * (jnp.exp(-0.5 * pre * pre) * 0.3989422804014327)
        back = (grad * slope).astype(BF)
        dpre[here, :] = back
        up_sum[...] += jnp.sum(back.astype(F32), axis=0, keepdims=True)
        parts[here, :] = dot(back, wu[...], 1, 1).astype(BF)
        out.core((4 - dx) % 4)

    tokens_in.arrived(0)
    pair(0)
    tokens_in.forward(1)
    tokens_in.forward(3)
    tokens_in.arrived(1)
    pair(1)
    tokens_in.forward(2)
    tokens_in.arrived(3)
    pair(3)
    out.pass_on(3)
    tokens_in.arrived(2)
    pair(2)
    out.pass_on(1)
    out.pass_on(2)

    def end_step(b, _):
        here = pl.ds(pl.multiple_of(b * 256, 256), 256)
        ends[here, :] = dot(act[here, :], wd[...], 1, 0).astype(BF)
        return 0

    lax.fori_loop(0, 4, end_step, 0)
    wdown_grad[...] = dot(act[...], cg[...], 0, 0).astype(BF)
    pulled = out.total()
    sums[4:5, :] = jnp.sum(pulled * hat, axis=0, keepdims=True)
    sums[5:6, :] = jnp.sum(pulled, axis=0, keepdims=True)
    given = cot[...].astype(F32)
    middle = given + norm_back(pulled, hat, rstd, rows[4:5, :])
    dmid[...] = middle
    low[...] = middle.astype(BF)
    back_in = Gather(at, lines, low, lambda k: slot_of(dbg, k))
    slot_of(dbg, at.xc)[...] = low[...]
    sums[0:1, :] = jnp.sum(low[...].astype(F32), axis=0, keepdims=True)
    sums[1:2, :] = jnp.sum(given, axis=0, keepdims=True)
    sums[2:4, :] = jnp.zeros((2, D), F32)
    sums[6:8, :] = jnp.zeros((2, D), F32)
    wup_grad[...] = dot(n2g[...], dpre[...], 0, 0).astype(BF)
    back_in.finish()
    tokens_in.sent()
    out.sent()
    for copy in copies:
        copy.wait_send()


class Halving:
    def __init__(self, at, lines, whole, first, sums, second, y_first, cut=None):
        self.at, self.lines, self.whole, self.y_first = at, lines, whole, y_first
        self.first, self.sums, self.second = first, sums, second
        self.cut = () if cut is None else (slice(None),) * 2 + (cut,)
        self.one, self.two = [], []

    def block(self, y, z):
        return self.whole[(z // 2, y, z % 2) + self.cut[2:]]

    def start(self):
        at = self.at
        for d in (2, 1, 3):
            if self.y_first:
                to, device = (slice(None), (at.y + d) % 4, slice(None)), at.along_y(d)
            else:
                z = (at.z + d) % 4
                to, device = (z // 2, slice(None), z % 2), at.along_z(d)
            copy = self.lines.copy(self.whole.at[to + self.cut[2:]], self.first.at[d - 1], device)
            copy.start()
            self.one.append(copy)

    def turn(self):
        at = self.at
        for copy in self.one:
            copy.wait_recv()
        for n in range(4):
            acc = self.block(at.y, n) if self.y_first else self.block(n, at.z)
            acc = acc.astype(F32)
            for d in range(3):
                got = self.first[d, n // 2, n % 2] if self.y_first else self.first[d, n]
                acc = acc + got.astype(F32)
            self.sums[n] = acc.astype(self.sums.dtype)
        for d in (2, 1, 3):
            if self.y_first:
                to, device = (at.z + d) % 4, at.along_z(d)
            else:
                to, device = (at.y + d) % 4, at.along_y(d)
            copy = self.lines.copy(self.sums.at[to], self.second.at[d - 1], device)
            copy.start()
            self.two.append(copy)

    def total(self):
        for copy in self.two:
            copy.wait_recv()
        acc = self.sums[self.at.z if self.y_first else self.at.y].astype(F32)
        for d in range(3):
            acc = acc + self.second[d].astype(F32)
        return acc

    def sent(self):
        for copy in self.one + self.two:
            copy.wait_send()


def halving_scratch(y_first, dims, of=BF):
    lead = (3, 2, 2) if y_first else (3, 4)
    return [VMEM(lead + dims, of), VMEM((4,) + dims, of), VMEM((3,) + dims, of)]


def pull_kernel(
    db_at, wout_at, n1_at, wq_at, att, q, k, v, kr, vr, lse,
    ends, wup_grad, wdown_grad, tok, dmid, mid, rows, sums, up_sum,
    xgrad, result, wide_q, wide_u, wdown_out, wout_out, small,
    db, wout, n1, wq,
    do, delta, dq, dk, dv, away, back, dqkv, parts,
    core, part, ring, core2, part2, ring2,
    wout_grad, wqkv_grad, points,
    u1, u2, u3, d1, d2, d3, o1, o2, o3, p1, p2, p3, g1, g2, g3, v1, v2, v3,
    low_u, low_q, turn, point, local, send, recv,
):
    at = Place()
    loads = [
        pltpu.make_async_copy(src, dst, local.at[n])
        for n, (src, dst) in enumerate(((db_at, db), (wout_at, wout), (n1_at, n1), (wq_at, wq)))
    ]
    for load in loads:
        load.start()
    swapped = (at.xc, at.zl * 8 + at.i)
    barrier = pltpu.get_barrier_semaphore()

    @pl.when(at.i != at.xc)
    def _():
        pl.semaphore_signal(barrier, inc=1, device_id=swapped, device_id_type=MESH)

    greet(
        [at.in_group(*d) for d in GROUP]
        + [at.along_y(d) for d in (1, 2, 3)]
        + [at.along_z(d) for d in (1, 2, 3)],
        jnp.where(at.i != at.xc, 1, 0),
    )
    lines = Lines(send, recv)
    ups = Halving(at, lines, wup_grad, u1, u2, u3, True)
    downs = Halving(at, lines, wdown_grad, d1, d2, d3, False)
    outs = Halving(at, lines, wout_grad, o1, o2, o3, False)
    ups.start()
    downs.start()
    closing = Reduce(at, lines, lambda n: slot_of(ends, n), core2, part2, ring2)
    for dx in (2, 1, 3, 0):
        closing.core(dx)
    for load in loads:
        load.wait()
    rows_w = wout[pl.ds(pl.multiple_of(at.xc * 128, 128), 128), :]
    grads = dot(db[...], rows_w, 1, 1).astype(BF)
    do[...] = grads
    made = dot(att[...], db[...], 0, 0)
    for zl in range(2):
        for i in range(8):
            b = (zl * 8 + i) * 8
            wout_grad[i // 4, i % 4, zl] = made[b : b + 8, :]
    outs.start()
    both = grads.astype(F32) * att[...].astype(F32)
    delta[...] = by_head(
        jnp.sum(both * lanes_of(0, 1.0), axis=-1, keepdims=True),
        jnp.sum(both * lanes_of(1, 1.0), axis=-1, keepdims=True),
    )
    for dx in (2, 1, 3):
        closing.pass_on(dx)

    def pull(keys, values, fresh):
        dk[...] = jnp.zeros_like(dk)
        dv[...] = jnp.zeros_like(dv)

        def step(t, _):
            part = pl.ds(pl.multiple_of(t * QB, QB), QB)
            block, grad = q[part, :], do[part, :]
            outs = []
            for h in range(2):
                mine = block * lanes_of(h, 0.125).astype(BF)
                pulled = grad * lanes_of(h, 1.0).astype(BF)
                prob = jnp.exp(dot(mine, keys[...], 1, 1) - lse[part, 64 * h : 64 * h + 1])
                dprob = dot(pulled, values[...], 1, 1)
                raw = (prob * (dprob - delta[part, 64 * h : 64 * h + 1])).astype(BF)
                dv[...] += dot(pulled, prob.astype(BF), 0, 0)
                dk[...] += dot(mine, raw, 0, 0)
                outs.append(dot(raw, keys[...], 1, 0))
            out = by_head(*outs) * 0.125
            dq[part, :] = out if fresh else dq[part, :] + out
            return 0

        lax.fori_loop(0, 1024 // QB, step, 0)

    pull(kr, vr, True)
    away[0] = dk[...].astype(BF)
    away[1] = dv[...].astype(BF)
    swap = lines.copy(away, back, at.across())
    swap.start()
    ups.turn()
    downs.turn()
    outs.turn()
    pull(k, v, False)
    swap.wait()
    dqkv[:, 0:128] = dq[...].astype(BF)
    dqkv[:, 128:256] = jnp.transpose(dk[...] + back[0].astype(F32)).astype(BF)
    dqkv[:, 256:384] = jnp.transpose(dv[...] + back[1].astype(F32)).astype(BF)

    inner = Reduce(at, lines, lambda n: slot_of(parts, n), core, part, ring)
    shift_sum = jnp.zeros((1, D), F32)
    both_sum = jnp.zeros((1, D), F32)
    before = None
    for dx in (2, 1, 3, 0):
        here = pl.ds(pl.multiple_of(((at.x + dx) % 4) * 256, 256), 256)
        made = dot(dqkv[here, :], wq[...], 1, 1)
        parts[here, :] = made.astype(BF)
        inner.core(dx)
        shift_sum = shift_sum + jnp.sum(made, axis=0, keepdims=True)
        both_sum = both_sum + jnp.sum(made * n1[here, :].astype(F32), axis=0, keepdims=True)
        if before is not None:
            inner.pass_on(before)
        before = dx
    made = dot(n1[...], dqkv[...], 0, 0).astype(BF)
    for n in range(16):
        wqkv_grad[n // 8, (n // 2) % 4, n % 2] = made[n * 64 : n * 64 + 64, :]
    firsts = Halving(at, lines, wqkv_grad, p1, p2, p3, True, slice(0, 32))
    seconds = Halving(at, lines, wqkv_grad, g1, g2, g3, False, slice(32, 64))
    firsts.start()
    seconds.start()
    qkv_sum = jnp.sum(dqkv[...].astype(F32), axis=0, keepdims=True)
    gain_sum = (both_sum - rows[3:4, :] * shift_sum) / rows[2:3, :]
    for n in range(16):
        wide = slice((n // 2) * 128, (n // 2) * 128 + 128)
        to = (n // 8, (n // 2) % 4, n % 2)
        points[to + (slice(0, 2),)] = sums[0:2, wide]
        points[to + (slice(2, 3),)] = gain_sum[:, wide]
        points[to + (slice(3, 4),)] = shift_sum[:, wide]
        points[to + (slice(4, 6),)] = sums[4:6, wide]
        points[to + (slice(6, 7),)] = up_sum[:, (n // 4) * 128 : (n // 4) * 128 + 128]
        mine = qkv_sum[:, 0:128] if n < 8 else qkv_sum[:, 256:384]
        points[to + (slice(7, 8),)] = jnp.where(at.xc == n % 8, mine, 0.0)
    vectors = Halving(at, lines, points, v1, v2, v3, True)
    vectors.start()
    third = []

    def to_group(src, dst):
        for dx, dc in GROUP:
            to = ((at.x + dx) % 4) * 2 + (at.c + dc) % 2
            copy = lines.copy(src(to), dst, at.in_group(dx, dc))
            copy.start()
            third.append(copy)

    acc = ups.total()
    for b in range(8):
        low_u[b] = acc[b * 8 : (b + 1) * 8, :]
    to_group(lambda n: low_u.at[n], wide_u.at[at.xc])
    wide_u[at.xc] = low_u[at.xc]
    wdown_out[...] = downs.total()
    turn[...] = outs.total()
    across = lines.copy(turn, wout_out, swapped)

    @pl.when(at.i != at.xc)
    def _():
        across.start()

    @pl.when(at.i == at.xc)
    def _():
        wout_out[...] = turn[...]

    result[...] = (mid[...] + closing.total() + rows[1:2, :]).astype(BF)
    vectors.turn()
    firsts.turn()
    seconds.turn()
    pulled = inner.total()
    hat, rstd = normed(tok[...].astype(F32))
    xgrad[...] = (dmid[...] + norm_back(pulled, hat, rstd, rows[2:3, :])).astype(BF)
    point[...] = vectors.total()
    to_group(lambda n: point, small.at[at.xc])
    small[at.xc] = point[...]
    for half, acc in enumerate((firsts.total(), seconds.total())):
        for b in range(4):
            low_q[half * 4 + b] = acc[b * 8 : (b + 1) * 8, :]
    to_group(lambda n: low_q.at[n], wide_q.at[at.xc])
    wide_q[at.xc] = low_q[at.xc]

    @pl.when(at.i != at.xc)
    def _():
        across.wait()

    for copy in third:
        copy.wait()
    for part_sum in (ups, downs, outs, firsts, seconds, vectors, inner, closing):
        part_sum.sent()


def lay_kernel(
    xgrad_at, result_at, wide_q, wide_u, wdown_at, wout_at, small,
    result, xgrad, wqkv, qv, wout, ob, wup, ub, wdown, db, g1, s1, g2, s2,
):
    at = Place()
    xgrad[...] = xgrad_at[...]
    result[...] = result_at[...]
    wdown[...] = wdown_at[...]
    wout[...] = wout_at[...]
    for n in range(3):
        for b in range(8):
            wqkv[:, n * D + b * 128 : n * D + b * 128 + 128] = wide_q[b, :, n * 128 : n * 128 + 128]
    lane = lax.broadcasted_iota(jnp.int32, (8, 128), 1)
    for m in range(16):
        for half in range(2):
            out = jnp.zeros((8, 128), F32)
            for b in range(4):
                word = wide_u[half * 4 + b, :, (m // 4) * 128 : (m // 4) * 128 + 128]
                turned = pltpu.roll(word, (b * 32 - (m % 4) * 32) % 128, 1)
                out = jnp.where(lane // 32 == b, turned, out)
            wup[:, m * 256 + half * 128 : m * 256 + half * 128 + 128] = out
    total = small[0]
    for b in range(1, 8):
        total = total + small[b]
    spot = at.zl * 64 + at.xc * 8
    eight = pltpu.roll(total, (128 - spot) % 128, 1)
    for k, ref in enumerate((ob, db, g1, s1, g2, s2)):
        ref[...] = eight[k : k + 1, 0:8]
    own = pltpu.roll(small[at.xc], (128 - ((at.i * 2 + at.zl) % 4) * 32) % 128, 1)
    ub[...] = own[6:7, 0:32]
    bias = pltpu.roll(total, (128 - at.xc * 16) % 128, 1)
    qv[...] = bias[7:8, 0:16]


def on_device(
    tokens, w_qkv, qv_bias, w_out, out_bias, w_up, up_bias, w_down, down_bias,
    gain_one, shift_one, gain_two, shift_two, cotangent,
):
    i, j = lax.axis_index("dp"), lax.axis_index("seq")
    zl, xc = j // 8, j % 8
    c = j % 2
    x, cot = tokens[0], cotangent[0]
    wq = jnp.concatenate(
        [lax.dynamic_slice_in_dim(w_qkv, n * D + xc * 128, 128, axis=1) for n in range(3)], axis=1
    )
    at_row = lax.broadcasted_iota(jnp.int32, (1024, 128), 0)
    at_col = lax.broadcasted_iota(jnp.int32, (1024, 128), 1)
    pick = (
        at_row == (at_col // 64) * 512 + ((at_col // 32) % 2) * 256 + xc * 32 + at_col % 32
    ).astype(BF)
    wu = jnp.concatenate(
        [
            jnp.dot(w_up[:, n * 1024 : (n + 1) * 1024], pick, preferred_element_type=F32).astype(BF)
            for n in range(4)
        ],
        axis=1,
    )
    wd = lax.dynamic_index_in_dim(w_down.reshape(2, 8, 32, D), xc, axis=1, keepdims=False)
    wd = wd.reshape(64, D)
    wo = lax.dynamic_slice_in_dim(w_out, c * 64, 64, axis=0)
    vec = jnp.concatenate(
        [
            out_bias, down_bias, gain_one, shift_one, gain_two, shift_two, up_bias, qv_bias,
            jnp.zeros((512,), BF),
        ]
    ).reshape(16, 128)
    n_lines = 14 + 14 + 21 + 1 + 2 + 7
    (n1, cg, wqg, wug, wdg, wog, vg, q, k, v, kr, vr, att, lse) = call(
        head_kernel, "gather_and_attend", 1, "vavaaav",
        [
            ("v", shape(8, T, D)), ("a", shape(8, T, D)), ("v", shape(8, 128, 384)),
            ("a", shape(8, 128, 512)), ("a", shape(8, 64, D)), ("a", shape(8, 2, 64, D)),
            ("v", shape(8, 16, 128)),
            *[("v", shape(1024, 128))] * 6,
            ("v", shape(1024, 128, of=F32)),
        ],
        [
            VMEM((8, T, D), BF), VMEM((8, D), F32), VMEM((8, 16, 128), F32),
            VMEM((1024, 128), F32), VMEM((1024, 128), F32),
            DMA((n_lines,)), DMA((n_lines,)), DMA((4,)),
        ],
        (x, cot, wq, wu, wd, wo, vec),
    )
    full_out = wog.reshape(D, D)
    flat = vg[:, :6].astype(F32)
    flat = jnp.moveaxis(flat, 1, 0).reshape(6, D)
    rows = jnp.concatenate([flat, flat[:2]])
    ub = lax.dynamic_index_in_dim(vg[:, 6:10].reshape(8, 2, 8, 32), xc, axis=2, keepdims=False)
    ub = ub.reshape(1, 512).astype(F32)
    mid, dmid, dbg, ends, wup_grad, wdown_grad, sums, up_sum = call(
        mlp_kernel, "mlp", 2, "vvvvvaaaa",
        [
            ("v", shape(T, D, of=F32)), ("v", shape(T, D, of=F32)), ("v", shape(D, D)),
            ("v", shape(D, D)), ("v", shape(D, 512)), ("v", shape(512, D)),
            ("v", shape(8, D, of=F32)), ("v", shape(1, 512, of=F32)),
        ],
        [
            VMEM((D, D), BF), VMEM((D, 512), BF), VMEM((512, D), BF), VMEM((D, D), BF),
            VMEM((T, D), BF), VMEM((T, D), BF), VMEM((T, D), BF), VMEM((D, D), BF),
            VMEM((D, 512), BF), VMEM((D, 512), BF), VMEM((D, D), BF),
            *REDUCE_SCRATCH, DMA((4,)), DMA((28,)), DMA((28,)),
        ],
        (att, x, cot, rows, ub, full_out, wug.reshape(D, 512), wdg.reshape(512, D), cg.reshape(D, D)),
    )
    lines = 7 + 7 + 6 * 6 + 1 + 21 + 1
    parts = call(
        pull_kernel, "attention_back", 3, "aaaa" + "v" * 16,
        [
            ("v", shape(T, D)), ("v", shape(T, D)), ("v", shape(8, 8, 384, of=F32)),
            ("v", shape(8, 8, 512, of=F32)), ("v", shape(32, D, of=F32)),
            ("v", shape(8, D, of=F32)), ("v", shape(8, 8, 128, of=F32)),
        ],
        [
            VMEM((D, D), BF), VMEM((D, D), BF), VMEM((D, D), BF), VMEM((D, 384), BF),
            VMEM((1024, 128), BF), VMEM((1024, 128), F32), VMEM((1024, 128), F32),
            VMEM((128, 1024), F32), VMEM((128, 1024), F32),
            VMEM((2, 128, 1024), BF), VMEM((2, 128, 1024), BF),
            VMEM((D, 384), BF), VMEM((D, D), BF),
            *REDUCE_SCRATCH, *REDUCE_SCRATCH,
            VMEM((2, 4, 2, 8, D), F32), VMEM((2, 4, 2, 64, 384), BF), VMEM((2, 4, 2, 8, 128), F32),
            *halving_scratch(True, (64, 512)), *halving_scratch(False, (32, D)),
            *halving_scratch(False, (8, D), F32), *halving_scratch(True, (32, 384)),
            *halving_scratch(False, (32, 384)), *halving_scratch(True, (8, 128), F32),
            VMEM((8, 8, 512), F32), VMEM((8, 8, 384), F32), VMEM((8, D), F32), VMEM((8, 128), F32),
            DMA((4,)), DMA((lines,)), DMA((lines,)),
        ],
        (
            dbg, full_out, n1.reshape(D, D), wqg.reshape(D, 384), att, q, k, v, kr, vr, lse,
            ends, wup_grad.reshape(2, 4, 2, 64, 512), wdown_grad.reshape(2, 4, 2, 32, D),
            x, dmid, mid, rows, sums, up_sum,
        ),
    )
    line = shape(1, 8, of=F32)
    outs = pl.pallas_call(
        lay_kernel,
        name="lay_out",
        in_specs=[vm_spec()] * 7,
        out_specs=[vm_spec()] * 14,
        out_shape=[
            shape(T, D), shape(T, D), shape(8, 3 * D, of=F32), shape(1, 16, of=F32),
            shape(8, D, of=F32), line, shape(8, 4 * D, of=F32), shape(1, 32, of=F32),
            shape(32, D, of=F32), line, line, line, line, line,
        ],
    )(*parts)
    outs = list(outs)
    for n in (0, 1):
        outs[n] = outs[n][None]
    for n in (3, 5, 7, 9, 10, 11, 12, 13):
        outs[n] = outs[n].reshape(-1)
    return tuple(outs)


def solution(mesh):
    return jax.shard_map(
        on_device,
        mesh=mesh,
        in_specs=(
            P("dp", "seq", None), P("dp", None), P("dp"), P("dp", None), P("dp"), P("dp", None),
            P("dp"), P("dp", None), P("dp"), P("dp"), P("dp"), P("dp"), P("dp"),
            P("dp", "seq", None),
        ),
        out_specs=(
            P("dp", "seq", None), P("dp", "seq", None), P(("dp", "seq"), None), P(("dp", "seq")),
            P(("dp", "seq"), None), P(("dp", "seq")), P(("dp", "seq"), None), P(("dp", "seq")),
            P(("dp", "seq"), None), P(("dp", "seq")), P(("dp", "seq")), P(("dp", "seq")),
            P(("dp", "seq")), P(("dp", "seq")),
        ),
        check_vma=False,
    )
```

```python
import functools

import jax
import jax.numpy as jnp
from jax import lax
from jax.experimental import pallas as pl
from jax.experimental.pallas import tpu as pltpu
from jax.sharding import PartitionSpec as P

MESH = pl.DeviceIdType.MESH
EPS = 1e-06
BF = jnp.bfloat16
F32 = jnp.float32
D = 1024
T = 128
VMEM = pltpu.VMEM
ANY = pl.ANY
DMA = pltpu.SemaphoreType.DMA


class Place:
    def __init__(self):
        self.i, self.j = lax.axis_index("dp"), lax.axis_index("seq")
        self.zh, self.y = self.i // 4, self.i % 4
        self.zl, self.xc = self.j // 8, self.j % 8
        self.x, self.c = self.xc // 2, self.xc % 2
        self.z = self.zh * 2 + self.zl

    def in_group(self, dx, dc):
        return (self.i, self.zl * 8 + ((self.x + dx) % 4) * 2 + (self.c + dc) % 2)

    def sibling(self):
        return self.in_group(0, 1)

    def across(self):
        return (self.i, (1 - self.zl) * 8 + self.xc)

    def along_y(self, dy):
        return (self.zh * 4 + (self.y + dy) % 4, self.j)

    def along_z(self, dz):
        z = (self.z + dz) % 4
        return ((z // 2) * 4 + self.y, (z % 2) * 8 + self.xc)

    def mirror(self):
        return ((1 - self.zh) * 4 + self.y, (1 - self.zl) * 8 + self.xc)


GROUP = [(dx, dc) for dx in range(4) for dc in range(2) if (dx, dc) != (0, 0)]
STEPS = (1, 2, 3)


def greet(devices, more=0):
    barrier = pltpu.get_barrier_semaphore()
    for device in devices:
        pl.semaphore_signal(barrier, inc=1, device_id=device, device_id_type=MESH)
    pl.semaphore_wait(barrier, len(devices) + more)


class Lines:
    def __init__(self, send, recv):
        self.send, self.recv, self.used = send, recv, 0

    def copy(self, src, dst, device):
        k = self.used
        self.used += 1
        return pltpu.make_async_remote_copy(
            src_ref=src,
            dst_ref=dst,
            send_sem=self.send.at[k],
            recv_sem=self.recv.at[k],
            device_id=device,
            device_id_type=MESH,
        )


def slot_of(ref, k, size=T):
    return ref.at[pl.ds(pl.multiple_of(k * size, size), size)]


class Gather:
    def __init__(self, at, lines, own, slot):
        self.at, self.lines, self.slot = at, lines, slot
        self.ring, self.forwards = {}, {}
        for dx in (1, 3, 2):
            self.ring[dx] = lines.copy(own, slot(at.xc), at.in_group(dx, 0))
            self.ring[dx].start()
        self.beside = lines.copy(own, slot(at.xc), at.sibling())
        self.beside.start()

    def forward(self, dx):
        at = self.at
        self.ring[dx].wait_recv()
        here = self.slot(((at.x + 4 - dx) % 4) * 2 + at.c)
        self.forwards[dx] = self.lines.copy(here, here, at.sibling())
        self.forwards[dx].start()

    def arrived(self, dx):
        (self.forwards[dx] if dx else self.beside).wait_recv()

    def sent(self):
        self.beside.wait_send()
        for dx in (1, 3, 2):
            self.forwards[dx].wait_send()
            self.ring[dx].wait_send()

    def finish(self):
        for dx in (1, 3, 2):
            self.forward(dx)
        for dx in (0, 1, 3, 2):
            self.arrived(dx)
        self.sent()


class Reduce:
    def __init__(self, at, lines, slot, from_core, sums, from_ring):
        self.at, self.lines, self.slot = at, lines, slot
        self.from_core, self.sums, self.from_ring = from_core, sums, from_ring
        self.cores, self.ring = {}, {}

    def core(self, dx):
        at = self.at
        theirs = self.slot(((at.x + dx) % 4) * 2 + 1 - at.c)
        self.cores[dx] = self.lines.copy(theirs, self.from_core.at[dx], at.sibling())
        self.cores[dx].start()

    def pass_on(self, dx):
        at = self.at
        self.cores[dx].wait_recv()
        mine = self.slot(((at.x + dx) % 4) * 2 + at.c)
        self.sums[dx] = (mine[...].astype(F32) + self.from_core[dx].astype(F32)).astype(BF)
        copy = self.lines.copy(self.sums.at[dx], self.from_ring.at[dx], at.in_group(dx, 0))
        copy.start()
        self.ring[dx] = copy

    def total(self):
        self.cores[0].wait_recv()
        total = self.slot(self.at.xc)[...].astype(F32) + self.from_core[0].astype(F32)
        for dx, copy in self.ring.items():
            copy.wait_recv()
            total = total + self.from_ring[dx].astype(F32)
        return total

    def sent(self):
        for copy in [*self.cores.values(), *self.ring.values()]:
            copy.wait_send()


REDUCE_SCRATCH = [VMEM((4, T, D), BF), VMEM((4, T, D), BF), VMEM((4, T, D), BF)]


def normed(values):
    center = values - jnp.mean(values, axis=-1, keepdims=True)
    rstd = lax.rsqrt(jnp.mean(center * center, axis=-1, keepdims=True) + EPS)
    return center * rstd, rstd


def lanes_of(head, value):
    lane = lax.broadcasted_iota(jnp.int32, (1, 128), 1)
    mine = (lane < 64) if head == 0 else (lane >= 64)
    return jnp.where(mine, value, 0.0).astype(F32)


def by_head(zero, one):
    lane = lax.broadcasted_iota(jnp.int32, (1, 128), 1)
    return jnp.where(lane < 64, zero, one)


def dot(a, b, ca, cb):
    return lax.dot_general(a, b, (((ca,), (cb,)), ((), ())), preferred_element_type=F32)


def norm_back(pulled, hat, rstd, gain):
    scaled = pulled * gain
    inner = jnp.mean(scaled * hat, axis=-1, keepdims=True)
    return rstd * (scaled - jnp.mean(scaled, axis=-1, keepdims=True) - hat * inner)


class Halving:
    def __init__(self, at, lines, whole, first, sums, second, y_first, cut=None):
        self.at, self.lines, self.whole, self.y_first = at, lines, whole, y_first
        self.first, self.sums, self.second = first, sums, second
        self.cut = () if cut is None else (slice(None),) * 2 + (cut,)
        self.one, self.two = [], []

    def block(self, y, z):
        return self.whole[(z // 2, y, z % 2) + self.cut[2:]]

    def start(self):
        at = self.at
        for d in (2, 1, 3):
            if self.y_first:
                to, device = (slice(None), (at.y + d) % 4, slice(None)), at.along_y(d)
            else:
                z = (at.z + d) % 4
                to, device = (z // 2, slice(None), z % 2), at.along_z(d)
            copy = self.lines.copy(self.whole.at[to + self.cut[2:]], self.first.at[d - 1], device)
            copy.start()
            self.one.append(copy)

    def turn(self):
        at = self.at
        for copy in self.one:
            copy.wait_recv()
        for n in range(4):
            acc = self.block(at.y, n) if self.y_first else self.block(n, at.z)
            acc = acc.astype(F32)
            for d in range(3):
                got = self.first[d, n // 2, n % 2] if self.y_first else self.first[d, n]
                acc = acc + got.astype(F32)
            self.sums[n] = acc.astype(self.sums.dtype)
        for d in (2, 1, 3):
            if self.y_first:
                to, device = (at.z + d) % 4, at.along_z(d)
            else:
                to, device = (at.y + d) % 4, at.along_y(d)
            copy = self.lines.copy(self.sums.at[to], self.second.at[d - 1], device)
            copy.start()
            self.two.append(copy)

    def total(self):
        for copy in self.two:
            copy.wait_recv()
        acc = self.sums[self.at.z if self.y_first else self.at.y].astype(F32)
        for d in range(3):
            acc = acc + self.second[d].astype(F32)
        return acc

    def sent(self):
        for copy in self.one + self.two:
            copy.wait_send()


def halving_scratch(y_first, dims, of=BF):
    lead = (3, 2, 2) if y_first else (3, 4)
    return [VMEM(lead + dims, of), VMEM((4,) + dims, of), VMEM((3,) + dims, of)]


class Spread:
    def __init__(self, at, lines, slot, z_first):
        self.at, self.lines, self.slot, self.z_first = at, lines, slot, z_first
        self.y, self.again = {}, {}

    def start(self, own=None):
        at = self.at
        own = self.slot(at.i) if own is None else own
        self.z = self.lines.copy(own, self.slot(at.i), at.mirror())
        self.z.start()
        for d in STEPS:
            self.y[d] = self.lines.copy(own, self.slot(at.i), at.along_y(d))
            self.y[d].start()

    def forward(self):
        at = self.at
        if self.z_first:
            self.z.wait_recv()
            block = self.slot((1 - at.zh) * 4 + at.y)
            for d in STEPS:
                self.again[d] = self.lines.copy(block, block, at.along_y(d))
                self.again[d].start()
        else:
            for d in STEPS:
                self.y[d].wait_recv()
                block = self.slot(at.zh * 4 + (at.y + 4 - d) % 4)
                self.again[d] = self.lines.copy(block, block, at.mirror())
                self.again[d].start()

    def arrived(self):
        for copy in self.y.values() if self.z_first else [self.z]:
            copy.wait_recv()
        for copy in self.again.values():
            copy.wait_recv()

    def sent(self):
        for copy in [self.z, *self.y.values(), *self.again.values()]:
            copy.wait_send()


def any_spec():
    return pl.BlockSpec(memory_space=ANY)


def vm_spec():
    return pl.BlockSpec(memory_space=VMEM)


def shape(*dims, of=BF):
    return jax.ShapeDtypeStruct(dims, of)


def layer_kernel(
    x, cot, vec, w_qkv, w_out, w_up, w_down,
    xgrad, result, wide_q, wide_u, wdown_out, wout_out, small,
    vg, wkv, wq, wu, wd, wo_mine, wout, w_up_here, rows, ub,
    xg, n1, cg, q, k, v, kr, vr, att, lse, top, total, mixed, mid, own, n2g, act, dpre, dmid, low, db,
    parts_a, core_a, part_a, ring_a, ends, core_b, part_b, ring_b, parts_c, core_c, part_c, ring_c,
    do, delta, dq, dk, dv, away, back, dqkv, sums, up_sum,
    wup_grad, wdown_grad, wout_grad, wqkv_grad, points,
    u1, u2, u3, d1, d2, d3, o1, o2, o3, p1, p2, p3, g1, g2, g3, v1, v2, v3,
    low_u, low_q, turn, point, local, send, recv,
):
    at = Place()
    mine = pl.ds(pl.multiple_of(at.xc * 128, 128), 128)
    loads = []

    def load(src, dst):
        loads.append(pltpu.make_async_copy(src, dst, local.at[len(loads)]))
        loads[-1].start()
        return loads[-1]

    def columns(n):
        return w_qkv.at[:, pl.ds(pl.multiple_of(n * D + at.xc * 128, 128), 128)]

    got_kv = [load(columns(n + 1), wkv.at[at.i, :, n * 128 : n * 128 + 128]) for n in range(2)]
    got_q = load(columns(0), wq.at[at.i])
    got_up = load(w_up, w_up_here)
    got_wo = load(
        w_out.at[pl.ds(pl.multiple_of(at.xc * 16, 16), 16)], wo_mine.at[at.i]
    )
    got_wd = load(w_down.at[:, at.xc], wd.at[at.i])
    swapped = (at.xc, at.zl * 8 + at.i)
    barrier = pltpu.get_barrier_semaphore()

    @pl.when(at.i != at.xc)
    def _():
        pl.semaphore_signal(barrier, inc=1, device_id=swapped, device_id_type=MESH)

    greet(
        [at.in_group(*d) for d in GROUP]
        + [at.along_y(d) for d in STEPS]
        + [at.along_z(d) for d in STEPS],
        jnp.where(at.i != at.xc, 1, 0),
    )
    lines = Lines(send, recv)
    vec_in = Spread(at, lines, lambda i: vg.at[i], True)
    kv_in = Spread(at, lines, lambda i: wkv.at[i], True)
    q_in = Spread(at, lines, lambda i: wq.at[i], True)
    wo_in = Spread(at, lines, lambda i: wo_mine.at[i], True)
    wd_in = Spread(at, lines, lambda i: wd.at[i], True)
    wu_in = Spread(at, lines, lambda i: wu.at[i], False)

    x_in = Gather(at, lines, x, lambda n: slot_of(xg, n))
    vec_in.start(vec)
    for copy in got_kv:
        copy.wait()
    kv_in.start()
    got_q.wait()
    q_in.start()
    vg[at.i] = vec[...]
    slot_of(xg, at.xc)[...] = x[...]
    slot_of(cg, at.xc)[...] = cot[...]
    vec_in.forward()
    kv_in.forward()
    got_up.wait()
    at_row = lax.broadcasted_iota(jnp.int32, (1024, 128), 0)
    at_col = lax.broadcasted_iota(jnp.int32, (1024, 128), 1)
    spot = (at_col // 64) * 512 + ((at_col // 32) % 2) * 256 + at.xc * 32 + at_col % 32
    pick = jnp.where(at_row == spot, 1.0, 0.0).astype(BF)
    for n in range(4):
        wu[at.i, :, n * 128 : n * 128 + 128] = dot(
            w_up_here[:, n * 1024 : (n + 1) * 1024], pick, 1, 0
        ).astype(BF)
    q_in.forward()
    for copy in (got_wo, got_wd):
        copy.wait()
    wo_in.start()
    wu_in.start()
    wd_in.start()
    vec_in.arrived()
    for d in range(8):
        rows[0:6, d * 128 : d * 128 + 128] = vg[d, 0:6, :]
    kv_in.arrived()
    at_k = pl.ds(10 + at.xc % 2, 1)
    q_bias = vg[at.xc // 2, at_k, :]
    v_bias = vg[4 + at.xc // 2, at_k, :]
    swaps = []

    def kv_pair(dx):
        here = pl.ds(pl.multiple_of(((at.x + 4 - dx) % 4) * 256, 256), 256)
        hat, _ = normed(xg[here, :].astype(F32))
        hat = (hat * rows[2:3, :] + rows[3:4, :]).astype(BF)
        n1[here, :] = hat
        made = dot(hat, wkv[...].reshape(D, 256), 1, 0)
        k[here, :] = made[:, 0:128].astype(BF)
        v[here, :] = (made[:, 128:256] + v_bias).astype(BF)
        for src, dst in ((k, kr), (v, vr)):
            copy = lines.copy(src.at[here], dst.at[here], at.across())
            copy.start()
            swaps.append(copy)

    x_in.forward(1)
    x_in.forward(3)
    x_in.arrived(0)
    kv_pair(0)
    x_in.forward(2)
    x_in.arrived(1)
    kv_pair(1)
    x_in.arrived(3)
    kv_pair(3)
    x_in.arrived(2)
    kv_pair(2)
    cot_in = Gather(at, lines, cot, lambda n: slot_of(cg, n))
    wo_in.forward()
    wd_in.forward()
    q_in.arrived()
    for b in range(4):
        here = slice(b * 256, b * 256 + 256)
        q[here, :] = (dot(n1[here, :], wq[...].reshape(D, 128), 1, 0) + q_bias).astype(BF)

    def attend(part, keys, values, fresh):
        block = q[part, :]
        tops, masses, outs, fades = [], [], [], []
        for h in range(2):
            score = dot(block * lanes_of(h, 0.125).astype(BF), keys[...], 1, 1)
            peak = jnp.max(score, axis=-1, keepdims=True)
            if not fresh:
                old = top[part, 64 * h : 64 * h + 1]
                peak = jnp.maximum(old, peak)
                fades.append(jnp.exp(old - peak))
            expo = jnp.exp(score - peak)
            tops.append(peak)
            masses.append(jnp.sum(expo, axis=-1, keepdims=True))
            outs.append(dot(expo.astype(BF), values[...], 1, 0))
        peak, added, out = by_head(*tops), by_head(*masses), by_head(*outs)
        if fresh:
            top[part, :] = peak
            lse[part, :] = added
            total[part, :] = out
        else:
            fade = by_head(*fades)
            mass = lse[part, :] * fade + added
            att[part, :] = ((total[part, :] * fade + out) / mass).astype(BF)
            lse[part, :] = peak + jnp.log(mass)

    def near_step(t, _):
        attend(pl.ds(pl.multiple_of(t * 512, 512), 512), k, v, True)
        return 0

    lax.fori_loop(0, 2, near_step, 0)
    wu_in.forward()
    wo_in.arrived()
    wo_own = wo_mine
    out_in = Gather(at, lines, wo_own, lambda n: wout.at[:, n])
    wout[:, at.xc] = wo_mine[...]
    cot_in.forward(1)
    cot_in.forward(3)
    for copy in swaps:
        copy.wait_recv()
    given = []
    for dx in (2, 1, 3, 0):
        attend(pl.ds(pl.multiple_of(((at.x + dx) % 4) * 256, 256), 256), kr, vr, False)
        for dc in range(2):
            if (dx, dc) != (0, 0):
                to = ((at.x + dx) % 4) * 2 + (at.c + dc) % 2
                copy = lines.copy(slot_of(att, to), mixed.at[:, mine], at.in_group(dx, dc))
                copy.start()
                given.append(copy)
    mixed[:, mine] = slot_of(att, at.xc)[...]
    cot_in.forward(2)
    for dx in (1, 3, 2):
        out_in.forward(dx)
    lane = lax.broadcasted_iota(jnp.int32, (1, 128), 1)
    for m in range(4):
        word = jnp.zeros((1, 128), F32)
        for b in range(4):
            row = vg[m * 2 + b // 2, pl.ds(6 + (b % 2) * 2 + at.xc // 4, 1), :]
            row = pltpu.roll(row, (b * 32 + 128 - (at.xc % 4) * 32) % 128, 1)
            word = jnp.where(lane // 32 == b, row, word)
        ub[:, m * 128 : m * 128 + 128] = word
    for dx in (0, 1, 3, 2):
        out_in.arrived(dx)
    for copy in given:
        copy.wait_recv()

    middle = x[...].astype(F32) + rows[0:1, :]
    middle = middle + dot(mixed[...], wout[...].reshape(D, D), 1, 0)
    mid[...] = middle
    hat, rstd = normed(middle)
    own[...] = (hat * rows[4:5, :] + rows[5:6, :]).astype(BF)
    tokens_in = Gather(at, lines, own, lambda n: slot_of(n2g, n))
    slot_of(n2g, at.xc)[...] = own[...]
    up_sum[...] = jnp.zeros_like(up_sum)
    out = Reduce(at, lines, lambda n: slot_of(parts_a, n), core_a, part_a, ring_a)
    wd_in.arrived()
    wu_in.arrived()
    for dx in (0, 1, 3, 2):
        cot_in.arrived(dx)

    def pair(dx):
        here = pl.ds(pl.multiple_of(((at.x + 4 - dx) % 4) * 256, 256), 256)
        ups = wu[...].reshape(D, 512)
        pre = dot(n2g[here, :], ups, 1, 0) + ub[...]
        grad = dot(cg[here, :], wd[...].reshape(512, D), 1, 1)
        cdf = 0.5 * (1.0 + lax.erf(pre * (0.5**0.5)))
        act[here, :] = (pre * cdf).astype(BF)
        slope = cdf + pre * (jnp.exp(-0.5 * pre * pre) * 0.3989422804014327)
        pulled = (grad * slope).astype(BF)
        dpre[here, :] = pulled
        up_sum[...] += jnp.sum(pulled.astype(F32), axis=0, keepdims=True)
        parts_a[here, :] = dot(pulled, ups, 1, 1).astype(BF)
        out.core((4 - dx) % 4)

    tokens_in.arrived(0)
    pair(0)
    tokens_in.forward(1)
    tokens_in.forward(3)
    tokens_in.arrived(1)
    pair(1)
    tokens_in.forward(2)
    tokens_in.arrived(3)
    pair(3)
    out.pass_on(3)
    tokens_in.arrived(2)
    pair(2)
    out.pass_on(1)
    out.pass_on(2)

    def end_step(b, _):
        here = pl.ds(pl.multiple_of(b * 256, 256), 256)
        ends[here, :] = dot(act[here, :], wd[...].reshape(512, D), 1, 0).astype(BF)
        return 0

    lax.fori_loop(0, 4, end_step, 0)
    made = dot(act[...], cg[...], 0, 0).astype(BF)
    for n in range(16):
        wdown_grad[n // 8, (n // 2) % 4, n % 2] = made[n * 32 : n * 32 + 32, :]
    downs = Halving(at, lines, wdown_grad, d1, d2, d3, False)
    downs.start()
    pulled = out.total()
    sums[4:5, :] = jnp.sum(pulled * hat, axis=0, keepdims=True)
    sums[5:6, :] = jnp.sum(pulled, axis=0, keepdims=True)
    middle = cot[...].astype(F32) + norm_back(pulled, hat, rstd, rows[4:5, :])
    dmid[...] = middle
    low[...] = middle.astype(BF)
    back_in = Gather(at, lines, low, lambda n: slot_of(db, n))
    slot_of(db, at.xc)[...] = low[...]
    sums[0:1, :] = jnp.sum(low[...].astype(F32), axis=0, keepdims=True)
    sums[1:2, :] = jnp.sum(cot[...].astype(F32), axis=0, keepdims=True)
    made = dot(n2g[...], dpre[...], 0, 0).astype(BF)
    for n in range(16):
        wup_grad[n // 8, (n // 2) % 4, n % 2] = made[n * 64 : n * 64 + 64, :]
    ups = Halving(at, lines, wup_grad, u1, u2, u3, True)
    ups.start()
    back_in.finish()

    outs = Halving(at, lines, wout_grad, o1, o2, o3, False)
    closing = Reduce(at, lines, lambda n: slot_of(ends, n), core_b, part_b, ring_b)
    for dx in (2, 1, 3, 0):
        closing.core(dx)
    grads = dot(db[...], wout[at.xc].reshape(128, D), 1, 1).astype(BF)
    do[...] = grads
    both = grads.astype(F32) * att[...].astype(F32)
    delta[...] = by_head(
        jnp.sum(both * lanes_of(0, 1.0), axis=-1, keepdims=True),
        jnp.sum(both * lanes_of(1, 1.0), axis=-1, keepdims=True),
    )

    def pull(keys, values, half, fresh):
        there = slice(half * 512, half * 512 + 512)
        dk[:, there] = jnp.zeros((128, 512), F32)
        dv[:, there] = jnp.zeros((128, 512), F32)

        def step(t, _):
            part = pl.ds(pl.multiple_of(t * 512, 512), 512)
            block, grad = q[part, :], do[part, :]
            made = []
            for h in range(2):
                some = block * lanes_of(h, 0.125).astype(BF)
                pulled = grad * lanes_of(h, 1.0).astype(BF)
                prob = jnp.exp(dot(some, keys[there, :], 1, 1) - lse[part, 64 * h : 64 * h + 1])
                dprob = dot(pulled, values[there, :], 1, 1)
                raw = (prob * (dprob - delta[part, 64 * h : 64 * h + 1])).astype(BF)
                dv[:, there] += dot(pulled, prob.astype(BF), 0, 0)
                dk[:, there] += dot(some, raw, 0, 0)
                made.append(dot(raw, keys[there, :], 1, 0))
            out = by_head(*made) * 0.125
            dq[part, :] = out if fresh else dq[part, :] + out
            return 0

        lax.fori_loop(0, 2, step, 0)

    returns = []
    for half in range(2):
        pull(kr, vr, half, half == 0)
        there = slice(half * 512, half * 512 + 512)
        away[half, 0] = dk[:, there].astype(BF)
        away[half, 1] = dv[:, there].astype(BF)
        copy = lines.copy(away.at[half], back.at[half], at.across())
        copy.start()
        returns.append(copy)
        if half == 0:
            for dx in (2, 1, 3):
                closing.pass_on(dx)
            made = dot(att[...], db[...], 0, 0)
            for zl in range(2):
                for i in range(8):
                    b = (zl * 8 + i) * 8
                    wout_grad[i // 4, i % 4, zl] = made[b : b + 8, :]
            outs.start()
    downs.turn()
    pull(k, v, 0, False)
    ups.turn()
    pull(k, v, 1, False)
    outs.turn()
    dqkv[:, 0:128] = dq[...].astype(BF)
    for half in range(2):
        returns[half].wait_recv()
        there = slice(half * 512, half * 512 + 512)
        for n, ref in enumerate((dk, dv)):
            made = jnp.transpose(ref[:, there] + back[half, n].astype(F32))
            dqkv[there, 128 + n * 128 : 256 + n * 128] = made.astype(BF)

    inner = Reduce(at, lines, lambda n: slot_of(parts_c, n), core_c, part_c, ring_c)
    shift_sum = jnp.zeros((1, D), F32)
    both_sum = jnp.zeros((1, D), F32)
    before = None
    for dx in (2, 1, 3, 0):
        here = pl.ds(pl.multiple_of(((at.x + dx) % 4) * 256, 256), 256)
        made = dot(dqkv[here, 0:128], wq[...].reshape(D, 128), 1, 1)
        made = made + dot(dqkv[here, 128:384], wkv[...].reshape(D, 256), 1, 1)
        parts_c[here, :] = made.astype(BF)
        inner.core(dx)
        shift_sum = shift_sum + jnp.sum(made, axis=0, keepdims=True)
        both_sum = both_sum + jnp.sum(made * n1[here, :].astype(F32), axis=0, keepdims=True)
        if before is not None:
            inner.pass_on(before)
        before = dx
    made = dot(n1[...], dqkv[...], 0, 0).astype(BF)
    for n in range(16):
        wqkv_grad[n // 8, (n // 2) % 4, n % 2] = made[n * 64 : n * 64 + 64, :]
    firsts = Halving(at, lines, wqkv_grad, p1, p2, p3, True, slice(0, 32))
    seconds = Halving(at, lines, wqkv_grad, g1, g2, g3, False, slice(32, 64))
    firsts.start()
    seconds.start()
    qkv_sum = jnp.sum(dqkv[...].astype(F32), axis=0, keepdims=True)
    gain_sum = (both_sum - rows[3:4, :] * shift_sum) / rows[2:3, :]
    for n in range(16):
        wide = slice((n // 2) * 128, (n // 2) * 128 + 128)
        to = (n // 8, (n // 2) % 4, n % 2)
        points[to + (slice(0, 2),)] = sums[0:2, wide]
        points[to + (slice(2, 3),)] = gain_sum[:, wide]
        points[to + (slice(3, 4),)] = shift_sum[:, wide]
        points[to + (slice(4, 6),)] = sums[4:6, wide]
        points[to + (slice(6, 7),)] = up_sum[:, (n // 4) * 128 : (n // 4) * 128 + 128]
        some = qkv_sum[:, 0:128] if n < 8 else qkv_sum[:, 256:384]
        points[to + (slice(7, 8),)] = jnp.where(at.xc == n % 8, some, 0.0)
    vectors = Halving(at, lines, points, v1, v2, v3, True)
    vectors.start()
    third = []

    def to_group(src, dst):
        for dx, dc in GROUP:
            to = ((at.x + dx) % 4) * 2 + (at.c + dc) % 2
            copy = lines.copy(src(to), dst, at.in_group(dx, dc))
            copy.start()
            third.append(copy)

    acc = ups.total()
    for b in range(8):
        low_u[b] = acc[b * 8 : (b + 1) * 8, :]
    to_group(lambda n: low_u.at[n], wide_u.at[at.xc])
    wide_u[at.xc] = low_u[at.xc]
    wdown_out[...] = downs.total()
    turn[...] = outs.total()
    across = lines.copy(turn, wout_out, swapped)

    @pl.when(at.i != at.xc)
    def _():
        across.start()

    @pl.when(at.i == at.xc)
    def _():
        wout_out[...] = turn[...]

    result[...] = (mid[...] + closing.total() + rows[1:2, :]).astype(BF)
    vectors.turn()
    firsts.turn()
    seconds.turn()
    pulled = inner.total()
    hat, rstd = normed(x[...].astype(F32))
    xgrad[...] = (dmid[...] + norm_back(pulled, hat, rstd, rows[2:3, :])).astype(BF)
    point[...] = vectors.total()
    to_group(lambda n: point, small.at[at.xc])
    small[at.xc] = point[...]
    for half, acc in enumerate((firsts.total(), seconds.total())):
        for b in range(4):
            low_q[half * 4 + b] = acc[b * 8 : (b + 1) * 8, :]
    to_group(lambda n: low_q.at[n], wide_q.at[at.xc])
    wide_q[at.xc] = low_q[at.xc]

    @pl.when(at.i != at.xc)
    def _():
        across.wait()

    for copy in third:
        copy.wait()
    for copy in swaps + given + returns:
        copy.wait_send()
    for flow in (
        vec_in, kv_in, q_in, wo_in, wd_in, wu_in, x_in, cot_in, out_in, tokens_in,
        ups, downs, outs, firsts, seconds, vectors, out, inner, closing,
    ):
        flow.sent()


def lay_kernel(
    xgrad_at, result_at, wide_q, wide_u, wdown_at, wout_at, small,
    result, xgrad, wqkv, qv, wout, ob, wup, ub, wdown, db, g1, s1, g2, s2,
):
    at = Place()
    xgrad[...] = xgrad_at[...]
    result[...] = result_at[...]
    wdown[...] = wdown_at[...]
    wout[...] = wout_at[...]
    for n in range(3):
        for b in range(8):
            wqkv[:, n * D + b * 128 : n * D + b * 128 + 128] = wide_q[b, :, n * 128 : n * 128 + 128]
    lane = lax.broadcasted_iota(jnp.int32, (8, 128), 1)
    for m in range(16):
        for half in range(2):
            out = jnp.zeros((8, 128), F32)
            for b in range(4):
                word = wide_u[half * 4 + b, :, (m // 4) * 128 : (m // 4) * 128 + 128]
                turned = pltpu.roll(word, (b * 32 - (m % 4) * 32) % 128, 1)
                out = jnp.where(lane // 32 == b, turned, out)
            wup[:, m * 256 + half * 128 : m * 256 + half * 128 + 128] = out
    total = small[0]
    for b in range(1, 8):
        total = total + small[b]
    spot = at.zl * 64 + at.xc * 8
    eight = pltpu.roll(total, (128 - spot) % 128, 1)
    for k, ref in enumerate((ob, db, g1, s1, g2, s2)):
        ref[...] = eight[k : k + 1, 0:8]
    own = pltpu.roll(small[at.xc], (128 - ((at.i * 2 + at.zl) % 4) * 32) % 128, 1)
    ub[...] = own[6:7, 0:32]
    bias = pltpu.roll(total, (128 - at.xc * 16) % 128, 1)
    qv[...] = bias[7:8, 0:16]


def on_device(
    tokens, w_qkv, qv_bias, w_out, out_bias, w_up, up_bias, w_down, down_bias,
    gain_one, shift_one, gain_two, shift_two, cotangent,
):
    vec, row = jnp.zeros((16, 128), F32), 0
    for vector in (
        out_bias, down_bias, gain_one, shift_one, gain_two, shift_two, up_bias, qv_bias
    ):
        lines = vector.astype(F32).reshape(-1, 128)
        vec = vec + jnp.pad(lines, ((row, 16 - row - lines.shape[0]), (0, 0)))
        row += lines.shape[0]
    block, whole, half = VMEM((T, D), BF), VMEM((D, D), BF), VMEM((D, 512), BF)
    narrow, tall = VMEM((D, 128), BF), VMEM((D, 128), F32)
    n_lines = 6 * 7 + 5 * 7 + 8 + 7 + 3 * 7 + 2 + 6 * 6 + 3 * 7 + 1
    parts = pl.pallas_call(
        layer_kernel,
        name="layer",
        in_specs=[vm_spec()] * 3 + [any_spec()] * 4,
        out_specs=[vm_spec()] * 7,
        out_shape=[
            shape(T, D), shape(T, D), shape(8, 8, 384, of=F32), shape(8, 8, 512, of=F32),
            shape(32, D, of=F32), shape(8, D, of=F32), shape(8, 8, 128, of=F32),
        ],
        scratch_shapes=[
            VMEM((8, 16, 128), F32), VMEM((8, 128, 256), BF), VMEM((8, 128, 128), BF),
            VMEM((8, 128, 512), BF), VMEM((8, 2, 32, D), BF), VMEM((8, 16, D), BF),
            VMEM((8, 8, 16, D), BF), VMEM((128, 4 * D), BF), VMEM((8, D), F32), VMEM((1, 512), F32),
            whole, whole, whole, *[narrow] * 6, *[tall] * 3, block, VMEM((T, D), F32), block,
            whole, half, half, VMEM((T, D), F32), block, whole,
            *[whole, *REDUCE_SCRATCH] * 3,
            narrow, tall, tall, VMEM((128, D), F32), VMEM((128, D), F32),
            VMEM((2, 2, 128, 512), BF), VMEM((2, 2, 128, 512), BF), VMEM((D, 384), BF),
            VMEM((8, D), F32), VMEM((1, 512), F32),
            VMEM((2, 4, 2, 64, 512), BF), VMEM((2, 4, 2, 32, D), BF), VMEM((2, 4, 2, 8, D), F32),
            VMEM((2, 4, 2, 64, 384), BF), VMEM((2, 4, 2, 8, 128), F32),
            *halving_scratch(True, (64, 512)), *halving_scratch(False, (32, D)),
            *halving_scratch(False, (8, D), F32), *halving_scratch(True, (32, 384)),
            *halving_scratch(False, (32, 384)), *halving_scratch(True, (8, 128), F32),
            VMEM((8, 8, 512), F32), VMEM((8, 8, 384), F32), VMEM((8, D), F32), VMEM((8, 128), F32),
            DMA((8,)), DMA((n_lines,)), DMA((n_lines,)),
        ],
        compiler_params=pltpu.CompilerParams(
            collective_id=1, has_side_effects=True, vmem_limit_bytes=60 * 2**20
        ),
    )(tokens[0], cotangent[0], vec, w_qkv, w_out, w_up, w_down.reshape(2, 8, 32, D))
    line = shape(1, 8, of=F32)
    outs = pl.pallas_call(
        lay_kernel,
        name="lay_out",
        in_specs=[vm_spec()] * 7,
        out_specs=[vm_spec()] * 14,
        out_shape=[
            shape(T, D), shape(T, D), shape(8, 3 * D, of=F32), shape(1, 16, of=F32),
            shape(8, D, of=F32), line, shape(8, 4 * D, of=F32), shape(1, 32, of=F32),
            shape(32, D, of=F32), line, line, line, line, line,
        ],
    )(*parts)
    outs = list(outs)
    for n in (0, 1):
        outs[n] = outs[n][None]
    for n in (3, 5, 7, 9, 10, 11, 12, 13):
        outs[n] = outs[n].reshape(-1)
    return tuple(outs)


def solution(mesh):
    return jax.shard_map(
        on_device,
        mesh=mesh,
        in_specs=(
            P("dp", "seq", None), P("dp", None), P("dp"), P("dp", None), P("dp"), P("dp", None),
            P("dp"), P("dp", None), P("dp"), P("dp"), P("dp"), P("dp"), P("dp"),
            P("dp", "seq", None),
        ),
        out_specs=(
            P("dp", "seq", None), P("dp", "seq", None), P(("dp", "seq"), None), P(("dp", "seq")),
            P(("dp", "seq"), None), P(("dp", "seq")), P(("dp", "seq"), None), P(("dp", "seq")),
            P(("dp", "seq"), None), P(("dp", "seq")), P(("dp", "seq")), P(("dp", "seq")),
            P(("dp", "seq")), P(("dp", "seq")),
        ),
        check_vma=False,
    )
```

```python
import functools

import jax
import jax.numpy as jnp
from jax import lax
from jax.experimental import pallas as pl
from jax.experimental.pallas import tpu as pltpu
from jax.sharding import PartitionSpec as P

MESH = pl.DeviceIdType.MESH
EPS = 1e-06
BF = jnp.bfloat16
F32 = jnp.float32
D = 1024
T = 128
VMEM = pltpu.VMEM
ANY = pl.ANY
DMA = pltpu.SemaphoreType.DMA


class Place:
    def __init__(self):
        self.i, self.j = lax.axis_index("dp"), lax.axis_index("seq")
        self.zh, self.y = self.i // 4, self.i % 4
        self.zl, self.xc = self.j // 8, self.j % 8
        self.x, self.c = self.xc // 2, self.xc % 2
        self.z = self.zh * 2 + self.zl
        self.fc = ((self.x + self.y) % 4) * 2 + self.c

    def in_group(self, dx, dc):
        return (self.i, self.zl * 8 + ((self.x + dx) % 4) * 2 + (self.c + dc) % 2)

    def sibling(self):
        return self.in_group(0, 1)

    def across(self):
        return (self.i, (1 - self.zl) * 8 + self.xc)

    def along_y(self, dy):
        return (self.zh * 4 + (self.y + dy) % 4, self.j)

    def on_x(self, dx):
        return self.in_group(dx, 0)

    def aslant(self, dy):
        return (
            self.zh * 4 + (self.y + dy) % 4,
            self.zl * 8 + ((self.x + 4 - dy) % 4) * 2 + self.c,
        )

    def along_z(self, dz):
        z = (self.z + dz) % 4
        return ((z // 2) * 4 + self.y, (z % 2) * 8 + self.xc)

    def mirror(self):
        return ((1 - self.zh) * 4 + self.y, (1 - self.zl) * 8 + self.xc)


GROUP = [(dx, dc) for dx in range(4) for dc in range(2) if (dx, dc) != (0, 0)]
STEPS = (1, 2, 3)


def greet(devices, more=0):
    barrier = pltpu.get_barrier_semaphore()
    for device in devices:
        pl.semaphore_signal(barrier, inc=1, device_id=device, device_id_type=MESH)
    pl.semaphore_wait(barrier, len(devices) + more)


class Lines:
    def __init__(self, send, recv):
        self.send, self.recv, self.used = send, recv, 0

    def copy(self, src, dst, device):
        k = self.used
        self.used += 1
        return pltpu.make_async_remote_copy(
            src_ref=src,
            dst_ref=dst,
            send_sem=self.send.at[k],
            recv_sem=self.recv.at[k],
            device_id=device,
            device_id_type=MESH,
        )


def slot_of(ref, k, size=T):
    return ref.at[pl.ds(pl.multiple_of(k * size, size), size)]


class Gather:
    def __init__(self, at, lines, own, put, got, to):
        self.at, self.lines, self.got = at, lines, got
        self.ring, self.forwards = {}, {}
        for dx in (1, 3, 2):
            self.ring[dx] = lines.copy(own, put(dx), to(dx))
            self.ring[dx].start()
        self.beside = lines.copy(own, put(0), at.sibling())
        self.beside.start()

    def forward(self, dx):
        self.ring[dx].wait_recv()
        here = self.got(dx)
        self.forwards[dx] = self.lines.copy(here, here, self.at.sibling())
        self.forwards[dx].start()

    def arrived(self, dx):
        (self.forwards[dx] if dx else self.beside).wait_recv()

    def sent(self):
        self.beside.wait_send()
        for dx in (1, 3, 2):
            self.forwards[dx].wait_send()
            self.ring[dx].wait_send()

    def finish(self):
        for dx in (1, 3, 2):
            self.forward(dx)
        for dx in (0, 1, 3, 2):
            self.arrived(dx)
        self.sent()


def gather_group(at, lines, own, slot):
    return Gather(
        at, lines, own,
        lambda dx: slot(at.xc),
        lambda dx: slot(((at.x + 4 - dx) % 4) * 2 + at.c),
        at.on_x,
    )


def half_of(ref, back, ring, core):
    start = back * 256 + ring * 128 + core * 64
    return ref.at[pl.ds(pl.multiple_of(start, 64), 64)]


class Halves:
    def __init__(self, at, lines, own, ref):
        self.both = [
            Gather(
                at, lines, own.at[64 * ring : 64 * ring + 64],
                lambda d, ring=ring: half_of(ref, d, ring, at.c),
                lambda d, ring=ring: half_of(ref, d, ring, at.c),
                (at.on_x, at.along_y)[ring],
            )
            for ring in range(2)
        ]
        for ring in range(2):
            half_of(ref, 0, ring, at.c)[...] = own[64 * ring : 64 * ring + 64, :]

    def forward(self, d):
        for one in self.both:
            one.forward(d)

    def arrived(self, d):
        for one in self.both:
            one.arrived(d)

    def sent(self):
        for one in self.both:
            one.sent()


class Reduce:
    def __init__(self, at, lines, slot, to, from_core, sums, from_ring):
        self.at, self.lines, self.slot, self.to = at, lines, slot, to
        self.from_core, self.sums, self.from_ring = from_core, sums, from_ring
        self.cores, self.ring = {}, {}

    def core(self, dx):
        theirs = self.slot(dx, 1 - self.at.c)
        self.cores[dx] = self.lines.copy(theirs, self.from_core.at[dx], self.at.sibling())
        self.cores[dx].start()

    def pass_on(self, dx):
        self.cores[dx].wait_recv()
        mine = self.slot(dx, self.at.c)
        self.sums[dx] = (mine[...].astype(F32) + self.from_core[dx].astype(F32)).astype(BF)
        copy = self.lines.copy(self.sums.at[dx], self.from_ring.at[dx], self.to(dx))
        copy.start()
        self.ring[dx] = copy

    def total(self):
        self.cores[0].wait_recv()
        total = self.slot(0, self.at.c)[...].astype(F32) + self.from_core[0].astype(F32)
        for dx, copy in self.ring.items():
            copy.wait_recv()
            total = total + self.from_ring[dx].astype(F32)
        return total

    def sent(self):
        for copy in [*self.cores.values(), *self.ring.values()]:
            copy.wait_send()


class ReduceHalves:
    def __init__(self, at, lines, ref, from_core, sums, from_ring):
        self.both = [
            Reduce(
                at, lines,
                lambda d, core, ring=ring: half_of(ref, (4 - d) % 4, ring, core),
                (at.on_x, at.along_y)[ring],
                from_core.at[ring], sums.at[ring], from_ring.at[ring],
            )
            for ring in range(2)
        ]

    def core(self, d):
        for one in self.both:
            one.core(d)

    def pass_on(self, d):
        for one in self.both:
            one.pass_on(d)

    def sent(self):
        for one in self.both:
            one.sent()


HALVES_SCRATCH = [VMEM((2, 4, 64, D), BF)] * 3
REDUCE_SCRATCH = [VMEM((4, T, D), BF), VMEM((4, T, D), BF), VMEM((4, T, D), BF)]


def normed(values):
    center = values - jnp.mean(values, axis=-1, keepdims=True)
    rstd = lax.rsqrt(jnp.mean(center * center, axis=-1, keepdims=True) + EPS)
    return center * rstd, rstd


def lanes_of(head, value):
    lane = lax.broadcasted_iota(jnp.int32, (1, 128), 1)
    mine = (lane < 64) if head == 0 else (lane >= 64)
    return jnp.where(mine, value, 0.0).astype(F32)


def by_head(zero, one):
    lane = lax.broadcasted_iota(jnp.int32, (1, 128), 1)
    return jnp.where(lane < 64, zero, one)


def dot(a, b, ca, cb):
    return lax.dot_general(a, b, (((ca,), (cb,)), ((), ())), preferred_element_type=F32)


def norm_back(pulled, hat, rstd, gain):
    scaled = pulled * gain
    inner = jnp.mean(scaled * hat, axis=-1, keepdims=True)
    return rstd * (scaled - jnp.mean(scaled, axis=-1, keepdims=True) - hat * inner)


class Halving:
    def __init__(self, at, lines, whole, first, sums, second, y_first, cut=None, along=None):
        self.along = at.along_y if along is None else along
        self.at, self.lines, self.whole, self.y_first = at, lines, whole, y_first
        self.first, self.sums, self.second = first, sums, second
        self.cut = () if cut is None else (slice(None),) * 2 + (cut,)
        self.one, self.two = [], []

    def block(self, y, z):
        return self.whole[(z // 2, y, z % 2) + self.cut[2:]]

    def start(self):
        at = self.at
        for d in (2, 1, 3):
            if self.y_first:
                to, device = (slice(None), (at.y + d) % 4, slice(None)), self.along(d)
            else:
                z = (at.z + d) % 4
                to, device = (z // 2, slice(None), z % 2), at.along_z(d)
            copy = self.lines.copy(self.whole.at[to + self.cut[2:]], self.first.at[d - 1], device)
            copy.start()
            self.one.append(copy)

    def turn(self):
        at = self.at
        for copy in self.one:
            copy.wait_recv()
        for n in range(4):
            acc = self.block(at.y, n) if self.y_first else self.block(n, at.z)
            acc = acc.astype(F32)
            for d in range(3):
                got = self.first[d, n // 2, n % 2] if self.y_first else self.first[d, n]
                acc = acc + got.astype(F32)
            self.sums[n] = acc.astype(self.sums.dtype)
        for d in (2, 1, 3):
            if self.y_first:
                to, device = (at.z + d) % 4, at.along_z(d)
            else:
                to, device = (at.y + d) % 4, self.along(d)
            copy = self.lines.copy(self.sums.at[to], self.second.at[d - 1], device)
            copy.start()
            self.two.append(copy)

    def total(self):
        for copy in self.two:
            copy.wait_recv()
        acc = self.sums[self.at.z if self.y_first else self.at.y].astype(F32)
        for d in range(3):
            acc = acc + self.second[d].astype(F32)
        return acc

    def sent(self):
        for copy in self.one + self.two:
            copy.wait_send()


def halving_scratch(y_first, dims, of=BF):
    lead = (3, 2, 2) if y_first else (3, 4)
    return [VMEM(lead + dims, of), VMEM((4,) + dims, of), VMEM((3,) + dims, of)]


class Spread:
    def __init__(self, at, lines, slot, z_first):
        self.at, self.lines, self.slot, self.z_first = at, lines, slot, z_first
        self.y, self.again = {}, {}

    def start(self, own=None, others=None):
        at = self.at
        own = self.slot(at.i) if own is None else own
        self.z = self.lines.copy(own, self.slot(at.i), at.mirror())
        self.z.start()
        for d in STEPS:
            block = own if others is None else others(d)
            self.y[d] = self.lines.copy(block, self.slot(at.i), at.along_y(d))
            self.y[d].start()

    def forward(self):
        at = self.at
        if self.z_first:
            self.z.wait_recv()
            block = self.slot((1 - at.zh) * 4 + at.y)
            for d in STEPS:
                self.again[d] = self.lines.copy(block, block, at.along_y(d))
                self.again[d].start()
        else:
            for d in STEPS:
                self.y[d].wait_recv()
                block = self.slot(at.zh * 4 + (at.y + 4 - d) % 4)
                self.again[d] = self.lines.copy(block, block, at.mirror())
                self.again[d].start()

    def arrived(self):
        for copy in self.y.values() if self.z_first else [self.z]:
            copy.wait_recv()
        for copy in self.again.values():
            copy.wait_recv()

    def sent(self):
        for copy in [self.z, *self.y.values(), *self.again.values()]:
            copy.wait_send()


def any_spec():
    return pl.BlockSpec(memory_space=ANY)


def vm_spec():
    return pl.BlockSpec(memory_space=VMEM)


def shape(*dims, of=BF):
    return jax.ShapeDtypeStruct(dims, of)


def layer_kernel(
    x, cot, vec, w_qkv, w_out, w_up, w_down,
    xgrad, result, wide_q, wide_u, wdown_out, wout_out, small,
    vg, wkv, wq, wu, wd, wo_mine, wout, w_up_here, picked, rows, ub,
    xg, n1, cg, q, k, v, kr, vr, att, lse, top, total, mixed, mid, own, n2g, act, dpre, dmid, low, db,
    parts_a, core_a, part_a, ring_a, ends, core_b, part_b, ring_b, parts_c, core_c, part_c, ring_c,
    do, delta, dq, dk, dv, away, back, dqkv, sums, up_sum,
    wup_grad, wdown_grad, wout_grad, wqkv_grad, points,
    u1, u2, u3, d1, d2, d3, o1, o2, o3, p1, p2, p3, g1, g2, g3, v1, v2, v3,
    low_u, low_q, turn, down_turn, point, local, send, recv,
):
    at = Place()
    mine = pl.ds(pl.multiple_of(at.xc * 128, 128), 128)
    loads = []

    def load(src, dst):
        loads.append(pltpu.make_async_copy(src, dst, local.at[len(loads)]))
        loads[-1].start()
        return loads[-1]

    def columns(n):
        return w_qkv.at[:, pl.ds(pl.multiple_of(n * D + at.xc * 128, 128), 128)]

    got_kv = [load(columns(n + 1), wkv.at[at.i, :, n * 128 : n * 128 + 128]) for n in range(2)]
    got_q = load(columns(0), wq.at[at.i])
    got_up = load(w_up, w_up_here)
    got_wo = load(
        w_out.at[pl.ds(pl.multiple_of(at.xc * 16, 16), 16)], wo_mine.at[at.i]
    )
    got_wd = load(w_down.at[:, at.fc], wd.at[at.i])
    swapped = (at.xc, at.zl * 8 + at.i)
    barrier = pltpu.get_barrier_semaphore()

    @pl.when(at.i != at.xc)
    def _():
        pl.semaphore_signal(barrier, inc=1, device_id=swapped, device_id_type=MESH)

    greet(
        [at.in_group(*d) for d in GROUP]
        + [at.along_y(d) for d in STEPS]
        + [at.along_z(d) for d in STEPS],
        jnp.where(at.i != at.xc, 1, 0),
    )
    lines = Lines(send, recv)
    vec_in = Spread(at, lines, lambda i: vg.at[i], True)
    kv_in = Spread(at, lines, lambda i: wkv.at[i], True)
    q_in = Spread(at, lines, lambda i: wq.at[i], True)
    wo_in = Spread(at, lines, lambda i: wo_mine.at[i], True)
    wd_in = Spread(at, lines, lambda i: wd.at[i], False)
    wu_in = Spread(at, lines, lambda i: wu.at[i], False)

    x_in = gather_group(at, lines, x, lambda n: slot_of(xg, n))
    vec_in.start(vec)
    for copy in got_kv:
        copy.wait()
    kv_in.start()
    got_wo.wait()
    wo_in.start()
    got_q.wait()
    q_in.start()
    vg[at.i] = vec[...]
    slot_of(xg, at.xc)[...] = x[...]
    vec_in.forward()
    kv_in.forward()
    wo_in.forward()
    q_in.forward()
    got_up.wait()
    at_row = lax.broadcasted_iota(jnp.int32, (1024, 128), 0)
    at_col = lax.broadcasted_iota(jnp.int32, (1024, 128), 1)
    spot = (at_col // 64) * 512 + ((at_col // 32) % 2) * 256 + at_col % 32

    def part_on(d):
        return ((at.x + at.y + d) % 4) * 2 + at.c

    for d in range(4):
        pick = jnp.where(at_row - spot == part_on(d) * 32, 1.0, 0.0).astype(BF)
        for n in range(4):
            picked[d, :, n * 128 : n * 128 + 128] = dot(
                w_up_here[:, n * 1024 : (n + 1) * 1024], pick, 1, 0
            ).astype(BF)
    wu[at.i] = picked[0]
    vec_in.arrived()
    for d in range(8):
        rows[0:6, d * 128 : d * 128 + 128] = vg[d, 0:6, :]
    kv_in.arrived()
    got_wd.wait()
    wu_in.start(picked.at[0], lambda d: picked.at[d])
    wd_in.start(None, lambda d: w_down.at[:, part_on(d)])
    at_k = pl.ds(10 + at.xc % 2, 1)
    q_bias = vg[at.xc // 2, at_k, :]
    v_bias = vg[4 + at.xc // 2, at_k, :]
    swaps = []

    def kv_pair(dx):
        here = pl.ds(pl.multiple_of(((at.x + 4 - dx) % 4) * 256, 256), 256)
        hat, _ = normed(xg[here, :].astype(F32))
        hat = (hat * rows[2:3, :] + rows[3:4, :]).astype(BF)
        n1[here, :] = hat
        made = dot(hat, wkv[...].reshape(D, 256), 1, 0)
        k[here, :] = made[:, 0:128].astype(BF)
        v[here, :] = (made[:, 128:256] + v_bias).astype(BF)
        for src, dst in ((k, kr), (v, vr)):
            copy = lines.copy(src.at[here], dst.at[here], at.across())
            copy.start()
            swaps.append(copy)

    x_in.forward(1)
    x_in.forward(3)
    x_in.arrived(0)
    kv_pair(0)
    x_in.forward(2)
    x_in.arrived(1)
    kv_pair(1)
    x_in.arrived(3)
    kv_pair(3)
    x_in.arrived(2)
    kv_pair(2)
    wo_in.arrived()
    out_in = gather_group(at, lines, wo_mine, lambda n: wout.at[:, n])
    wout[:, at.xc] = wo_mine[...]
    cot_in = Halves(at, lines, cot, cg)
    q_in.arrived()
    for b in range(4):
        here = slice(b * 256, b * 256 + 256)
        q[here, :] = (dot(n1[here, :], wq[...].reshape(D, 128), 1, 0) + q_bias).astype(BF)

    def attend(part, keys, values, fresh):
        block = q[part, :]
        tops, masses, outs, fades = [], [], [], []
        for h in range(2):
            score = dot(block * lanes_of(h, 0.125).astype(BF), keys[...], 1, 1)
            peak = jnp.max(score, axis=-1, keepdims=True)
            if not fresh:
                old = top[part, 64 * h : 64 * h + 1]
                peak = jnp.maximum(old, peak)
                fades.append(jnp.exp(old - peak))
            expo = jnp.exp(score - peak)
            tops.append(peak)
            masses.append(jnp.sum(expo, axis=-1, keepdims=True))
            outs.append(dot(expo.astype(BF), values[...], 1, 0))
        peak, added, out = by_head(*tops), by_head(*masses), by_head(*outs)
        if fresh:
            top[part, :] = peak
            lse[part, :] = added
            total[part, :] = out
        else:
            fade = by_head(*fades)
            mass = lse[part, :] * fade + added
            att[part, :] = ((total[part, :] * fade + out) / mass).astype(BF)
            lse[part, :] = peak + jnp.log(mass)

    def near_step(t, _):
        attend(pl.ds(pl.multiple_of(t * 512, 512), 512), k, v, True)
        return 0

    near_step(0, 0)
    wu_in.forward()
    wd_in.forward()
    near_step(1, 0)
    out_in.forward(1)
    out_in.forward(3)
    for copy in swaps:
        copy.wait_recv()
    given = []
    for dx in (2, 1, 3, 0):
        attend(pl.ds(pl.multiple_of(((at.x + dx) % 4) * 256, 256), 256), kr, vr, False)
        for dc in range(2):
            if (dx, dc) != (0, 0):
                to = ((at.x + dx) % 4) * 2 + (at.c + dc) % 2
                copy = lines.copy(slot_of(att, to), mixed.at[:, mine], at.in_group(dx, dc))
                copy.start()
                given.append(copy)
    mixed[:, mine] = slot_of(att, at.xc)[...]
    out_in.forward(2)
    for dx in (1, 3, 2):
        cot_in.forward(dx)
    lane = lax.broadcasted_iota(jnp.int32, (1, 128), 1)
    for m in range(4):
        word = jnp.zeros((1, 128), F32)
        for b in range(4):
            row = vg[m * 2 + b // 2, pl.ds(6 + (b % 2) * 2 + at.fc // 4, 1), :]
            row = pltpu.roll(row, (b * 32 + 128 - (at.fc % 4) * 32) % 128, 1)
            word = jnp.where(lane // 32 == b, row, word)
        ub[:, m * 128 : m * 128 + 128] = word
    for dx in (0, 1, 3, 2):
        out_in.arrived(dx)
    for copy in given:
        copy.wait_recv()

    middle = x[...].astype(F32) + rows[0:1, :]
    middle = middle + dot(mixed[...], wout[...].reshape(D, D), 1, 0)
    mid[...] = middle
    hat, rstd = normed(middle)
    own[...] = (hat * rows[4:5, :] + rows[5:6, :]).astype(BF)
    tokens_in = Halves(at, lines, own, n2g)
    up_sum[...] = jnp.zeros_like(up_sum)
    out = ReduceHalves(at, lines, parts_a, core_a, part_a, ring_a)
    wd_in.arrived()
    wu_in.arrived()
    for dx in (0, 1, 3, 2):
        cot_in.arrived(dx)

    def pair(dx):
        here = slice(dx * 256, dx * 256 + 256)
        ups = wu[...].reshape(D, 512)
        pre = dot(n2g[here, :], ups, 1, 0) + ub[...]
        grad = dot(cg[here, :], wd[...].reshape(512, D), 1, 1)
        cdf = 0.5 * (1.0 + lax.erf(pre * (0.5**0.5)))
        act[here, :] = (pre * cdf).astype(BF)
        slope = cdf + pre * (jnp.exp(-0.5 * pre * pre) * 0.3989422804014327)
        pulled = (grad * slope).astype(BF)
        dpre[here, :] = pulled
        up_sum[...] += jnp.sum(pulled.astype(F32), axis=0, keepdims=True)
        parts_a[here, :] = dot(pulled, ups, 1, 1).astype(BF)
        out.core((4 - dx) % 4)

    tokens_in.arrived(0)
    pair(0)
    tokens_in.forward(1)
    tokens_in.forward(3)
    tokens_in.arrived(1)
    pair(1)
    tokens_in.forward(2)
    tokens_in.arrived(3)
    pair(3)
    out.pass_on(3)
    tokens_in.arrived(2)
    pair(2)
    out.pass_on(1)
    out.pass_on(2)

    def end_step(b, _):
        here = pl.ds(pl.multiple_of(b * 256, 256), 256)
        ends[here, :] = dot(act[here, :], wd[...].reshape(512, D), 1, 0).astype(BF)
        return 0

    lax.fori_loop(0, 4, end_step, 0)
    made = dot(act[...], cg[...], 0, 0).astype(BF)
    for n in range(16):
        wdown_grad[n // 8, (n // 2) % 4, n % 2] = made[n * 32 : n * 32 + 32, :]
    downs = Halving(at, lines, wdown_grad, d1, d2, d3, False, along=at.aslant)
    downs.start()
    for ring in range(2):
        dmid[64 * ring : 64 * ring + 64, :] = out.both[ring].total()
    pulled = dmid[...]
    sums[4:5, :] = jnp.sum(pulled * hat, axis=0, keepdims=True)
    sums[5:6, :] = jnp.sum(pulled, axis=0, keepdims=True)
    middle = cot[...].astype(F32) + norm_back(pulled, hat, rstd, rows[4:5, :])
    dmid[...] = middle
    low[...] = middle.astype(BF)
    back_in = gather_group(at, lines, low, lambda n: slot_of(db, n))
    slot_of(db, at.xc)[...] = low[...]
    sums[0:1, :] = jnp.sum(low[...].astype(F32), axis=0, keepdims=True)
    sums[1:2, :] = jnp.sum(cot[...].astype(F32), axis=0, keepdims=True)
    made = dot(n2g[...], dpre[...], 0, 0).astype(BF)
    for n in range(16):
        wup_grad[n // 8, (n // 2) % 4, n % 2] = made[n * 64 : n * 64 + 64, :]
    ups = Halving(at, lines, wup_grad, u1, u2, u3, True, along=at.aslant)
    ups.start()
    back_in.finish()

    outs = Halving(at, lines, wout_grad, o1, o2, o3, True)
    closing = ReduceHalves(at, lines, ends, core_b, part_b, ring_b)
    for dx in (2, 1, 3, 0):
        closing.core(dx)
    grads = dot(db[...], wout[at.xc].reshape(128, D), 1, 1).astype(BF)
    do[...] = grads
    both = grads.astype(F32) * att[...].astype(F32)
    delta[...] = by_head(
        jnp.sum(both * lanes_of(0, 1.0), axis=-1, keepdims=True),
        jnp.sum(both * lanes_of(1, 1.0), axis=-1, keepdims=True),
    )

    def pull(keys, values, half, fresh):
        there = slice(half * 512, half * 512 + 512)
        dk[:, there] = jnp.zeros((128, 512), F32)
        dv[:, there] = jnp.zeros((128, 512), F32)

        def step(t, _):
            part = pl.ds(pl.multiple_of(t * 512, 512), 512)
            block, grad = q[part, :], do[part, :]
            made = []
            for h in range(2):
                some = block * lanes_of(h, 0.125).astype(BF)
                pulled = grad * lanes_of(h, 1.0).astype(BF)
                prob = jnp.exp(dot(some, keys[there, :], 1, 1) - lse[part, 64 * h : 64 * h + 1])
                dprob = dot(pulled, values[there, :], 1, 1)
                raw = (prob * (dprob - delta[part, 64 * h : 64 * h + 1])).astype(BF)
                dv[:, there] += dot(pulled, prob.astype(BF), 0, 0)
                dk[:, there] += dot(some, raw, 0, 0)
                made.append(dot(raw, keys[there, :], 1, 0))
            out = by_head(*made) * 0.125
            dq[part, :] = out if fresh else dq[part, :] + out
            return 0

        lax.fori_loop(0, 2, step, 0)

    returns = []
    for half in range(2):
        pull(kr, vr, half, half == 0)
        there = slice(half * 512, half * 512 + 512)
        away[half, 0] = dk[:, there].astype(BF)
        away[half, 1] = dv[:, there].astype(BF)
        copy = lines.copy(away.at[half], back.at[half], at.across())
        copy.start()
        returns.append(copy)
        if half == 0:
            for dx in (2, 1, 3):
                closing.pass_on(dx)
            made = dot(att[...], db[...], 0, 0)
            for zl in range(2):
                for i in range(8):
                    b = (zl * 8 + i) * 8
                    wout_grad[i // 4, i % 4, zl] = made[b : b + 8, :]
            outs.start()
    downs.turn()
    pull(k, v, 0, False)
    ups.turn()
    pull(k, v, 1, False)
    outs.turn()
    dqkv[:, 0:128] = dq[...].astype(BF)
    for half in range(2):
        returns[half].wait_recv()
        there = slice(half * 512, half * 512 + 512)
        for n, ref in enumerate((dk, dv)):
            made = jnp.transpose(ref[:, there] + back[half, n].astype(F32))
            dqkv[there, 128 + n * 128 : 256 + n * 128] = made.astype(BF)

    inner = Reduce(
        at, lines,
        lambda d, core: slot_of(parts_c, ((at.x + d) % 4) * 2 + core),
        at.on_x, core_c, part_c, ring_c,
    )
    shift_sum = jnp.zeros((1, D), F32)
    both_sum = jnp.zeros((1, D), F32)
    before = None
    for dx in (2, 1, 3, 0):
        here = pl.ds(pl.multiple_of(((at.x + dx) % 4) * 256, 256), 256)
        made = dot(dqkv[here, 0:128], wq[...].reshape(D, 128), 1, 1)
        made = made + dot(dqkv[here, 128:384], wkv[...].reshape(D, 256), 1, 1)
        parts_c[here, :] = made.astype(BF)
        inner.core(dx)
        shift_sum = shift_sum + jnp.sum(made, axis=0, keepdims=True)
        both_sum = both_sum + jnp.sum(made * n1[here, :].astype(F32), axis=0, keepdims=True)
        if before is not None:
            inner.pass_on(before)
        before = dx
    made = dot(n1[...], dqkv[...], 0, 0).astype(BF)
    for n in range(16):
        wqkv_grad[n // 8, (n // 2) % 4, n % 2] = made[n * 64 : n * 64 + 64, :]
    firsts = Halving(at, lines, wqkv_grad, p1, p2, p3, True, slice(0, 32))
    seconds = Halving(at, lines, wqkv_grad, g1, g2, g3, False, slice(32, 64))
    firsts.start()
    seconds.start()
    qkv_sum = jnp.sum(dqkv[...].astype(F32), axis=0, keepdims=True)
    gain_sum = (both_sum - rows[3:4, :] * shift_sum) / rows[2:3, :]
    for n in range(16):
        wide = slice((n // 2) * 128, (n // 2) * 128 + 128)
        to = (n // 8, (n // 2) % 4, n % 2)
        points[to + (slice(0, 2),)] = sums[0:2, wide]
        points[to + (slice(2, 3),)] = gain_sum[:, wide]
        points[to + (slice(3, 4),)] = shift_sum[:, wide]
        points[to + (slice(4, 6),)] = sums[4:6, wide]
        some = up_sum[:, (n // 4) * 128 : (n // 4) * 128 + 128]
        some = pltpu.roll(some, ((at.fc % 4) * 32 + 128 - (n % 4) * 32) % 128, 1)
        some = jnp.where(lane // 32 == at.fc % 4, some, 0.0)
        for b in range(2):
            points[to + (slice(6 + b, 7 + b),)] = jnp.where(at.fc // 4 == b, some, 0.0)
        some = qkv_sum[:, 0:128] if n < 8 else qkv_sum[:, 256:384]
        points[to + (slice(8, 9),)] = jnp.where(at.xc == n % 8, some, 0.0)
        points[to + (slice(9, 16),)] = jnp.zeros((7, 128), F32)
    vectors = Halving(at, lines, points, v1, v2, v3, True)
    vectors.start()
    third = []

    def to_group(src, dst):
        for dx, dc in GROUP:
            to = ((at.x + dx) % 4) * 2 + (at.c + dc) % 2
            copy = lines.copy(src(to), dst, at.in_group(dx, dc))
            copy.start()
            third.append(copy)

    acc = ups.total()
    for b in range(8):
        low_u[b] = acc[b * 8 : (b + 1) * 8, :]
    to_group(lambda n: low_u.at[n], wide_u.at[at.fc])
    wide_u[at.fc] = low_u[at.xc]
    down_turn[...] = downs.total()
    shifted = lines.copy(down_turn, wdown_out, at.on_x(at.y))

    @pl.when(at.y != 0)
    def _():
        shifted.start()

    @pl.when(at.y == 0)
    def _():
        wdown_out[...] = down_turn[...]

    turn[...] = outs.total()
    across = lines.copy(turn, wout_out, swapped)

    @pl.when(at.i != at.xc)
    def _():
        across.start()

    @pl.when(at.i == at.xc)
    def _():
        wout_out[...] = turn[...]

    for ring in range(2):
        some = slice(64 * ring, 64 * ring + 64)
        result[some, :] = (mid[some, :] + closing.both[ring].total() + rows[1:2, :]).astype(BF)
    vectors.turn()
    firsts.turn()
    seconds.turn()
    pulled = inner.total()
    hat, rstd = normed(x[...].astype(F32))
    xgrad[...] = (dmid[...] + norm_back(pulled, hat, rstd, rows[2:3, :])).astype(BF)
    point[...] = vectors.total()
    to_group(lambda n: point, small.at[at.xc])
    small[at.xc] = point[...]
    for half, acc in enumerate((firsts.total(), seconds.total())):
        for b in range(4):
            low_q[half * 4 + b] = acc[b * 8 : (b + 1) * 8, :]
    to_group(lambda n: low_q.at[n], wide_q.at[at.xc])
    wide_q[at.xc] = low_q[at.xc]

    @pl.when(at.i != at.xc)
    def _():
        across.wait()

    @pl.when(at.y != 0)
    def _():
        shifted.wait()

    for copy in third:
        copy.wait()
    for copy in swaps + given + returns:
        copy.wait_send()
    for flow in (
        vec_in, kv_in, q_in, wo_in, wd_in, wu_in, x_in, cot_in, out_in, tokens_in,
        ups, downs, outs, firsts, seconds, vectors, out, inner, closing,
    ):
        flow.sent()


def lay_kernel(
    xgrad_at, result_at, wide_q, wide_u, wdown_at, wout_at, small,
    result, xgrad, wqkv, qv, wout, ob, wup, ub, wdown, db, g1, s1, g2, s2,
):
    at = Place()
    xgrad[...] = xgrad_at[...]
    result[...] = result_at[...]
    wdown[...] = wdown_at[...]
    wout[...] = wout_at[...]
    for n in range(3):
        for b in range(8):
            wqkv[:, n * D + b * 128 : n * D + b * 128 + 128] = wide_q[b, :, n * 128 : n * 128 + 128]
    lane = lax.broadcasted_iota(jnp.int32, (8, 128), 1)
    for m in range(16):
        for half in range(2):
            out = jnp.zeros((8, 128), F32)
            for b in range(4):
                word = wide_u[half * 4 + b, :, (m // 4) * 128 : (m // 4) * 128 + 128]
                turned = pltpu.roll(word, (b * 32 - (m % 4) * 32) % 128, 1)
                out = jnp.where(lane // 32 == b, turned, out)
            wup[:, m * 256 + half * 128 : m * 256 + half * 128 + 128] = out
    total = small[0]
    for b in range(1, 8):
        total = total + small[b]
    spot = at.zl * 64 + at.xc * 8
    eight = pltpu.roll(total, (128 - spot) % 128, 1)
    for k, ref in enumerate((ob, db, g1, s1, g2, s2)):
        ref[...] = eight[k : k + 1, 0:8]
    own = jnp.where(at.xc // 4 == 0, total[6:7, :], total[7:8, :])
    ub[...] = pltpu.roll(own, (128 - (at.xc % 4) * 32) % 128, 1)[:, 0:32]
    bias = pltpu.roll(total, (128 - at.xc * 16) % 128, 1)
    qv[...] = bias[8:9, 0:16]


def on_device(
    tokens, w_qkv, qv_bias, w_out, out_bias, w_up, up_bias, w_down, down_bias,
    gain_one, shift_one, gain_two, shift_two, cotangent,
):
    vec, row = jnp.zeros((16, 128), F32), 0
    for vector in (
        out_bias, down_bias, gain_one, shift_one, gain_two, shift_two, up_bias, qv_bias
    ):
        lines = vector.astype(F32).reshape(-1, 128)
        vec = vec + jnp.pad(lines, ((row, 16 - row - lines.shape[0]), (0, 0)))
        row += lines.shape[0]
    block, whole, half = VMEM((T, D), BF), VMEM((D, D), BF), VMEM((D, 512), BF)
    narrow, tall = VMEM((D, 128), BF), VMEM((D, 128), F32)
    n_lines = 6 * 7 + 7 * 7 + 8 + 7 + 5 * 7 + 2 + 6 * 6 + 3 * 7 + 2
    parts = pl.pallas_call(
        layer_kernel,
        name="layer",
        in_specs=[vm_spec()] * 3 + [any_spec()] * 4,
        out_specs=[vm_spec()] * 7,
        out_shape=[
            shape(T, D), shape(T, D), shape(8, 8, 384, of=F32), shape(8, 8, 512, of=F32),
            shape(32, D, of=F32), shape(8, D, of=F32), shape(8, 16, 128, of=F32),
        ],
        scratch_shapes=[
            VMEM((8, 16, 128), F32), VMEM((8, 128, 256), BF), VMEM((8, 128, 128), BF),
            VMEM((8, 128, 512), BF), VMEM((8, 2, 32, D), BF), VMEM((8, 16, D), BF),
            VMEM((8, 8, 16, D), BF), VMEM((128, 4 * D), BF), VMEM((4, 128, 512), BF),
            VMEM((8, D), F32), VMEM((1, 512), F32),
            whole, whole, whole, *[narrow] * 6, *[tall] * 3, block, VMEM((T, D), F32), block,
            whole, half, half, VMEM((T, D), F32), block, whole,
            *[whole, *HALVES_SCRATCH] * 2, whole, *REDUCE_SCRATCH,
            narrow, tall, tall, VMEM((128, D), F32), VMEM((128, D), F32),
            VMEM((2, 2, 128, 512), BF), VMEM((2, 2, 128, 512), BF), VMEM((D, 384), BF),
            VMEM((8, D), F32), VMEM((1, 512), F32),
            VMEM((2, 4, 2, 64, 512), BF), VMEM((2, 4, 2, 32, D), BF), VMEM((2, 4, 2, 8, D), F32),
            VMEM((2, 4, 2, 64, 384), BF), VMEM((2, 4, 2, 16, 128), F32),
            *halving_scratch(True, (64, 512)), *halving_scratch(False, (32, D)),
            *halving_scratch(True, (8, D), F32), *halving_scratch(True, (32, 384)),
            *halving_scratch(False, (32, 384)), *halving_scratch(True, (16, 128), F32),
            VMEM((8, 8, 512), F32), VMEM((8, 8, 384), F32), VMEM((8, D), F32), VMEM((32, D), F32),
            VMEM((16, 128), F32),
            DMA((8,)), DMA((n_lines,)), DMA((n_lines,)),
        ],
        compiler_params=pltpu.CompilerParams(
            collective_id=1, has_side_effects=True, vmem_limit_bytes=60 * 2**20
        ),
    )(tokens[0], cotangent[0], vec, w_qkv, w_out, w_up, w_down.reshape(2, 8, 32, D))
    line = shape(1, 8, of=F32)
    outs = pl.pallas_call(
        lay_kernel,
        name="lay_out",
        in_specs=[vm_spec()] * 7,
        out_specs=[vm_spec()] * 14,
        out_shape=[
            shape(T, D), shape(T, D), shape(8, 3 * D, of=F32), shape(1, 16, of=F32),
            shape(8, D, of=F32), line, shape(8, 4 * D, of=F32), shape(1, 32, of=F32),
            shape(32, D, of=F32), line, line, line, line, line,
        ],
    )(*parts)
    outs = list(outs)
    for n in (0, 1):
        outs[n] = outs[n][None]
    for n in (3, 5, 7, 9, 10, 11, 12, 13):
        outs[n] = outs[n].reshape(-1)
    return tuple(outs)


def solution(mesh):
    return jax.shard_map(
        on_device,
        mesh=mesh,
        in_specs=(
            P("dp", "seq", None), P("dp", None), P("dp"), P("dp", None), P("dp"), P("dp", None),
            P("dp"), P("dp", None), P("dp"), P("dp"), P("dp"), P("dp"), P("dp"),
            P("dp", "seq", None),
        ),
        out_specs=(
            P("dp", "seq", None), P("dp", "seq", None), P(("dp", "seq"), None), P(("dp", "seq")),
            P(("dp", "seq"), None), P(("dp", "seq")), P(("dp", "seq"), None), P(("dp", "seq")),
            P(("dp", "seq"), None), P(("dp", "seq")), P(("dp", "seq")), P(("dp", "seq")),
            P(("dp", "seq")), P(("dp", "seq")),
        ),
        check_vma=False,
    )
```

```python
import functools

import jax
import jax.numpy as jnp
from jax import lax
from jax.experimental import pallas as pl
from jax.experimental.pallas import tpu as pltpu
from jax.sharding import PartitionSpec as P

MESH = pl.DeviceIdType.MESH
EPS = 1e-06
BF = jnp.bfloat16
F32 = jnp.float32
D = 1024
T = 128
VMEM = pltpu.VMEM
ANY = pl.ANY
DMA = pltpu.SemaphoreType.DMA


class Place:
    def __init__(self):
        self.i, self.j = lax.axis_index("dp"), lax.axis_index("seq")
        self.zh, self.y = self.i // 4, self.i % 4
        self.zl, self.xc = self.j // 8, self.j % 8
        self.x, self.c = self.xc // 2, self.xc % 2
        self.z = self.zh * 2 + self.zl
        self.fc = ((self.x + self.y) % 4) * 2 + self.c

    def in_group(self, dx, dc):
        return (self.i, self.zl * 8 + ((self.x + dx) % 4) * 2 + (self.c + dc) % 2)

    def sibling(self):
        return self.in_group(0, 1)

    def across(self):
        return (self.i, (1 - self.zl) * 8 + self.xc)

    def along_y(self, dy):
        return (self.zh * 4 + (self.y + dy) % 4, self.j)

    def on_x(self, dx):
        return self.in_group(dx, 0)

    def aslant(self, dy):
        return (
            self.zh * 4 + (self.y + dy) % 4,
            self.zl * 8 + ((self.x + 4 - dy) % 4) * 2 + self.c,
        )

    def along_z(self, dz):
        z = (self.z + dz) % 4
        return ((z // 2) * 4 + self.y, (z % 2) * 8 + self.xc)

    def mirror(self):
        return ((1 - self.zh) * 4 + self.y, (1 - self.zl) * 8 + self.xc)


GROUP = [(dx, dc) for dx in range(4) for dc in range(2) if (dx, dc) != (0, 0)]
STEPS = (1, 2, 3)


def greet(devices, more=0):
    barrier = pltpu.get_barrier_semaphore()
    for device in devices:
        pl.semaphore_signal(barrier, inc=1, device_id=device, device_id_type=MESH)
    pl.semaphore_wait(barrier, len(devices) + more)


class Lines:
    def __init__(self, send, recv):
        self.send, self.recv, self.used = send, recv, 0

    def copy(self, src, dst, device):
        k = self.used
        self.used += 1
        return pltpu.make_async_remote_copy(
            src_ref=src,
            dst_ref=dst,
            send_sem=self.send.at[k],
            recv_sem=self.recv.at[k],
            device_id=device,
            device_id_type=MESH,
        )


def slot_of(ref, k, size=T):
    return ref.at[pl.ds(pl.multiple_of(k * size, size), size)]


class Gather:
    def __init__(self, at, lines, own, put, got, to):
        self.at, self.lines, self.got = at, lines, got
        self.ring, self.forwards = {}, {}
        for dx in (1, 3, 2):
            self.ring[dx] = lines.copy(own, put(dx), to(dx))
            self.ring[dx].start()
        self.beside = lines.copy(own, put(0), at.sibling())
        self.beside.start()

    def forward(self, dx):
        self.ring[dx].wait_recv()
        here = self.got(dx)
        self.forwards[dx] = self.lines.copy(here, here, self.at.sibling())
        self.forwards[dx].start()

    def arrived(self, dx):
        (self.forwards[dx] if dx else self.beside).wait_recv()

    def sent(self):
        self.beside.wait_send()
        for dx in (1, 3, 2):
            self.forwards[dx].wait_send()
            self.ring[dx].wait_send()

    def finish(self):
        for dx in (1, 3, 2):
            self.forward(dx)
        for dx in (0, 1, 3, 2):
            self.arrived(dx)
        self.sent()


def gather_group(at, lines, own, slot):
    return Gather(
        at, lines, own,
        lambda dx: slot(at.xc),
        lambda dx: slot(((at.x + 4 - dx) % 4) * 2 + at.c),
        at.on_x,
    )


def half_of(ref, back, ring, core):
    start = back * 256 + ring * 128 + core * 64
    return ref.at[pl.ds(pl.multiple_of(start, 64), 64)]


class Halves:
    def __init__(self, at, lines, own, ref):
        self.both = [
            Gather(
                at, lines, own.at[64 * ring : 64 * ring + 64],
                lambda d, ring=ring: half_of(ref, d, ring, at.c),
                lambda d, ring=ring: half_of(ref, d, ring, at.c),
                (at.on_x, at.along_y)[ring],
            )
            for ring in range(2)
        ]
        for ring in range(2):
            half_of(ref, 0, ring, at.c)[...] = own[64 * ring : 64 * ring + 64, :]

    def forward(self, d):
        for one in self.both:
            one.forward(d)

    def arrived(self, d):
        for one in self.both:
            one.arrived(d)

    def sent(self):
        for one in self.both:
            one.sent()


class Reduce:
    def __init__(self, at, lines, slot, to, from_core, sums, from_ring):
        self.at, self.lines, self.slot, self.to = at, lines, slot, to
        self.from_core, self.sums, self.from_ring = from_core, sums, from_ring
        self.cores, self.ring = {}, {}

    def core(self, dx):
        theirs = self.slot(dx, 1 - self.at.c)
        self.cores[dx] = self.lines.copy(theirs, self.from_core.at[dx], self.at.sibling())
        self.cores[dx].start()

    def pass_on(self, dx):
        self.cores[dx].wait_recv()
        mine = self.slot(dx, self.at.c)
        self.sums[dx] = (mine[...].astype(F32) + self.from_core[dx].astype(F32)).astype(BF)
        copy = self.lines.copy(self.sums.at[dx], self.from_ring.at[dx], self.to(dx))
        copy.start()
        self.ring[dx] = copy

    def total(self):
        self.cores[0].wait_recv()
        total = self.slot(0, self.at.c)[...].astype(F32) + self.from_core[0].astype(F32)
        for dx, copy in self.ring.items():
            copy.wait_recv()
            total = total + self.from_ring[dx].astype(F32)
        return total

    def sent(self):
        for copy in [*self.cores.values(), *self.ring.values()]:
            copy.wait_send()


class ReduceHalves:
    def __init__(self, at, lines, ref, from_core, sums, from_ring):
        self.both = [
            Reduce(
                at, lines,
                lambda d, core, ring=ring: half_of(ref, (4 - d) % 4, ring, core),
                (at.on_x, at.along_y)[ring],
                from_core.at[ring], sums.at[ring], from_ring.at[ring],
            )
            for ring in range(2)
        ]

    def core(self, d):
        for one in self.both:
            one.core(d)

    def pass_on(self, d):
        for one in self.both:
            one.pass_on(d)

    def sent(self):
        for one in self.both:
            one.sent()


HALVES_SCRATCH = [VMEM((2, 4, 64, D), BF)] * 3
REDUCE_SCRATCH = [VMEM((4, T, D), BF), VMEM((4, T, D), BF), VMEM((4, T, D), BF)]


def normed(values):
    center = values - jnp.mean(values, axis=-1, keepdims=True)
    rstd = lax.rsqrt(jnp.mean(center * center, axis=-1, keepdims=True) + EPS)
    return center * rstd, rstd


def lanes_of(head, value):
    lane = lax.broadcasted_iota(jnp.int32, (1, 128), 1)
    mine = (lane < 64) if head == 0 else (lane >= 64)
    return jnp.where(mine, value, 0.0).astype(F32)


def by_head(zero, one):
    lane = lax.broadcasted_iota(jnp.int32, (1, 128), 1)
    return jnp.where(lane < 64, zero, one)


def dot(a, b, ca, cb):
    return lax.dot_general(a, b, (((ca,), (cb,)), ((), ())), preferred_element_type=F32)


def norm_back(pulled, hat, rstd, gain):
    scaled = pulled * gain
    inner = jnp.mean(scaled * hat, axis=-1, keepdims=True)
    return rstd * (scaled - jnp.mean(scaled, axis=-1, keepdims=True) - hat * inner)


class Halving:
    def __init__(self, at, lines, whole, first, sums, second, y_first, cut=None, along=None):
        self.along = at.along_y if along is None else along
        self.at, self.lines, self.whole, self.y_first = at, lines, whole, y_first
        self.first, self.sums, self.second = first, sums, second
        self.cut = () if cut is None else (slice(None),) * 2 + (cut,)
        self.one, self.two = [], []

    def block(self, y, z):
        return self.whole[(z // 2, y, z % 2) + self.cut[2:]]

    def start(self):
        at = self.at
        for d in (2, 1, 3):
            if self.y_first:
                to, device = (slice(None), (at.y + d) % 4, slice(None)), self.along(d)
            else:
                z = (at.z + d) % 4
                to, device = (z // 2, slice(None), z % 2), at.along_z(d)
            copy = self.lines.copy(self.whole.at[to + self.cut[2:]], self.first.at[d - 1], device)
            copy.start()
            self.one.append(copy)

    def turn(self):
        at = self.at
        for copy in self.one:
            copy.wait_recv()
        for n in range(4):
            acc = self.block(at.y, n) if self.y_first else self.block(n, at.z)
            acc = acc.astype(F32)
            for d in range(3):
                got = self.first[d, n // 2, n % 2] if self.y_first else self.first[d, n]
                acc = acc + got.astype(F32)
            self.sums[n] = acc.astype(self.sums.dtype)
        for d in (2, 1, 3):
            if self.y_first:
                to, device = (at.z + d) % 4, at.along_z(d)
            else:
                to, device = (at.y + d) % 4, self.along(d)
            copy = self.lines.copy(self.sums.at[to], self.second.at[d - 1], device)
            copy.start()
            self.two.append(copy)

    def total(self):
        for copy in self.two:
            copy.wait_recv()
        acc = self.sums[self.at.z if self.y_first else self.at.y].astype(F32)
        for d in range(3):
            acc = acc + self.second[d].astype(F32)
        return acc

    def sent(self):
        for copy in self.one + self.two:
            copy.wait_send()


def halving_scratch(y_first, dims, of=BF):
    lead = (3, 2, 2) if y_first else (3, 4)
    return [VMEM(lead + dims, of), VMEM((4,) + dims, of), VMEM((3,) + dims, of)]


class Spread:
    def __init__(self, at, lines, slot, z_first):
        self.at, self.lines, self.slot, self.z_first = at, lines, slot, z_first
        self.y, self.again = {}, {}

    def start(self, own=None, others=None):
        at = self.at
        own = self.slot(at.i) if own is None else own
        self.z = self.lines.copy(own, self.slot(at.i), at.mirror())
        self.z.start()
        for d in STEPS:
            block = own if others is None else others(d)
            self.y[d] = self.lines.copy(block, self.slot(at.i), at.along_y(d))
            self.y[d].start()

    def forward(self):
        at = self.at
        if self.z_first:
            self.z.wait_recv()
            block = self.slot((1 - at.zh) * 4 + at.y)
            for d in STEPS:
                self.again[d] = self.lines.copy(block, block, at.along_y(d))
                self.again[d].start()
        else:
            for d in STEPS:
                self.y[d].wait_recv()
                block = self.slot(at.zh * 4 + (at.y + 4 - d) % 4)
                self.again[d] = self.lines.copy(block, block, at.mirror())
                self.again[d].start()

    def arrived(self):
        for copy in self.y.values() if self.z_first else [self.z]:
            copy.wait_recv()
        for copy in self.again.values():
            copy.wait_recv()

    def sent(self):
        for copy in [self.z, *self.y.values(), *self.again.values()]:
            copy.wait_send()


def any_spec():
    return pl.BlockSpec(memory_space=ANY)


def vm_spec():
    return pl.BlockSpec(memory_space=VMEM)


def shape(*dims, of=BF):
    return jax.ShapeDtypeStruct(dims, of)


def layer_kernel(
    x, cot, vec, w_qkv, w_out, w_up, w_down,
    xgrad, result, wide_q, wide_u, wdown_out, wout_out, small,
    vg, wkv, wq, wu, wd, wo_mine, wout, w_up_here, picked, rows, ub,
    xg, n1, cg, q, k, v, kr, vr, att, lse, top, total, mixed, mid, own, n2g, act, dpre, dmid, low, db,
    parts_a, core_a, part_a, ring_a, ends, core_b, part_b, ring_b, parts_c, core_c, part_c, ring_c,
    pulls, do, delta, dq, dk, dv, away, back, dqkv, sums, up_sum,
    wup_grad, wdown_grad, wout_grad, wqkv_grad, points,
    u1, u2, u3, d1, d2, d3, o1, o2, o3, p1, p2, p3, g1, g2, g3, v1, v2, v3,
    low_u, low_q, turn, down_turn, point, local, send, recv,
):
    at = Place()
    mine = pl.ds(pl.multiple_of(at.xc * 128, 128), 128)
    loads = []

    def load(src, dst):
        loads.append(pltpu.make_async_copy(src, dst, local.at[len(loads)]))
        loads[-1].start()
        return loads[-1]

    def columns(n):
        return w_qkv.at[:, pl.ds(pl.multiple_of(n * D + at.xc * 128, 128), 128)]

    got_kv = [load(columns(n + 1), wkv.at[at.i, :, n * 128 : n * 128 + 128]) for n in range(2)]
    got_q = load(columns(0), wq.at[at.i])
    got_up = load(w_up, w_up_here)
    got_wo = load(
        w_out.at[pl.ds(pl.multiple_of(at.xc * 16, 16), 16)], wo_mine.at[at.i]
    )
    got_wd = load(w_down.at[:, at.fc], wd.at[at.i])
    swapped = (at.xc, at.zl * 8 + at.i)
    barrier = pltpu.get_barrier_semaphore()

    @pl.when(at.i != at.xc)
    def _():
        pl.semaphore_signal(barrier, inc=1, device_id=swapped, device_id_type=MESH)

    greet(
        [at.in_group(*d) for d in GROUP]
        + [at.along_y(d) for d in STEPS]
        + [at.along_z(d) for d in STEPS],
        jnp.where(at.i != at.xc, 1, 0),
    )
    lines = Lines(send, recv)
    vec_in = Spread(at, lines, lambda i: vg.at[i], True)
    kv_in = Spread(at, lines, lambda i: wkv.at[i], True)
    q_in = Spread(at, lines, lambda i: wq.at[i], True)
    wo_in = Spread(at, lines, lambda i: wo_mine.at[i], True)
    wd_in = Spread(at, lines, lambda i: wd.at[i], False)
    wu_in = Spread(at, lines, lambda i: wu.at[i], False)

    x_in = gather_group(at, lines, x, lambda n: slot_of(xg, n))
    vec_in.start(vec)
    for copy in got_kv:
        copy.wait()
    kv_in.start()
    got_wo.wait()
    wo_in.start()
    got_q.wait()
    q_in.start()
    vg[at.i] = vec[...]
    slot_of(xg, at.xc)[...] = x[...]
    vec_in.forward()
    kv_in.forward()
    wo_in.forward()
    q_in.forward()
    got_up.wait()
    at_row = lax.broadcasted_iota(jnp.int32, (1024, 128), 0)
    at_col = lax.broadcasted_iota(jnp.int32, (1024, 128), 1)
    spot = (at_col // 64) * 512 + ((at_col // 32) % 2) * 256 + at_col % 32

    def part_on(d):
        return ((at.x + at.y + d) % 4) * 2 + at.c

    for d in range(4):
        pick = jnp.where(at_row - spot == part_on(d) * 32, 1.0, 0.0).astype(BF)
        for n in range(4):
            picked[d, :, n * 128 : n * 128 + 128] = dot(
                w_up_here[:, n * 1024 : (n + 1) * 1024], pick, 1, 0
            ).astype(BF)
    wu[at.i] = picked[0]
    vec_in.arrived()
    for d in range(8):
        rows[0:6, d * 128 : d * 128 + 128] = vg[d, 0:6, :]
    kv_in.arrived()
    got_wd.wait()
    wu_in.start(picked.at[0], lambda d: picked.at[d])
    wd_in.start(None, lambda d: w_down.at[:, part_on(d)])
    at_k = pl.ds(10 + at.xc % 2, 1)
    q_bias = vg[at.xc // 2, at_k, :]
    v_bias = vg[4 + at.xc // 2, at_k, :]
    swaps = []

    def kv_pair(dx):
        here = pl.ds(pl.multiple_of(((at.x + 4 - dx) % 4) * 256, 256), 256)
        hat, _ = normed(xg[here, :].astype(F32))
        hat = (hat * rows[2:3, :] + rows[3:4, :]).astype(BF)
        n1[here, :] = hat
        made = dot(hat, wkv[...].reshape(D, 256), 1, 0)
        k[here, :] = made[:, 0:128].astype(BF)
        v[here, :] = (made[:, 128:256] + v_bias).astype(BF)
        for src, dst in ((k, kr), (v, vr)):
            copy = lines.copy(src.at[here], dst.at[here], at.across())
            copy.start()
            swaps.append(copy)

    x_in.forward(1)
    x_in.forward(3)
    x_in.arrived(0)
    kv_pair(0)
    x_in.forward(2)
    x_in.arrived(1)
    kv_pair(1)
    x_in.arrived(3)
    kv_pair(3)
    x_in.arrived(2)
    kv_pair(2)
    wo_in.arrived()
    out_in = gather_group(at, lines, wo_mine, lambda n: wout.at[:, n])
    wout[:, at.xc] = wo_mine[...]
    cot_in = Halves(at, lines, cot, cg)
    q_in.arrived()
    for b in range(4):
        here = slice(b * 256, b * 256 + 256)
        q[here, :] = (dot(n1[here, :], wq[...].reshape(D, 128), 1, 0) + q_bias).astype(BF)

    def attend(part, keys, values, fresh):
        block = q[part, :]
        tops, masses, outs, fades = [], [], [], []
        for h in range(2):
            score = dot(block * lanes_of(h, 0.125).astype(BF), keys[...], 1, 1)
            peak = jnp.max(score, axis=-1, keepdims=True)
            if not fresh:
                old = top[part, 64 * h : 64 * h + 1]
                peak = jnp.maximum(old, peak)
                fades.append(jnp.exp(old - peak))
            expo = jnp.exp(score - peak)
            tops.append(peak)
            masses.append(jnp.sum(expo, axis=-1, keepdims=True))
            outs.append(dot(expo.astype(BF), values[...], 1, 0))
        peak, added, out = by_head(*tops), by_head(*masses), by_head(*outs)
        if fresh:
            top[part, :] = peak
            lse[part, :] = added
            total[part, :] = out
        else:
            fade = by_head(*fades)
            mass = lse[part, :] * fade + added
            att[part, :] = ((total[part, :] * fade + out) / mass).astype(BF)
            lse[part, :] = peak + jnp.log(mass)

    def near_step(t, _):
        attend(pl.ds(pl.multiple_of(t * 512, 512), 512), k, v, True)
        return 0

    near_step(0, 0)
    wu_in.forward()
    wd_in.forward()
    near_step(1, 0)
    out_in.forward(1)
    out_in.forward(3)
    for copy in swaps:
        copy.wait_recv()
    given = []
    for dx in (2, 1, 3, 0):
        attend(pl.ds(pl.multiple_of(((at.x + dx) % 4) * 256, 256), 256), kr, vr, False)
        for dc in range(2):
            if (dx, dc) != (0, 0):
                to = ((at.x + dx) % 4) * 2 + (at.c + dc) % 2
                copy = lines.copy(slot_of(att, to), mixed.at[:, mine], at.in_group(dx, dc))
                copy.start()
                given.append(copy)
    mixed[:, mine] = slot_of(att, at.xc)[...]
    out_in.forward(2)
    for dx in (1, 3, 2):
        cot_in.forward(dx)
    lane = lax.broadcasted_iota(jnp.int32, (1, 128), 1)
    for m in range(4):
        word = jnp.zeros((1, 128), F32)
        for b in range(4):
            row = vg[m * 2 + b // 2, pl.ds(6 + (b % 2) * 2 + at.fc // 4, 1), :]
            row = pltpu.roll(row, (b * 32 + 128 - (at.fc % 4) * 32) % 128, 1)
            word = jnp.where(lane // 32 == b, row, word)
        ub[:, m * 128 : m * 128 + 128] = word
    for dx in (0, 1, 3, 2):
        out_in.arrived(dx)
    for copy in given:
        copy.wait_recv()

    middle = x[...].astype(F32) + rows[0:1, :]
    middle = middle + dot(mixed[...], wout[...].reshape(D, D), 1, 0)
    mid[...] = middle
    hat, rstd = normed(middle)
    own[...] = (hat * rows[4:5, :] + rows[5:6, :]).astype(BF)
    tokens_in = Halves(at, lines, own, n2g)
    up_sum[...] = jnp.zeros_like(up_sum)
    out = ReduceHalves(at, lines, parts_a, core_a, part_a, ring_a)
    wd_in.arrived()
    wu_in.arrived()
    for dx in (0, 1, 3, 2):
        cot_in.arrived(dx)

    def pair(dx):
        here = slice(dx * 256, dx * 256 + 256)
        ups = wu[...].reshape(D, 512)
        pre = dot(n2g[here, :], ups, 1, 0) + ub[...]
        grad = dot(cg[here, :], wd[...].reshape(512, D), 1, 1)
        cdf = 0.5 * (1.0 + lax.erf(pre * (0.5**0.5)))
        act[here, :] = (pre * cdf).astype(BF)
        slope = cdf + pre * (jnp.exp(-0.5 * pre * pre) * 0.3989422804014327)
        pulled = (grad * slope).astype(BF)
        dpre[here, :] = pulled
        up_sum[...] += jnp.sum(pulled.astype(F32), axis=0, keepdims=True)
        parts_a[here, :] = dot(pulled, ups, 1, 1).astype(BF)
        out.core((4 - dx) % 4)

    tokens_in.arrived(0)
    pair(0)
    tokens_in.forward(1)
    tokens_in.forward(3)
    tokens_in.arrived(1)
    pair(1)
    tokens_in.forward(2)
    tokens_in.arrived(3)
    pair(3)
    out.pass_on(3)
    tokens_in.arrived(2)
    pair(2)
    out.pass_on(1)
    out.pass_on(2)

    def end_step(b, _):
        here = pl.ds(pl.multiple_of(b * 256, 256), 256)
        ends[here, :] = dot(act[here, :], wd[...].reshape(512, D), 1, 0).astype(BF)
        return 0

    lax.fori_loop(0, 4, end_step, 0)
    made = dot(act[...], cg[...], 0, 0).astype(BF)
    for n in range(16):
        wdown_grad[n // 8, (n // 2) % 4, n % 2] = made[n * 32 : n * 32 + 32, :]
    downs = Halving(at, lines, wdown_grad, d1, d2, d3, False, along=at.aslant)
    downs.start()
    for ring in range(2):
        dmid[64 * ring : 64 * ring + 64, :] = out.both[ring].total()
    pulled = dmid[...]
    sums[4:5, :] = jnp.sum(pulled * hat, axis=0, keepdims=True)
    sums[5:6, :] = jnp.sum(pulled, axis=0, keepdims=True)
    middle = cot[...].astype(F32) + norm_back(pulled, hat, rstd, rows[4:5, :])
    dmid[...] = middle
    low[...] = middle.astype(BF)
    made = dot(low[...], wout[...].reshape(D, D), 1, 1).astype(BF)
    for n in range(8):
        pulls[n] = made[:, n * 128 : n * 128 + 128]
    taken = []
    for dx, dc in GROUP:
        to = ((at.x + dx) % 4) * 2 + (at.c + dc) % 2
        copy = lines.copy(pulls.at[to], slot_of(do, at.xc), at.in_group(dx, dc))
        copy.start()
        taken.append(copy)
    slot_of(do, at.xc)[...] = pulls[at.xc]
    sums[0:1, :] = jnp.sum(low[...].astype(F32), axis=0, keepdims=True)
    sums[1:2, :] = jnp.sum(cot[...].astype(F32), axis=0, keepdims=True)
    made = dot(n2g[...], dpre[...], 0, 0).astype(BF)
    for n in range(16):
        wup_grad[n // 8, (n // 2) % 4, n % 2] = made[n * 64 : n * 64 + 64, :]
    ups = Halving(at, lines, wup_grad, u1, u2, u3, True, along=at.aslant)
    ups.start()
    outs = Halving(at, lines, wout_grad, o1, o2, o3, True)
    closing = ReduceHalves(at, lines, ends, core_b, part_b, ring_b)
    for dx in (2, 1, 3, 0):
        closing.core(dx)
    for copy in taken:
        copy.wait_recv()
    back_in = gather_group(at, lines, low, lambda n: slot_of(db, n))
    slot_of(db, at.xc)[...] = low[...]
    both = do[...].astype(F32) * att[...].astype(F32)
    delta[...] = by_head(
        jnp.sum(both * lanes_of(0, 1.0), axis=-1, keepdims=True),
        jnp.sum(both * lanes_of(1, 1.0), axis=-1, keepdims=True),
    )

    def pull(keys, values, half, fresh):
        there = slice(half * 512, half * 512 + 512)
        dk[:, there] = jnp.zeros((128, 512), F32)
        dv[:, there] = jnp.zeros((128, 512), F32)

        def step(t, _):
            part = pl.ds(pl.multiple_of(t * 512, 512), 512)
            block, grad = q[part, :], do[part, :]
            made = []
            for h in range(2):
                some = block * lanes_of(h, 0.125).astype(BF)
                pulled = grad * lanes_of(h, 1.0).astype(BF)
                prob = jnp.exp(dot(some, keys[there, :], 1, 1) - lse[part, 64 * h : 64 * h + 1])
                dprob = dot(pulled, values[there, :], 1, 1)
                raw = (prob * (dprob - delta[part, 64 * h : 64 * h + 1])).astype(BF)
                dv[:, there] += dot(pulled, prob.astype(BF), 0, 0)
                dk[:, there] += dot(some, raw, 0, 0)
                made.append(dot(raw, keys[there, :], 1, 0))
            out = by_head(*made) * 0.125
            dq[part, :] = out if fresh else dq[part, :] + out
            return 0

        lax.fori_loop(0, 2, step, 0)

    returns = []
    for half in range(2):
        pull(kr, vr, half, half == 0)
        there = slice(half * 512, half * 512 + 512)
        away[half, 0] = dk[:, there].astype(BF)
        away[half, 1] = dv[:, there].astype(BF)
        copy = lines.copy(away.at[half], back.at[half], at.across())
        copy.start()
        returns.append(copy)
        if half == 0:
            for dx in (2, 1, 3):
                closing.pass_on(dx)
    downs.turn()
    pull(k, v, 0, False)
    ups.turn()
    for dx in (1, 3, 2):
        back_in.forward(dx)
    pull(k, v, 1, False)
    for dx in (0, 1, 3, 2):
        back_in.arrived(dx)
    made = dot(att[...], db[...], 0, 0)
    for zl in range(2):
        for i in range(8):
            b = (zl * 8 + i) * 8
            wout_grad[i // 4, i % 4, zl] = made[b : b + 8, :]
    outs.start()
    dqkv[:, 0:128] = dq[...].astype(BF)
    for half in range(2):
        returns[half].wait_recv()
        there = slice(half * 512, half * 512 + 512)
        for n, ref in enumerate((dk, dv)):
            made = jnp.transpose(ref[:, there] + back[half, n].astype(F32))
            dqkv[there, 128 + n * 128 : 256 + n * 128] = made.astype(BF)

    inner = Reduce(
        at, lines,
        lambda d, core: slot_of(parts_c, ((at.x + d) % 4) * 2 + core),
        at.on_x, core_c, part_c, ring_c,
    )
    shift_sum = jnp.zeros((1, D), F32)
    both_sum = jnp.zeros((1, D), F32)
    before = None
    for dx in (2, 1, 3, 0):
        here = pl.ds(pl.multiple_of(((at.x + dx) % 4) * 256, 256), 256)
        made = dot(dqkv[here, 0:128], wq[...].reshape(D, 128), 1, 1)
        made = made + dot(dqkv[here, 128:384], wkv[...].reshape(D, 256), 1, 1)
        parts_c[here, :] = made.astype(BF)
        inner.core(dx)
        shift_sum = shift_sum + jnp.sum(made, axis=0, keepdims=True)
        both_sum = both_sum + jnp.sum(made * n1[here, :].astype(F32), axis=0, keepdims=True)
        if before is not None:
            inner.pass_on(before)
        before = dx
    made = dot(n1[...], dqkv[...], 0, 0).astype(BF)
    for n in range(16):
        wqkv_grad[n // 8, (n // 2) % 4, n % 2] = made[n * 64 : n * 64 + 64, :]
    firsts = Halving(at, lines, wqkv_grad, p1, p2, p3, True, slice(0, 32))
    seconds = Halving(at, lines, wqkv_grad, g1, g2, g3, False, slice(32, 64))
    firsts.start()
    seconds.start()
    qkv_sum = jnp.sum(dqkv[...].astype(F32), axis=0, keepdims=True)
    gain_sum = (both_sum - rows[3:4, :] * shift_sum) / rows[2:3, :]
    for n in range(16):
        wide = slice((n // 2) * 128, (n // 2) * 128 + 128)
        to = (n // 8, (n // 2) % 4, n % 2)
        points[to + (slice(0, 2),)] = sums[0:2, wide]
        points[to + (slice(2, 3),)] = gain_sum[:, wide]
        points[to + (slice(3, 4),)] = shift_sum[:, wide]
        points[to + (slice(4, 6),)] = sums[4:6, wide]
        some = up_sum[:, (n // 4) * 128 : (n // 4) * 128 + 128]
        some = pltpu.roll(some, ((at.fc % 4) * 32 + 128 - (n % 4) * 32) % 128, 1)
        some = jnp.where(lane // 32 == at.fc % 4, some, 0.0)
        for b in range(2):
            points[to + (slice(6 + b, 7 + b),)] = jnp.where(at.fc // 4 == b, some, 0.0)
        some = qkv_sum[:, 0:128] if n < 8 else qkv_sum[:, 256:384]
        points[to + (slice(8, 9),)] = jnp.where(at.xc == n % 8, some, 0.0)
        points[to + (slice(9, 16),)] = jnp.zeros((7, 128), F32)
    vectors = Halving(at, lines, points, v1, v2, v3, True)
    vectors.start()
    third = []

    def to_group(src, dst):
        for dx, dc in GROUP:
            to = ((at.x + dx) % 4) * 2 + (at.c + dc) % 2
            copy = lines.copy(src(to), dst, at.in_group(dx, dc))
            copy.start()
            third.append(copy)

    acc = ups.total()
    for b in range(8):
        low_u[b] = acc[b * 8 : (b + 1) * 8, :]
    to_group(lambda n: low_u.at[n], wide_u.at[at.fc])
    wide_u[at.fc] = low_u[at.xc]
    down_turn[...] = downs.total()
    shifted = lines.copy(down_turn, wdown_out, at.on_x(at.y))

    @pl.when(at.y != 0)
    def _():
        shifted.start()

    @pl.when(at.y == 0)
    def _():
        wdown_out[...] = down_turn[...]

    for ring in range(2):
        some = slice(64 * ring, 64 * ring + 64)
        result[some, :] = (mid[some, :] + closing.both[ring].total() + rows[1:2, :]).astype(BF)
    vectors.turn()
    outs.turn()
    firsts.turn()
    seconds.turn()
    for half, acc in enumerate((firsts.total(), seconds.total())):
        for b in range(4):
            low_q[half * 4 + b] = acc[b * 8 : (b + 1) * 8, :]
    to_group(lambda n: low_q.at[n], wide_q.at[at.xc])
    wide_q[at.xc] = low_q[at.xc]
    pulled = inner.total()
    hat, rstd = normed(x[...].astype(F32))
    xgrad[...] = (dmid[...] + norm_back(pulled, hat, rstd, rows[2:3, :])).astype(BF)
    point[...] = vectors.total()
    to_group(lambda n: point, small.at[at.xc])
    small[at.xc] = point[...]
    turn[...] = outs.total()
    across = lines.copy(turn, wout_out, swapped)

    @pl.when(at.i != at.xc)
    def _():
        across.start()

    @pl.when(at.i == at.xc)
    def _():
        wout_out[...] = turn[...]


    @pl.when(at.i != at.xc)
    def _():
        across.wait()

    @pl.when(at.y != 0)
    def _():
        shifted.wait()

    for copy in third:
        copy.wait()
    for copy in swaps + given + taken + returns:
        copy.wait_send()
    for flow in (
        vec_in, kv_in, q_in, wo_in, wd_in, wu_in, x_in, cot_in, out_in, tokens_in, back_in,
        ups, downs, outs, firsts, seconds, vectors, out, inner, closing,
    ):
        flow.sent()


def lay_kernel(
    xgrad_at, result_at, wide_q, wide_u, wdown_at, wout_at, small,
    result, xgrad, wqkv, qv, wout, ob, wup, ub, wdown, db, g1, s1, g2, s2,
):
    at = Place()
    xgrad[...] = xgrad_at[...]
    result[...] = result_at[...]
    wdown[...] = wdown_at[...]
    wout[...] = wout_at[...]
    for n in range(3):
        for b in range(8):
            wqkv[:, n * D + b * 128 : n * D + b * 128 + 128] = wide_q[b, :, n * 128 : n * 128 + 128]
    lane = lax.broadcasted_iota(jnp.int32, (8, 128), 1)
    for m in range(16):
        for half in range(2):
            out = jnp.zeros((8, 128), F32)
            for b in range(4):
                word = wide_u[half * 4 + b, :, (m // 4) * 128 : (m // 4) * 128 + 128]
                turned = pltpu.roll(word, (b * 32 - (m % 4) * 32) % 128, 1)
                out = jnp.where(lane // 32 == b, turned, out)
            wup[:, m * 256 + half * 128 : m * 256 + half * 128 + 128] = out
    total = small[0]
    for b in range(1, 8):
        total = total + small[b]
    spot = at.zl * 64 + at.xc * 8
    eight = pltpu.roll(total, (128 - spot) % 128, 1)
    for k, ref in enumerate((ob, db, g1, s1, g2, s2)):
        ref[...] = eight[k : k + 1, 0:8]
    own = jnp.where(at.xc // 4 == 0, total[6:7, :], total[7:8, :])
    ub[...] = pltpu.roll(own, (128 - (at.xc % 4) * 32) % 128, 1)[:, 0:32]
    bias = pltpu.roll(total, (128 - at.xc * 16) % 128, 1)
    qv[...] = bias[8:9, 0:16]


def on_device(
    tokens, w_qkv, qv_bias, w_out, out_bias, w_up, up_bias, w_down, down_bias,
    gain_one, shift_one, gain_two, shift_two, cotangent,
):
    vec, row = jnp.zeros((16, 128), F32), 0
    for vector in (
        out_bias, down_bias, gain_one, shift_one, gain_two, shift_two, up_bias, qv_bias
    ):
        lines = vector.astype(F32).reshape(-1, 128)
        vec = vec + jnp.pad(lines, ((row, 16 - row - lines.shape[0]), (0, 0)))
        row += lines.shape[0]
    block, whole, half = VMEM((T, D), BF), VMEM((D, D), BF), VMEM((D, 512), BF)
    narrow, tall = VMEM((D, 128), BF), VMEM((D, 128), F32)
    n_lines = 6 * 7 + 7 * 7 + 8 + 7 + 7 + 5 * 7 + 2 + 6 * 6 + 3 * 7 + 2
    parts = pl.pallas_call(
        layer_kernel,
        name="layer",
        in_specs=[vm_spec()] * 3 + [any_spec()] * 4,
        out_specs=[vm_spec()] * 7,
        out_shape=[
            shape(T, D), shape(T, D), shape(8, 8, 384, of=F32), shape(8, 8, 512, of=F32),
            shape(32, D, of=F32), shape(8, D, of=F32), shape(8, 16, 128, of=F32),
        ],
        scratch_shapes=[
            VMEM((8, 16, 128), F32), VMEM((8, 128, 256), BF), VMEM((8, 128, 128), BF),
            VMEM((8, 128, 512), BF), VMEM((8, 2, 32, D), BF), VMEM((8, 16, D), BF),
            VMEM((8, 8, 16, D), BF), VMEM((128, 4 * D), BF), VMEM((4, 128, 512), BF),
            VMEM((8, D), F32), VMEM((1, 512), F32),
            whole, whole, whole, *[narrow] * 6, *[tall] * 3, block, VMEM((T, D), F32), block,
            whole, half, half, VMEM((T, D), F32), block, whole,
            *[whole, *HALVES_SCRATCH] * 2, whole, *REDUCE_SCRATCH,
            VMEM((8, T, 128), BF), narrow, tall, tall, VMEM((128, D), F32), VMEM((128, D), F32),
            VMEM((2, 2, 128, 512), BF), VMEM((2, 2, 128, 512), BF), VMEM((D, 384), BF),
            VMEM((8, D), F32), VMEM((1, 512), F32),
            VMEM((2, 4, 2, 64, 512), BF), VMEM((2, 4, 2, 32, D), BF), VMEM((2, 4, 2, 8, D), F32),
            VMEM((2, 4, 2, 64, 384), BF), VMEM((2, 4, 2, 16, 128), F32),
            *halving_scratch(True, (64, 512)), *halving_scratch(False, (32, D)),
            *halving_scratch(True, (8, D), F32), *halving_scratch(True, (32, 384)),
            *halving_scratch(False, (32, 384)), *halving_scratch(True, (16, 128), F32),
            VMEM((8, 8, 512), F32), VMEM((8, 8, 384), F32), VMEM((8, D), F32), VMEM((32, D), F32),
            VMEM((16, 128), F32),
            DMA((8,)), DMA((n_lines,)), DMA((n_lines,)),
        ],
        compiler_params=pltpu.CompilerParams(
            collective_id=1, has_side_effects=True, vmem_limit_bytes=60 * 2**20
        ),
    )(tokens[0], cotangent[0], vec, w_qkv, w_out, w_up, w_down.reshape(2, 8, 32, D))
    line = shape(1, 8, of=F32)
    outs = pl.pallas_call(
        lay_kernel,
        name="lay_out",
        in_specs=[vm_spec()] * 7,
        out_specs=[vm_spec()] * 14,
        out_shape=[
            shape(T, D), shape(T, D), shape(8, 3 * D, of=F32), shape(1, 16, of=F32),
            shape(8, D, of=F32), line, shape(8, 4 * D, of=F32), shape(1, 32, of=F32),
            shape(32, D, of=F32), line, line, line, line, line,
        ],
    )(*parts)
    outs = list(outs)
    for n in (0, 1):
        outs[n] = outs[n][None]
    for n in (3, 5, 7, 9, 10, 11, 12, 13):
        outs[n] = outs[n].reshape(-1)
    return tuple(outs)


def solution(mesh):
    return jax.shard_map(
        on_device,
        mesh=mesh,
        in_specs=(
            P("dp", "seq", None), P("dp", None), P("dp"), P("dp", None), P("dp"), P("dp", None),
            P("dp"), P("dp", None), P("dp"), P("dp"), P("dp"), P("dp"), P("dp"),
            P("dp", "seq", None),
        ),
        out_specs=(
            P("dp", "seq", None), P("dp", "seq", None), P(("dp", "seq"), None), P(("dp", "seq")),
            P(("dp", "seq"), None), P(("dp", "seq")), P(("dp", "seq"), None), P(("dp", "seq")),
            P(("dp", "seq"), None), P(("dp", "seq")), P(("dp", "seq")), P(("dp", "seq")),
            P(("dp", "seq")), P(("dp", "seq")),
        ),
        check_vma=False,
    )
```

```python
import functools

import jax
import jax.numpy as jnp
from jax import lax
from jax.experimental import pallas as pl
from jax.experimental.pallas import tpu as pltpu
from jax.sharding import PartitionSpec as P

MESH = pl.DeviceIdType.MESH
EPS = 1e-06
BF = jnp.bfloat16
F32 = jnp.float32
D = 1024
T = 128
VMEM = pltpu.VMEM
ANY = pl.ANY
DMA = pltpu.SemaphoreType.DMA


class Place:
    def __init__(self):
        self.i, self.j = lax.axis_index("dp"), lax.axis_index("seq")
        self.zh, self.y = self.i // 4, self.i % 4
        self.zl, self.xc = self.j // 8, self.j % 8
        self.x, self.c = self.xc // 2, self.xc % 2
        self.z = self.zh * 2 + self.zl
        self.fc = ((self.x + self.y) % 4) * 2 + self.c

    def in_group(self, dx, dc):
        return (self.i, self.zl * 8 + ((self.x + dx) % 4) * 2 + (self.c + dc) % 2)

    def sibling(self):
        return self.in_group(0, 1)

    def across(self):
        return (self.i, (1 - self.zl) * 8 + self.xc)

    def along_y(self, dy):
        return (self.zh * 4 + (self.y + dy) % 4, self.j)

    def on_x(self, dx):
        return self.in_group(dx, 0)

    def aslant(self, dy):
        return (
            self.zh * 4 + (self.y + dy) % 4,
            self.zl * 8 + ((self.x + 4 - dy) % 4) * 2 + self.c,
        )

    def along_z(self, dz):
        z = (self.z + dz) % 4
        return ((z // 2) * 4 + self.y, (z % 2) * 8 + self.xc)

    def mirror(self):
        return ((1 - self.zh) * 4 + self.y, (1 - self.zl) * 8 + self.xc)


GROUP = [(dx, dc) for dx in range(4) for dc in range(2) if (dx, dc) != (0, 0)]
STEPS = (1, 2, 3)


def greet(devices, more=0):
    barrier = pltpu.get_barrier_semaphore()
    for device in devices:
        pl.semaphore_signal(barrier, inc=1, device_id=device, device_id_type=MESH)
    pl.semaphore_wait(barrier, len(devices) + more)


class Lines:
    def __init__(self, send, recv):
        self.send, self.recv, self.used = send, recv, 0

    def copy(self, src, dst, device):
        k = self.used
        self.used += 1
        return pltpu.make_async_remote_copy(
            src_ref=src,
            dst_ref=dst,
            send_sem=self.send.at[k],
            recv_sem=self.recv.at[k],
            device_id=device,
            device_id_type=MESH,
        )


def slot_of(ref, k, size=T):
    return ref.at[pl.ds(pl.multiple_of(k * size, size), size)]


class Gather:
    def __init__(self, at, lines, own, put, got, to):
        self.at, self.lines, self.got = at, lines, got
        self.ring, self.forwards = {}, {}
        for dx in (1, 3, 2):
            self.ring[dx] = lines.copy(own, put(dx), to(dx))
            self.ring[dx].start()
        self.beside = lines.copy(own, put(0), at.sibling())
        self.beside.start()

    def forward(self, dx):
        self.ring[dx].wait_recv()
        here = self.got(dx)
        self.forwards[dx] = self.lines.copy(here, here, self.at.sibling())
        self.forwards[dx].start()

    def arrived(self, dx):
        (self.forwards[dx] if dx else self.beside).wait_recv()

    def sent(self):
        self.beside.wait_send()
        for dx in (1, 3, 2):
            self.forwards[dx].wait_send()
            self.ring[dx].wait_send()

    def finish(self):
        for dx in (1, 3, 2):
            self.forward(dx)
        for dx in (0, 1, 3, 2):
            self.arrived(dx)
        self.sent()


def gather_group(at, lines, own, slot):
    return Gather(
        at, lines, own,
        lambda dx: slot(at.xc),
        lambda dx: slot(((at.x + 4 - dx) % 4) * 2 + at.c),
        at.on_x,
    )


def half_of(ref, back, ring, core):
    start = back * 256 + ring * 128 + core * 64
    return ref.at[pl.ds(pl.multiple_of(start, 64), 64)]


class Halves:
    def __init__(self, at, lines, own, ref):
        self.both = [
            Gather(
                at, lines, own.at[64 * ring : 64 * ring + 64],
                lambda d, ring=ring: half_of(ref, d, ring, at.c),
                lambda d, ring=ring: half_of(ref, d, ring, at.c),
                (at.on_x, at.along_y)[ring],
            )
            for ring in range(2)
        ]
        for ring in range(2):
            half_of(ref, 0, ring, at.c)[...] = own[64 * ring : 64 * ring + 64, :]

    def forward(self, d):
        for one in self.both:
            one.forward(d)

    def arrived(self, d):
        for one in self.both:
            one.arrived(d)

    def sent(self):
        for one in self.both:
            one.sent()


class Reduce:
    def __init__(self, at, lines, slot, to, from_core, sums, from_ring):
        self.at, self.lines, self.slot, self.to = at, lines, slot, to
        self.from_core, self.sums, self.from_ring = from_core, sums, from_ring
        self.cores, self.ring = {}, {}

    def core(self, dx):
        theirs = self.slot(dx, 1 - self.at.c)
        self.cores[dx] = self.lines.copy(theirs, self.from_core.at[dx], self.at.sibling())
        self.cores[dx].start()

    def pass_on(self, dx):
        self.cores[dx].wait_recv()
        mine = self.slot(dx, self.at.c)
        self.sums[dx] = (mine[...].astype(F32) + self.from_core[dx].astype(F32)).astype(BF)
        copy = self.lines.copy(self.sums.at[dx], self.from_ring.at[dx], self.to(dx))
        copy.start()
        self.ring[dx] = copy

    def total(self):
        self.cores[0].wait_recv()
        total = self.slot(0, self.at.c)[...].astype(F32) + self.from_core[0].astype(F32)
        for dx, copy in self.ring.items():
            copy.wait_recv()
            total = total + self.from_ring[dx].astype(F32)
        return total

    def sent(self):
        for copy in [*self.cores.values(), *self.ring.values()]:
            copy.wait_send()


class ReduceHalves:
    def __init__(self, at, lines, ref, from_core, sums, from_ring):
        self.both = [
            Reduce(
                at, lines,
                lambda d, core, ring=ring: half_of(ref, (4 - d) % 4, ring, core),
                (at.on_x, at.along_y)[ring],
                from_core.at[ring], sums.at[ring], from_ring.at[ring],
            )
            for ring in range(2)
        ]

    def core(self, d):
        for one in self.both:
            one.core(d)

    def pass_on(self, d):
        for one in self.both:
            one.pass_on(d)

    def sent(self):
        for one in self.both:
            one.sent()


HALVES_SCRATCH = [VMEM((2, 4, 64, D), BF)] * 3
REDUCE_SCRATCH = [VMEM((4, T, D), BF), VMEM((4, T, D), BF), VMEM((4, T, D), BF)]


def normed(values):
    center = values - jnp.mean(values, axis=-1, keepdims=True)
    rstd = lax.rsqrt(jnp.mean(center * center, axis=-1, keepdims=True) + EPS)
    return center * rstd, rstd


def lanes_of(head, value):
    lane = lax.broadcasted_iota(jnp.int32, (1, 128), 1)
    mine = (lane < 64) if head == 0 else (lane >= 64)
    return jnp.where(mine, value, 0.0).astype(F32)


def by_head(zero, one):
    lane = lax.broadcasted_iota(jnp.int32, (1, 128), 1)
    return jnp.where(lane < 64, zero, one)


def dot(a, b, ca, cb):
    return lax.dot_general(a, b, (((ca,), (cb,)), ((), ())), preferred_element_type=F32)


def norm_back(pulled, hat, rstd, gain):
    scaled = pulled * gain
    inner = jnp.mean(scaled * hat, axis=-1, keepdims=True)
    return rstd * (scaled - jnp.mean(scaled, axis=-1, keepdims=True) - hat * inner)


class Halving:
    def __init__(self, at, lines, whole, first, sums, second, y_first, cut=None, along=None):
        self.along = at.along_y if along is None else along
        self.at, self.lines, self.whole, self.y_first = at, lines, whole, y_first
        self.first, self.sums, self.second = first, sums, second
        self.cut = () if cut is None else (slice(None),) * 2 + (cut,)
        self.one, self.two = [], []

    def block(self, y, z):
        return self.whole[(z // 2, y, z % 2) + self.cut[2:]]

    def start(self):
        at = self.at
        for d in (2, 1, 3):
            if self.y_first:
                to, device = (slice(None), (at.y + d) % 4, slice(None)), self.along(d)
            else:
                z = (at.z + d) % 4
                to, device = (z // 2, slice(None), z % 2), at.along_z(d)
            copy = self.lines.copy(self.whole.at[to + self.cut[2:]], self.first.at[d - 1], device)
            copy.start()
            self.one.append(copy)

    def turn(self):
        at = self.at
        for copy in self.one:
            copy.wait_recv()
        for n in range(4):
            acc = self.block(at.y, n) if self.y_first else self.block(n, at.z)
            acc = acc.astype(F32)
            for d in range(3):
                got = self.first[d, n // 2, n % 2] if self.y_first else self.first[d, n]
                acc = acc + got.astype(F32)
            self.sums[n] = acc.astype(self.sums.dtype)
        for d in (2, 1, 3):
            if self.y_first:
                to, device = (at.z + d) % 4, at.along_z(d)
            else:
                to, device = (at.y + d) % 4, self.along(d)
            copy = self.lines.copy(self.sums.at[to], self.second.at[d - 1], device)
            copy.start()
            self.two.append(copy)

    def total(self):
        for copy in self.two:
            copy.wait_recv()
        acc = self.sums[self.at.z if self.y_first else self.at.y].astype(F32)
        for d in range(3):
            acc = acc + self.second[d].astype(F32)
        return acc

    def sent(self):
        for copy in self.one + self.two:
            copy.wait_send()


def halving_scratch(y_first, dims, of=BF):
    lead = (3, 2, 2) if y_first else (3, 4)
    return [VMEM(lead + dims, of), VMEM((4,) + dims, of), VMEM((3,) + dims, of)]


class Spread:
    def __init__(self, at, lines, slot, z_first):
        self.at, self.lines, self.slot, self.z_first = at, lines, slot, z_first
        self.y, self.again = {}, {}

    def start(self, own=None):
        self.start_z(own)
        self.start_y(own)

    def start_z(self, own=None):
        at = self.at
        own = self.slot(at.i) if own is None else own
        self.z = self.lines.copy(own, self.slot(at.i), at.mirror())
        self.z.start()

    def start_y(self, own=None, others=None):
        at = self.at
        own = self.slot(at.i) if own is None else own
        for d in STEPS:
            block = own if others is None else others(d)
            self.y[d] = self.lines.copy(block, self.slot(at.i), at.along_y(d))
            self.y[d].start()

    def forward(self):
        at = self.at
        if self.z_first:
            self.z.wait_recv()
            block = self.slot((1 - at.zh) * 4 + at.y)
            for d in STEPS:
                self.again[d] = self.lines.copy(block, block, at.along_y(d))
                self.again[d].start()
        else:
            for d in STEPS:
                self.y[d].wait_recv()
                block = self.slot(at.zh * 4 + (at.y + 4 - d) % 4)
                self.again[d] = self.lines.copy(block, block, at.mirror())
                self.again[d].start()

    def arrived(self):
        for copy in self.y.values() if self.z_first else [self.z]:
            copy.wait_recv()
        for copy in self.again.values():
            copy.wait_recv()

    def sent(self):
        for copy in [self.z, *self.y.values(), *self.again.values()]:
            copy.wait_send()


def any_spec():
    return pl.BlockSpec(memory_space=ANY)


def vm_spec():
    return pl.BlockSpec(memory_space=VMEM)


def shape(*dims, of=BF):
    return jax.ShapeDtypeStruct(dims, of)


def layer_kernel(
    x, cot, vec, w_qkv, w_out, w_up, w_down,
    xgrad, result, wide_q, wide_u, wdown_out, wout_out, small,
    vg, wkv, wq, wu, wd, wo_mine, wout, w_up_here, picked, rows, ub,
    xg, n1, cg, q, k, v, kr, vr, att, lse, top, total, mixed, mid, own, n2g, act, dpre, dmid, low, db,
    parts_a, core_a, part_a, ring_a, ends, core_b, part_b, ring_b, parts_c, core_c, part_c, ring_c,
    pulls, do, delta, dq, dk, dv, away, back, dqkv, sums, up_sum,
    wup_grad, wdown_grad, wout_grad, wqkv_grad, points,
    u1, u2, u3, d1, d2, d3, o1, o2, o3, p1, p2, p3, g1, g2, g3, v1, v2, v3,
    low_u, low_q, turn, down_turn, point, local, send, recv,
):
    at = Place()
    mine = pl.ds(pl.multiple_of(at.xc * 128, 128), 128)
    loads = []

    def load(src, dst):
        loads.append(pltpu.make_async_copy(src, dst, local.at[len(loads)]))
        loads[-1].start()
        return loads[-1]

    def columns(n):
        return w_qkv.at[:, pl.ds(pl.multiple_of(n * D + at.xc * 128, 128), 128)]

    got_kv = [load(columns(n + 1), wkv.at[at.i, :, n * 128 : n * 128 + 128]) for n in range(2)]
    got_q = load(columns(0), wq.at[at.i])
    got_up = load(w_up, w_up_here)
    got_wo = load(
        w_out.at[pl.ds(pl.multiple_of(at.xc * 16, 16), 16)], wo_mine.at[at.i]
    )
    got_wd = load(w_down.at[:, at.fc], wd.at[at.i])
    swapped = (at.xc, at.zl * 8 + at.i)
    barrier = pltpu.get_barrier_semaphore()

    @pl.when(at.i != at.xc)
    def _():
        pl.semaphore_signal(barrier, inc=1, device_id=swapped, device_id_type=MESH)

    greet(
        [at.in_group(*d) for d in GROUP]
        + [at.along_y(d) for d in STEPS]
        + [at.along_z(d) for d in STEPS],
        jnp.where(at.i != at.xc, 1, 0),
    )
    lines = Lines(send, recv)
    vec_in = Spread(at, lines, lambda i: vg.at[i], True)
    kv_in = Spread(at, lines, lambda i: wkv.at[i], True)
    q_in = Spread(at, lines, lambda i: wq.at[i], True)
    wo_in = Spread(at, lines, lambda i: wo_mine.at[i], True)
    wd_in = Spread(at, lines, lambda i: wd.at[i], False)
    wu_in = Spread(at, lines, lambda i: wu.at[i], False)

    x_in = gather_group(at, lines, x, lambda n: slot_of(xg, n))
    vec_in.start(vec)
    for copy in got_kv:
        copy.wait()
    kv_in.start()
    got_wo.wait()
    wo_in.start()
    got_q.wait()
    q_in.start()
    vg[at.i] = vec[...]
    slot_of(xg, at.xc)[...] = x[...]
    vec_in.forward()
    kv_in.forward()
    wo_in.forward()
    q_in.forward()
    got_up.wait()
    at_row = lax.broadcasted_iota(jnp.int32, (1024, 128), 0)
    at_col = lax.broadcasted_iota(jnp.int32, (1024, 128), 1)
    spot = (at_col // 64) * 512 + ((at_col // 32) % 2) * 256 + at_col % 32

    def part_on(d):
        return ((at.x + at.y + d) % 4) * 2 + at.c

    for d in range(4):
        pick = jnp.where(at_row - spot == part_on(d) * 32, 1.0, 0.0).astype(BF)
        for n in range(4):
            picked[d, :, n * 128 : n * 128 + 128] = dot(
                w_up_here[:, n * 1024 : (n + 1) * 1024], pick, 1, 0
            ).astype(BF)
    wu[at.i] = picked[0]
    got_wd.wait()
    wd_in.start_z()
    wu_in.start_z(picked.at[0])
    vec_in.arrived()
    for d in range(8):
        rows[0:6, d * 128 : d * 128 + 128] = vg[d, 0:6, :]
    kv_in.arrived()
    wd_in.start_y(None, lambda d: w_down.at[:, part_on(d)])
    at_k = pl.ds(10 + at.xc % 2, 1)
    q_bias = vg[at.xc // 2, at_k, :]
    v_bias = vg[4 + at.xc // 2, at_k, :]
    swaps = []

    def kv_pair(dx):
        here = pl.ds(pl.multiple_of(((at.x + 4 - dx) % 4) * 256, 256), 256)
        hat, _ = normed(xg[here, :].astype(F32))
        hat = (hat * rows[2:3, :] + rows[3:4, :]).astype(BF)
        n1[here, :] = hat
        made = dot(hat, wkv[...].reshape(D, 256), 1, 0)
        k[here, :] = made[:, 0:128].astype(BF)
        v[here, :] = (made[:, 128:256] + v_bias).astype(BF)
        for src, dst in ((k, kr), (v, vr)):
            copy = lines.copy(src.at[here], dst.at[here], at.across())
            copy.start()
            swaps.append(copy)

    x_in.forward(1)
    x_in.forward(3)
    x_in.arrived(0)
    kv_pair(0)
    wu_in.start_y(None, lambda d: picked.at[d])
    x_in.forward(2)
    x_in.arrived(1)
    kv_pair(1)
    x_in.arrived(3)
    kv_pair(3)
    x_in.arrived(2)
    kv_pair(2)
    wo_in.arrived()
    out_in = gather_group(at, lines, wo_mine, lambda n: wout.at[:, n])
    wout[:, at.xc] = wo_mine[...]
    cot_in = Halves(at, lines, cot, cg)
    q_in.arrived()
    for b in range(4):
        here = slice(b * 256, b * 256 + 256)
        q[here, :] = (dot(n1[here, :], wq[...].reshape(D, 128), 1, 0) + q_bias).astype(BF)

    def attend(part, keys, values, fresh):
        block = q[part, :]
        tops, masses, outs, fades = [], [], [], []
        for h in range(2):
            score = dot(block * lanes_of(h, 0.125).astype(BF), keys[...], 1, 1)
            peak = jnp.max(score, axis=-1, keepdims=True)
            if not fresh:
                old = top[part, 64 * h : 64 * h + 1]
                peak = jnp.maximum(old, peak)
                fades.append(jnp.exp(old - peak))
            expo = jnp.exp(score - peak)
            tops.append(peak)
            masses.append(jnp.sum(expo, axis=-1, keepdims=True))
            outs.append(dot(expo.astype(BF), values[...], 1, 0))
        peak, added, out = by_head(*tops), by_head(*masses), by_head(*outs)
        if fresh:
            top[part, :] = peak
            lse[part, :] = added
            total[part, :] = out
        else:
            fade = by_head(*fades)
            mass = lse[part, :] * fade + added
            att[part, :] = ((total[part, :] * fade + out) / mass).astype(BF)
            lse[part, :] = peak + jnp.log(mass)

    def near_step(t, _):
        attend(pl.ds(pl.multiple_of(t * 512, 512), 512), k, v, True)
        return 0

    near_step(0, 0)
    wd_in.forward()
    near_step(1, 0)
    wu_in.forward()
    out_in.forward(1)
    out_in.forward(3)
    for copy in swaps:
        copy.wait_recv()
    given = []
    for dx in (2, 1, 3, 0):
        attend(pl.ds(pl.multiple_of(((at.x + dx) % 4) * 256, 256), 256), kr, vr, False)
        for dc in range(2):
            if (dx, dc) != (0, 0):
                to = ((at.x + dx) % 4) * 2 + (at.c + dc) % 2
                copy = lines.copy(slot_of(att, to), mixed.at[:, mine], at.in_group(dx, dc))
                copy.start()
                given.append(copy)
    mixed[:, mine] = slot_of(att, at.xc)[...]
    out_in.forward(2)
    for dx in (1, 3, 2):
        cot_in.forward(dx)
    lane = lax.broadcasted_iota(jnp.int32, (1, 128), 1)
    for m in range(4):
        word = jnp.zeros((1, 128), F32)
        for b in range(4):
            row = vg[m * 2 + b // 2, pl.ds(6 + (b % 2) * 2 + at.fc // 4, 1), :]
            row = pltpu.roll(row, (b * 32 + 128 - (at.fc % 4) * 32) % 128, 1)
            word = jnp.where(lane // 32 == b, row, word)
        ub[:, m * 128 : m * 128 + 128] = word
    for dx in (0, 1, 3, 2):
        out_in.arrived(dx)
    for copy in given:
        copy.wait_recv()

    middle = x[...].astype(F32) + rows[0:1, :]
    middle = middle + dot(mixed[...], wout[...].reshape(D, D), 1, 0)
    mid[...] = middle
    hat, rstd = normed(middle)
    own[...] = (hat * rows[4:5, :] + rows[5:6, :]).astype(BF)
    tokens_in = Halves(at, lines, own, n2g)
    up_sum[...] = jnp.zeros_like(up_sum)
    out = ReduceHalves(at, lines, parts_a, core_a, part_a, ring_a)
    wd_in.arrived()
    wu_in.arrived()
    for dx in (0, 1, 3, 2):
        cot_in.arrived(dx)

    def pair(dx):
        here = slice(dx * 256, dx * 256 + 256)
        ups = wu[...].reshape(D, 512)
        pre = dot(n2g[here, :], ups, 1, 0) + ub[...]
        grad = dot(cg[here, :], wd[...].reshape(512, D), 1, 1)
        cdf = 0.5 * (1.0 + lax.erf(pre * (0.5**0.5)))
        act[here, :] = (pre * cdf).astype(BF)
        slope = cdf + pre * (jnp.exp(-0.5 * pre * pre) * 0.3989422804014327)
        pulled = (grad * slope).astype(BF)
        dpre[here, :] = pulled
        up_sum[...] += jnp.sum(pulled.astype(F32), axis=0, keepdims=True)
        parts_a[here, :] = dot(pulled, ups, 1, 1).astype(BF)
        out.core((4 - dx) % 4)

    tokens_in.arrived(0)
    pair(0)
    tokens_in.forward(1)
    tokens_in.forward(3)
    tokens_in.arrived(1)
    pair(1)
    tokens_in.forward(2)
    tokens_in.arrived(3)
    pair(3)
    out.pass_on(3)
    tokens_in.arrived(2)
    pair(2)
    out.pass_on(1)
    out.pass_on(2)

    def end_step(b, _):
        here = pl.ds(pl.multiple_of(b * 256, 256), 256)
        ends[here, :] = dot(act[here, :], wd[...].reshape(512, D), 1, 0).astype(BF)
        return 0

    lax.fori_loop(0, 4, end_step, 0)
    made = dot(act[...], cg[...], 0, 0).astype(BF)
    for n in range(16):
        wdown_grad[n // 8, (n // 2) % 4, n % 2] = made[n * 32 : n * 32 + 32, :]
    downs = Halving(at, lines, wdown_grad, d1, d2, d3, False, along=at.aslant)
    downs.start()
    for ring in range(2):
        dmid[64 * ring : 64 * ring + 64, :] = out.both[ring].total()
    pulled = dmid[...]
    sums[4:5, :] = jnp.sum(pulled * hat, axis=0, keepdims=True)
    sums[5:6, :] = jnp.sum(pulled, axis=0, keepdims=True)
    middle = cot[...].astype(F32) + norm_back(pulled, hat, rstd, rows[4:5, :])
    dmid[...] = middle
    low[...] = middle.astype(BF)
    made = dot(low[...], wout[...].reshape(D, D), 1, 1).astype(BF)
    for n in range(8):
        pulls[n] = made[:, n * 128 : n * 128 + 128]
    taken = []
    for dx, dc in GROUP:
        to = ((at.x + dx) % 4) * 2 + (at.c + dc) % 2
        copy = lines.copy(pulls.at[to], slot_of(do, at.xc), at.in_group(dx, dc))
        copy.start()
        taken.append(copy)
    slot_of(do, at.xc)[...] = pulls[at.xc]
    sums[0:1, :] = jnp.sum(low[...].astype(F32), axis=0, keepdims=True)
    sums[1:2, :] = jnp.sum(cot[...].astype(F32), axis=0, keepdims=True)
    made = dot(n2g[...], dpre[...], 0, 0).astype(BF)
    for n in range(16):
        wup_grad[n // 8, (n // 2) % 4, n % 2] = made[n * 64 : n * 64 + 64, :]
    ups = Halving(at, lines, wup_grad, u1, u2, u3, True, along=at.aslant)
    ups.start()
    outs = Halving(at, lines, wout_grad, o1, o2, o3, True)
    closing = ReduceHalves(at, lines, ends, core_b, part_b, ring_b)
    for dx in (2, 1, 3, 0):
        closing.core(dx)
    for copy in taken:
        copy.wait_recv()
    back_in = gather_group(at, lines, low, lambda n: slot_of(db, n))
    slot_of(db, at.xc)[...] = low[...]
    both = do[...].astype(F32) * att[...].astype(F32)
    delta[...] = by_head(
        jnp.sum(both * lanes_of(0, 1.0), axis=-1, keepdims=True),
        jnp.sum(both * lanes_of(1, 1.0), axis=-1, keepdims=True),
    )

    def pull(keys, values, half, fresh):
        there = slice(half * 512, half * 512 + 512)
        dk[:, there] = jnp.zeros((128, 512), F32)
        dv[:, there] = jnp.zeros((128, 512), F32)

        def step(t, _):
            part = pl.ds(pl.multiple_of(t * 512, 512), 512)
            block, grad = q[part, :], do[part, :]
            made = []
            for h in range(2):
                some = block * lanes_of(h, 0.125).astype(BF)
                pulled = grad * lanes_of(h, 1.0).astype(BF)
                prob = jnp.exp(dot(some, keys[there, :], 1, 1) - lse[part, 64 * h : 64 * h + 1])
                dprob = dot(pulled, values[there, :], 1, 1)
                raw = (prob * (dprob - delta[part, 64 * h : 64 * h + 1])).astype(BF)
                dv[:, there] += dot(pulled, prob.astype(BF), 0, 0)
                dk[:, there] += dot(some, raw, 0, 0)
                made.append(dot(raw, keys[there, :], 1, 0))
            out = by_head(*made) * 0.125
            dq[part, :] = out if fresh else dq[part, :] + out
            return 0

        lax.fori_loop(0, 2, step, 0)

    returns = []
    for half in range(2):
        pull(kr, vr, half, half == 0)
        there = slice(half * 512, half * 512 + 512)
        away[half, 0] = dk[:, there].astype(BF)
        away[half, 1] = dv[:, there].astype(BF)
        copy = lines.copy(away.at[half], back.at[half], at.across())
        copy.start()
        returns.append(copy)
        if half == 0:
            for dx in (2, 1, 3):
                closing.pass_on(dx)
    downs.turn()
    pull(k, v, 0, False)
    ups.turn()
    for dx in (1, 3, 2):
        back_in.forward(dx)
    pull(k, v, 1, False)
    for dx in (0, 1, 3, 2):
        back_in.arrived(dx)
    made = dot(att[...], db[...], 0, 0)
    for zl in range(2):
        for i in range(8):
            b = (zl * 8 + i) * 8
            wout_grad[i // 4, i % 4, zl] = made[b : b + 8, :]
    outs.start()
    dqkv[:, 0:128] = dq[...].astype(BF)
    for half in range(2):
        returns[half].wait_recv()
        there = slice(half * 512, half * 512 + 512)
        for n, ref in enumerate((dk, dv)):
            made = jnp.transpose(ref[:, there] + back[half, n].astype(F32))
            dqkv[there, 128 + n * 128 : 256 + n * 128] = made.astype(BF)

    inner = Reduce(
        at, lines,
        lambda d, core: slot_of(parts_c, ((at.x + d) % 4) * 2 + core),
        at.on_x, core_c, part_c, ring_c,
    )
    shift_sum = jnp.zeros((1, D), F32)
    both_sum = jnp.zeros((1, D), F32)
    before = None
    for dx in (2, 1, 3, 0):
        here = pl.ds(pl.multiple_of(((at.x + dx) % 4) * 256, 256), 256)
        made = dot(dqkv[here, 0:128], wq[...].reshape(D, 128), 1, 1)
        made = made + dot(dqkv[here, 128:384], wkv[...].reshape(D, 256), 1, 1)
        parts_c[here, :] = made.astype(BF)
        inner.core(dx)
        shift_sum = shift_sum + jnp.sum(made, axis=0, keepdims=True)
        both_sum = both_sum + jnp.sum(made * n1[here, :].astype(F32), axis=0, keepdims=True)
        if before is not None:
            inner.pass_on(before)
        before = dx
    made = dot(n1[...], dqkv[...], 0, 0).astype(BF)
    for n in range(16):
        wqkv_grad[n // 8, (n // 2) % 4, n % 2] = made[n * 64 : n * 64 + 64, :]
    firsts = Halving(at, lines, wqkv_grad, p1, p2, p3, True, slice(0, 32))
    seconds = Halving(at, lines, wqkv_grad, g1, g2, g3, False, slice(32, 64))
    firsts.start()
    seconds.start()
    qkv_sum = jnp.sum(dqkv[...].astype(F32), axis=0, keepdims=True)
    gain_sum = (both_sum - rows[3:4, :] * shift_sum) / rows[2:3, :]
    for n in range(16):
        wide = slice((n // 2) * 128, (n // 2) * 128 + 128)
        to = (n // 8, (n // 2) % 4, n % 2)
        points[to + (slice(0, 2),)] = sums[0:2, wide]
        points[to + (slice(2, 3),)] = gain_sum[:, wide]
        points[to + (slice(3, 4),)] = shift_sum[:, wide]
        points[to + (slice(4, 6),)] = sums[4:6, wide]
        some = up_sum[:, (n // 4) * 128 : (n // 4) * 128 + 128]
        some = pltpu.roll(some, ((at.fc % 4) * 32 + 128 - (n % 4) * 32) % 128, 1)
        some = jnp.where(lane // 32 == at.fc % 4, some, 0.0)
        for b in range(2):
            points[to + (slice(6 + b, 7 + b),)] = jnp.where(at.fc // 4 == b, some, 0.0)
        some = qkv_sum[:, 0:128] if n < 8 else qkv_sum[:, 256:384]
        points[to + (slice(8, 9),)] = jnp.where(at.xc == n % 8, some, 0.0)
        points[to + (slice(9, 16),)] = jnp.zeros((7, 128), F32)
    vectors = Halving(at, lines, points, v1, v2, v3, True)
    vectors.start()
    third = []

    def to_group(src, dst):
        for dx, dc in GROUP:
            to = ((at.x + dx) % 4) * 2 + (at.c + dc) % 2
            copy = lines.copy(src(to), dst, at.in_group(dx, dc))
            copy.start()
            third.append(copy)

    acc = ups.total()
    for b in range(8):
        low_u[b] = acc[b * 8 : (b + 1) * 8, :]
    to_group(lambda n: low_u.at[n], wide_u.at[at.fc])
    wide_u[at.fc] = low_u[at.xc]
    down_turn[...] = downs.total()
    shifted = lines.copy(down_turn, wdown_out, at.on_x(at.y))

    @pl.when(at.y != 0)
    def _():
        shifted.start()

    @pl.when(at.y == 0)
    def _():
        wdown_out[...] = down_turn[...]

    for ring in range(2):
        some = slice(64 * ring, 64 * ring + 64)
        result[some, :] = (mid[some, :] + closing.both[ring].total() + rows[1:2, :]).astype(BF)
    vectors.turn()
    outs.turn()
    firsts.turn()
    seconds.turn()
    for half, acc in enumerate((firsts.total(), seconds.total())):
        for b in range(4):
            low_q[half * 4 + b] = acc[b * 8 : (b + 1) * 8, :]
    to_group(lambda n: low_q.at[n], wide_q.at[at.xc])
    wide_q[at.xc] = low_q[at.xc]
    pulled = inner.total()
    hat, rstd = normed(x[...].astype(F32))
    xgrad[...] = (dmid[...] + norm_back(pulled, hat, rstd, rows[2:3, :])).astype(BF)
    point[...] = vectors.total()
    to_group(lambda n: point, small.at[at.xc])
    small[at.xc] = point[...]
    turn[...] = outs.total()
    across = lines.copy(turn, wout_out, swapped)

    @pl.when(at.i != at.xc)
    def _():
        across.start()

    @pl.when(at.i == at.xc)
    def _():
        wout_out[...] = turn[...]


    @pl.when(at.i != at.xc)
    def _():
        across.wait()

    @pl.when(at.y != 0)
    def _():
        shifted.wait()

    for copy in third:
        copy.wait()
    for copy in swaps + given + taken + returns:
        copy.wait_send()
    for flow in (
        vec_in, kv_in, q_in, wo_in, wd_in, wu_in, x_in, cot_in, out_in, tokens_in, back_in,
        ups, downs, outs, firsts, seconds, vectors, out, inner, closing,
    ):
        flow.sent()


def lay_kernel(
    xgrad_at, result_at, wide_q, wide_u, wdown_at, wout_at, small,
    result, xgrad, wqkv, qv, wout, ob, wup, ub, wdown, db, g1, s1, g2, s2,
):
    at = Place()
    xgrad[...] = xgrad_at[...]
    result[...] = result_at[...]
    wdown[...] = wdown_at[...]
    wout[...] = wout_at[...]
    for n in range(3):
        for b in range(8):
            wqkv[:, n * D + b * 128 : n * D + b * 128 + 128] = wide_q[b, :, n * 128 : n * 128 + 128]
    lane = lax.broadcasted_iota(jnp.int32, (8, 128), 1)
    for m in range(16):
        for half in range(2):
            out = jnp.zeros((8, 128), F32)
            for b in range(4):
                word = wide_u[half * 4 + b, :, (m // 4) * 128 : (m // 4) * 128 + 128]
                turned = pltpu.roll(word, (b * 32 - (m % 4) * 32) % 128, 1)
                out = jnp.where(lane // 32 == b, turned, out)
            wup[:, m * 256 + half * 128 : m * 256 + half * 128 + 128] = out
    total = small[0]
    for b in range(1, 8):
        total = total + small[b]
    spot = at.zl * 64 + at.xc * 8
    eight = pltpu.roll(total, (128 - spot) % 128, 1)
    for k, ref in enumerate((ob, db, g1, s1, g2, s2)):
        ref[...] = eight[k : k + 1, 0:8]
    own = jnp.where(at.xc // 4 == 0, total[6:7, :], total[7:8, :])
    ub[...] = pltpu.roll(own, (128 - (at.xc % 4) * 32) % 128, 1)[:, 0:32]
    bias = pltpu.roll(total, (128 - at.xc * 16) % 128, 1)
    qv[...] = bias[8:9, 0:16]


def on_device(
    tokens, w_qkv, qv_bias, w_out, out_bias, w_up, up_bias, w_down, down_bias,
    gain_one, shift_one, gain_two, shift_two, cotangent,
):
    vec, row = jnp.zeros((16, 128), F32), 0
    for vector in (
        out_bias, down_bias, gain_one, shift_one, gain_two, shift_two, up_bias, qv_bias
    ):
        lines = vector.astype(F32).reshape(-1, 128)
        vec = vec + jnp.pad(lines, ((row, 16 - row - lines.shape[0]), (0, 0)))
        row += lines.shape[0]
    block, whole, half = VMEM((T, D), BF), VMEM((D, D), BF), VMEM((D, 512), BF)
    narrow, tall = VMEM((D, 128), BF), VMEM((D, 128), F32)
    n_lines = 6 * 7 + 7 * 7 + 8 + 7 + 7 + 5 * 7 + 2 + 6 * 6 + 3 * 7 + 2
    parts = pl.pallas_call(
        layer_kernel,
        name="layer",
        in_specs=[vm_spec()] * 3 + [any_spec()] * 4,
        out_specs=[vm_spec()] * 7,
        out_shape=[
            shape(T, D), shape(T, D), shape(8, 8, 384, of=F32), shape(8, 8, 512, of=F32),
            shape(32, D, of=F32), shape(8, D, of=F32), shape(8, 16, 128, of=F32),
        ],
        scratch_shapes=[
            VMEM((8, 16, 128), F32), VMEM((8, 128, 256), BF), VMEM((8, 128, 128), BF),
            VMEM((8, 128, 512), BF), VMEM((8, 2, 32, D), BF), VMEM((8, 16, D), BF),
            VMEM((8, 8, 16, D), BF), VMEM((128, 4 * D), BF), VMEM((4, 128, 512), BF),
            VMEM((8, D), F32), VMEM((1, 512), F32),
            whole, whole, whole, *[narrow] * 6, *[tall] * 3, block, VMEM((T, D), F32), block,
            whole, half, half, VMEM((T, D), F32), block, whole,
            *[whole, *HALVES_SCRATCH] * 2, whole, *REDUCE_SCRATCH,
            VMEM((8, T, 128), BF), narrow, tall, tall, VMEM((128, D), F32), VMEM((128, D), F32),
            VMEM((2, 2, 128, 512), BF), VMEM((2, 2, 128, 512), BF), VMEM((D, 384), BF),
            VMEM((8, D), F32), VMEM((1, 512), F32),
            VMEM((2, 4, 2, 64, 512), BF), VMEM((2, 4, 2, 32, D), BF), VMEM((2, 4, 2, 8, D), F32),
            VMEM((2, 4, 2, 64, 384), BF), VMEM((2, 4, 2, 16, 128), F32),
            *halving_scratch(True, (64, 512)), *halving_scratch(False, (32, D)),
            *halving_scratch(True, (8, D), F32), *halving_scratch(True, (32, 384)),
            *halving_scratch(False, (32, 384)), *halving_scratch(True, (16, 128), F32),
            VMEM((8, 8, 512), F32), VMEM((8, 8, 384), F32), VMEM((8, D), F32), VMEM((32, D), F32),
            VMEM((16, 128), F32),
            DMA((8,)), DMA((n_lines,)), DMA((n_lines,)),
        ],
        compiler_params=pltpu.CompilerParams(
            collective_id=1, has_side_effects=True, vmem_limit_bytes=60 * 2**20
        ),
    )(tokens[0], cotangent[0], vec, w_qkv, w_out, w_up, w_down.reshape(2, 8, 32, D))
    line = shape(1, 8, of=F32)
    outs = pl.pallas_call(
        lay_kernel,
        name="lay_out",
        in_specs=[vm_spec()] * 7,
        out_specs=[vm_spec()] * 14,
        out_shape=[
            shape(T, D), shape(T, D), shape(8, 3 * D, of=F32), shape(1, 16, of=F32),
            shape(8, D, of=F32), line, shape(8, 4 * D, of=F32), shape(1, 32, of=F32),
            shape(32, D, of=F32), line, line, line, line, line,
        ],
    )(*parts)
    outs = list(outs)
    for n in (0, 1):
        outs[n] = outs[n][None]
    for n in (3, 5, 7, 9, 10, 11, 12, 13):
        outs[n] = outs[n].reshape(-1)
    return tuple(outs)


def solution(mesh):
    return jax.shard_map(
        on_device,
        mesh=mesh,
        in_specs=(
            P("dp", "seq", None), P("dp", None), P("dp"), P("dp", None), P("dp"), P("dp", None),
            P("dp"), P("dp", None), P("dp"), P("dp"), P("dp"), P("dp"), P("dp"),
            P("dp", "seq", None),
        ),
        out_specs=(
            P("dp", "seq", None), P("dp", "seq", None), P(("dp", "seq"), None), P(("dp", "seq")),
            P(("dp", "seq"), None), P(("dp", "seq")), P(("dp", "seq"), None), P(("dp", "seq")),
            P(("dp", "seq"), None), P(("dp", "seq")), P(("dp", "seq")), P(("dp", "seq")),
            P(("dp", "seq")), P(("dp", "seq")),
        ),
        check_vma=False,
    )
```
